32 devices in a mesh: dp: 8 (over z, core), mp: 4 (over y, x).
Axes of the slice: x: 2, y: 2, z: 4, core: 2. Of those that a mesh axis runs over, the one named last changes fastest.
Arguments:
- tokens: bfloat16 [16, 1024, 1600], P('dp', 'mp'), may hold values from -6 to 6
- cotangent: bfloat16 [16, 1024, 1600], P('dp', 'mp'), may hold values from -6 to 6
- block_order: int32 [8], replicated, may hold values from 0 to 7, each once
- qkv_weight: bfloat16 [2, 1600, 4800], P(None, 'dp'), may hold values from -0.15625 to 0.15625
- proj_weight: bfloat16 [2, 1600, 1600], P(None, 'dp'), may hold values from -3 to 3
- fc_weight: bfloat16 [2, 1600, 6400], P(None, 'dp', 'mp'), may hold values from -0.15625 to 0.15625
- fc2_weight: bfloat16 [2, 6400, 1600], P(None, 'mp', 'dp'), may hold values from -0.078125 to 0.078125
- fc_bias: bfloat16 [2, 6400], P(None, ('mp', 'dp')), may hold values from -1.5 to 1.5
- norm_gain: bfloat16 [2, 2, 1600], P(None, None, 'dp'), may hold values from 0.5 to 1.5
- norm_shift: bfloat16 [2, 2, 1600], P(None, None, 'dp'), may hold values from -1.5 to 1.5
- attn_bias: bfloat16 [2, 2, 1600], P(None, None, 'dp'), may hold values from -1.5 to 1.5
- out_bias: bfloat16 [2, 2, 1600], P(None, None, 'dp'), may hold values from -1.5 to 1.5
Outputs:
- outputs: float32 [16, 1024, 1600], P('dp', 'mp')
- input_grad: float32 [16, 1024, 1600], P('dp', 'mp')
- qkv_weight_grad: float32 [2, 1600, 4800], P(None, 'dp', 'mp')
- proj_weight_grad: float32 [2, 1600, 1600], P(None, 'dp', 'mp')
- fc_weight_grad: float32 [2, 1600, 6400], P(None, 'dp', 'mp')
- fc2_weight_grad: float32 [2, 6400, 1600], P(None, 'mp', 'dp')
- fc_bias_grad: float32 [2, 6400], P(None, ('mp', 'dp'))
- norm_gain_grad: float32 [2, 2, 1600], P(None, None, 'dp')
- norm_shift_grad: float32 [2, 2, 1600], P(None, None, 'dp')
- attn_bias_grad: float32 [2, 2, 1600], P(None, None, 'dp')
- out_bias_grad: float32 [2, 2, 1600], P(None, None, 'dp')
The draws below stay inside these ranges and needn't reach their ends.
Inputs may be any that keep to these rules, and one draw needn't show every extreme that they name: A permutation: block slot 2r and 2r + 1 of a sequence, held by index r of mp, hold the blocks numbered block_order[2r] and block_order[2r + 1] of 128 tokens.
All inputs are finite; a program needn't handle non-finite values.
Results may differ from the reference program's by a relative error of at most 0.015.
Values may be sent and summed in bfloat16 or wider, within the bound.
A program may use at most 448 MiB of HBM per device.

```python
import jax
import jax.numpy as jnp
from jax import lax

D = 1600
HD = 64
FF = 6400
SEQ_LEN = 1024
LAYERS = 2
BATCH = 16
N_DP = 8
N_MP = 4


def block_scale(stream_key, dims, split, low, high):
    factor_of, own = 1.0, jax.random.fold_in(stream_key, 6)
    for dim, parts in split:
        draws = jnp.exp(jax.random.uniform(jax.random.fold_in(own, dim), (parts,), jnp.float32, low / len(split), high / len(split)))
        factor_of = factor_of * jnp.repeat(draws, dims[dim] // parts).reshape([-1 if axis == dim else 1 for axis in range(len(dims))])
    return factor_of


def gaussian(rng, dims, scale, bound, split=(), kind=jnp.bfloat16):
    result = jax.random.normal(rng, dims, jnp.float32) * scale
    if len(split) > 0:
        result = block_scale(rng, dims, split, -0.22, 0.18) * result
    return jnp.clip(result, min=-bound, max=bound).astype(kind)


def setup_inputs(seed: int = 0) -> dict:
    keys = jax.random.split(jax.random.key(seed), 13)
    tokens = gaussian(keys[0], (BATCH, SEQ_LEN, D), 1.0, 6.0, ((0, 8), (1, 4)))
    cotangent = gaussian(keys[1], (BATCH, SEQ_LEN, D), 1.0, 6.0, ((0, 8), (1, 4)))
    block_order = jax.random.permutation(keys[2], 2 * N_MP).astype(jnp.int32)
    qkv_weight = gaussian(keys[3], (LAYERS, D, 3 * D), D ** -0.5, 0.15625, ((1, 8),))
    proj_weight = gaussian(keys[4], (LAYERS, D, D), (max(D // 400, 1)) ** -0.5, 3.0, ((1, 8),))
    fc_weight = gaussian(keys[5], (LAYERS, D, FF), D ** -0.5, 0.15625, ((1, 8), (2, 4)))
    fc2_weight = gaussian(keys[6], (LAYERS, FF, D), FF ** -0.5, 0.078125, ((1, 4), (2, 8)))
    fc_bias = gaussian(keys[7], (LAYERS, FF), 0.3, 1.5, ((1, 32),))
    norm_gain = jnp.clip(1.0 + 0.1 * jax.random.normal(keys[8], (LAYERS, 2, D), jnp.float32), 0.5, 1.5).astype(jnp.bfloat16)
    norm_shift = gaussian(keys[9], (LAYERS, 2, D), 0.3, 1.5, ((2, 8),))
    attn_bias = gaussian(keys[10], (LAYERS, 2, D), 0.3, 1.5, ((2, 8),))
    out_bias = gaussian(keys[11], (LAYERS, 2, D), 0.3, 1.5, ((2, 8),))
    return dict(tokens=tokens, cotangent=cotangent, block_order=block_order, qkv_weight=qkv_weight, proj_weight=proj_weight, fc_weight=fc_weight, fc2_weight=fc2_weight, fc_bias=fc_bias, norm_gain=norm_gain, norm_shift=norm_shift, attn_bias=attn_bias, out_bias=out_bias)


@jax.custom_vjp
def low(v):
    return lax.optimization_barrier(v.astype(jnp.bfloat16)).astype(jnp.float32)

@jax.custom_vjp
def low_back(v):
    return v

def low_keep(v):
    return (low(v), None)

def low_pass(kept, grad):
    return (grad,)

def back_keep(v):
    return (v, None)

def back_low(kept, grad):
    return (low(grad),)
low.defvjp(low_keep, low_pass)
low_back.defvjp(back_keep, back_low)
HIGH = lax.Precision.HIGHEST
eps = 1e-05

def layer_norm(value, gain, shift):
    mean = lax.optimization_barrier(jnp.mean(value, axis=-1, keepdims=True))
    centred = value - mean
    spread = lax.optimization_barrier(jnp.mean(centred * centred, axis=-1, keepdims=True))
    return centred * lax.rsqrt(spread + eps) * gain + shift

def layer_forward(hidden, params, visible, layer):
    qkv_w, proj_w, fc_w, fc2_w, fc_b, gain, shift, bias_in, bias_out = tuple((w[layer] for w in params))
    heads = D // HD
    scale = HD ** (-0.5)
    length = hidden.shape[0]
    normed = low(layer_norm(hidden, gain[0], shift[0]))
    mixed = jnp.dot(normed, qkv_w, precision=HIGH)
    query = low_back(low(mixed[:, :D] + bias_in[0]))
    key = low_back(low(mixed[:, D:2 * D]))
    value = low_back(low(mixed[:, 2 * D:] + bias_in[1]))
    query_heads = query.reshape(length, heads, HD)
    key_heads = key.reshape(length, heads, HD)
    value_heads = value.reshape(length, heads, HD)
    scores = low_back(jnp.einsum('qhd,khd->hqk', query_heads, key_heads, precision=HIGH) * scale)
    scores = jnp.where(visible[None], scores, -1e+30)
    top = lax.optimization_barrier(jnp.max(scores, axis=-1, keepdims=True))
    expo = jnp.exp(scores - top)
    probs = expo / lax.optimization_barrier(jnp.sum(expo, axis=-1, keepdims=True))
    attended = jnp.einsum('hqk,khd->qhd', low(probs), value_heads, precision=HIGH).reshape(length, D)
    attended = low_back(low(attended))
    branch = low_back(jnp.dot(attended, proj_w, precision=HIGH) + bias_out[0])
    middle = hidden + branch
    normed_two = low(layer_norm(middle, gain[1], shift[1]))
    inner = low_back(jnp.dot(normed_two, fc_w, precision=HIGH) + fc_b)
    active = low(jax.nn.gelu(inner, approximate=True))
    mlp_branch = low_back(jnp.dot(active, fc2_w, precision=HIGH) + bias_out[1])
    return middle + mlp_branch

def forward(hidden, params, visible):
    for layer in range(LAYERS):
        hidden = layer_forward(hidden, params, visible, layer)
    return hidden

def reference(tokens, cotangent, block_order, qkv_weight, proj_weight, fc_weight, fc2_weight, fc_bias, norm_gain, norm_shift, attn_bias, out_bias):
    block = SEQ_LEN // (2 * N_MP)
    rows = jnp.arange(SEQ_LEN, dtype=jnp.int32)
    places = block_order[rows // block].astype(jnp.int32) * block + rows % block
    visible = places[None, :] <= places[:, None]
    params = tuple((w.astype(jnp.float32) for w in (qkv_weight, proj_weight, fc_weight, fc2_weight, fc_bias, norm_gain, norm_shift, attn_bias, out_bias)))

    def step(totals, pair):
        seq_in, seq_cot = pair
        value, pullback = jax.vjp(lambda h, p: forward(h, p, visible), seq_in.astype(jnp.float32), params)
        in_grad, param_grads = pullback(seq_cot.astype(jnp.float32))
        totals = tuple((a + b for a, b in zip(totals, param_grads)))
        return (totals, (value, in_grad))
    zeros = tuple((jnp.zeros(p.shape, jnp.float32) for p in params))
    totals, (outputs, in_grads) = lax.scan(step, zeros, (tokens, cotangent))
    return (outputs, in_grads, totals[0] / N_DP, totals[1] / N_DP, totals[2] / N_DP, totals[3] / N_DP, totals[4] / N_DP, totals[5] / N_DP, totals[6] / N_DP, totals[7] / N_DP, totals[8] / N_DP)
```

```python
import functools

import jax
import jax.numpy as jnp
from jax import lax
from jax.experimental import pallas as pl
from jax.experimental.pallas import tpu as pltpu
from jax.sharding import PartitionSpec as P

HD = 64
LAYERS = 2


eps = 1e-05


def layer_norm(value, gain, shift):
    mean = jnp.mean(value, axis=-1, keepdims=True)
    centred = value - mean
    spread = jnp.mean(centred * centred, axis=-1, keepdims=True)
    return centred * lax.rsqrt(spread + eps) * gain + shift


def fetch_params(weights, layer):
    pieces = tuple((w[layer] for w in weights))
    return (
        lax.all_gather(pieces[0], "dp", axis=0, tiled=True),
        lax.all_gather(pieces[1], "dp", axis=0, tiled=True),
        lax.all_gather(pieces[2], "dp", axis=0, tiled=True),
        lax.all_gather(pieces[3], "dp", axis=1, tiled=True),
        lax.all_gather(pieces[4], "dp", axis=0, tiled=True),
        lax.all_gather(pieces[5], "dp", axis=1, tiled=True),
        lax.all_gather(pieces[6], "dp", axis=1, tiled=True),
        lax.all_gather(pieces[7], "dp", axis=1, tiled=True),
        lax.all_gather(pieces[8], "dp", axis=1, tiled=True),
    )


def fetch_again(weights, layer):
    pieces = tuple((w[layer] for w in weights))
    return (
        lax.all_gather(pieces[0], "dp", axis=0, tiled=True),
        lax.all_gather(pieces[1], "dp", axis=0, tiled=True),
        lax.all_gather(pieces[2], "dp", axis=0, tiled=True),
        lax.all_gather(pieces[3], "dp", axis=1, tiled=True),
        lax.all_gather(pieces[4], "dp", axis=0, tiled=True),
        lax.all_gather(pieces[5], "dp", axis=1, tiled=True),
        lax.all_gather(pieces[6], "dp", axis=1, tiled=True),
        lax.all_gather(pieces[7], "dp", axis=1, tiled=True),
        lax.all_gather(pieces[8], "dp", axis=1, tiled=True),
    )


def scores_of(query_heads, key_heads, visible, scale):
    scores = (
        jnp.einsum("qhd,khd->hqk", query_heads, key_heads, preferred_element_type=jnp.float32)
        * scale
    )
    return jnp.where(visible, scores, -1e30)


def general_body(
    tokens,
    cotangent,
    block_order,
    qkv_weight,
    proj_weight,
    fc_weight,
    fc2_weight,
    fc_bias,
    norm_gain,
    norm_shift,
    attn_bias,
    out_bias,
):
    weights = (
        qkv_weight,
        proj_weight,
        fc_weight,
        fc2_weight,
        fc_bias,
        norm_gain,
        norm_shift,
        attn_bias,
        out_bias,
    )
    seqs, local, width = tokens.shape
    heads = width // HD
    scale = HD ** (-0.5)
    model_size = lax.axis_size("mp")
    data_size = lax.axis_size("dp")
    length = local * model_size
    half = local // 2
    rank = lax.axis_index("mp")
    owned = lax.dynamic_slice_in_dim(block_order, 2 * rank, 2)
    offsets = jnp.arange(local, dtype=jnp.int32)
    query_place = jnp.where(offsets < half, owned[0], owned[1]) * half + offsets % half
    every = jnp.arange(length, dtype=jnp.int32)
    key_place = jnp.repeat(block_order, half) * half + every % half
    visible = key_place[None, :] <= query_place[:, None]
    count = seqs * local

    def attend_one(pack):
        query_heads, key_heads, value_heads = pack
        scores = scores_of(query_heads, key_heads, visible, scale)
        top = jnp.max(scores, axis=-1, keepdims=True)
        expo = jnp.exp(scores - top)
        total = jnp.sum(expo, axis=-1, keepdims=True)
        probs = (expo / total).astype(jnp.bfloat16)
        logsum = top + jnp.log(total)
        attended = jnp.einsum(
            "hqk,khd->qhd", probs, value_heads, preferred_element_type=jnp.float32
        )
        return (attended.reshape(local, width).astype(jnp.bfloat16), logsum)

    def attend_back(pack):
        query_heads, key_heads, value_heads, grad_heads, logsum = pack
        scores = scores_of(query_heads, key_heads, visible, scale)
        probs = jnp.exp(scores - logsum)
        prob_grad = jnp.einsum(
            "qhd,khd->hqk", grad_heads, value_heads, preferred_element_type=jnp.float32
        )
        value_grad = jnp.einsum(
            "hqk,qhd->khd",
            probs.astype(jnp.bfloat16),
            grad_heads,
            preferred_element_type=jnp.float32,
        )
        score_grad = (
            probs * (prob_grad - jnp.sum(probs * prob_grad, axis=-1, keepdims=True))
        ).astype(jnp.bfloat16)
        query_grad = (
            jnp.einsum("hqk,khd->qhd", score_grad, key_heads, preferred_element_type=jnp.float32)
            * scale
        )
        key_grad = (
            jnp.einsum("hqk,qhd->khd", score_grad, query_heads, preferred_element_type=jnp.float32)
            * scale
        )
        return (
            query_grad.reshape(local, width),
            key_grad.reshape(length, width),
            value_grad.reshape(length, width),
        )

    hidden = tokens.reshape(count, width).astype(jnp.float32)
    saved = []
    for layer in range(LAYERS):
        params = fetch_params(weights, layer)
        qkv_full, proj_full, fc_full, fc2_full, fc_b = (
            params[0],
            params[1],
            params[2],
            params[3],
            params[4],
        )
        gains = params[5].astype(jnp.float32)
        shifts = params[6].astype(jnp.float32)
        bias_in = params[7].astype(jnp.float32)
        bias_out = params[8].astype(jnp.float32)
        normed = layer_norm(hidden, gains[0], shifts[0]).astype(jnp.bfloat16)
        mixed = jnp.dot(normed, qkv_full, preferred_element_type=jnp.float32)
        query = (mixed[:, :width] + bias_in[0]).astype(jnp.bfloat16)
        key = mixed[:, width : 2 * width].astype(jnp.bfloat16)
        value = (mixed[:, 2 * width :] + bias_in[1]).astype(jnp.bfloat16)
        keys, values = (
            lax.all_gather(key.reshape(seqs, local, width), "mp", axis=1, tiled=True),
            lax.all_gather(value.reshape(seqs, local, width), "mp", axis=1, tiled=True),
        )
        query_heads = query.reshape(seqs, local, heads, HD)
        key_heads = keys.reshape(seqs, length, heads, HD)
        value_heads = values.reshape(seqs, length, heads, HD)
        attended, logsum = lax.map(attend_one, (query_heads, key_heads, value_heads))
        attended = attended.reshape(count, width)
        middle = (
            hidden + jnp.dot(attended, proj_full, preferred_element_type=jnp.float32) + bias_out[0]
        )
        normed_two = layer_norm(middle, gains[1], shifts[1]).astype(jnp.bfloat16)
        group_rows = lax.all_gather(normed_two, "mp", axis=0, tiled=True)
        inner = jnp.dot(group_rows, fc_full, preferred_element_type=jnp.float32) + fc_b.astype(
            jnp.float32
        )
        active = jax.nn.gelu(inner, approximate=True).astype(jnp.bfloat16)

        def down_rows(start, rows, active=active, fc2_full=fc2_full):
            return jnp.dot(active, fc2_full, preferred_element_type=jnp.float32)

        reduced = lax.psum_scatter(
            down_rows(jnp.int32(0), lax.axis_size("mp") * count).astype(jnp.bfloat16),
            "mp",
            scatter_dimension=0,
            tiled=True,
        ).astype(jnp.float32)
        output = middle + reduced + bias_out[1]
        kept_params = None
        kept_pairs = None
        saved.append(
            (
                hidden,
                normed,
                query,
                key,
                value,
                logsum,
                attended,
                middle,
                group_rows,
                inner,
                kept_params,
                kept_pairs,
            )
        )
        hidden = output
    outputs = hidden.reshape(seqs, local, width)
    grad = cotangent.reshape(count, width).astype(jnp.float32)
    collected = []
    for layer in reversed(range(LAYERS)):
        (
            hidden_in,
            normed,
            query,
            key,
            value,
            logsum,
            attended,
            middle,
            group_rows,
            inner,
            kept_params,
            kept_pairs,
        ) = saved[layer]
        params = fetch_again(weights, layer)
        keys, values = (
            lax.all_gather(key.reshape(seqs, local, width), "mp", axis=1, tiled=True),
            lax.all_gather(value.reshape(seqs, local, width), "mp", axis=1, tiled=True),
        )
        qkv_full, proj_full, fc_full, fc2_full = (params[0], params[1], params[2], params[3])
        gains = params[5].astype(jnp.float32)
        shifts = params[6].astype(jnp.float32)
        out_grad = grad.astype(jnp.bfloat16)
        mlp_bias_grad = jnp.sum(out_grad.astype(jnp.float32), axis=0)
        group_grad = lax.all_gather(out_grad, "mp", axis=0, tiled=True)
        active = jax.nn.gelu(inner, approximate=True).astype(jnp.bfloat16)
        fc2_grad = jnp.einsum("nf,nd->fd", active, group_grad, preferred_element_type=jnp.float32)
        active_grad = jnp.einsum(
            "nd,fd->nf", group_grad, fc2_full, preferred_element_type=jnp.float32
        )
        _, gelu_back = jax.vjp(lambda v: jax.nn.gelu(v, approximate=True), inner)
        inner_grad = gelu_back(active_grad)[0].astype(jnp.bfloat16)
        fc_bias_grad = jnp.sum(inner_grad.astype(jnp.float32), axis=0)
        fc_grad = jnp.einsum(
            "nd,nf->df", group_rows, inner_grad, preferred_element_type=jnp.float32
        )

        def back_rows(start, rows, inner_grad=inner_grad, fc_full=fc_full):
            return jnp.einsum("nf,df->nd", inner_grad, fc_full, preferred_element_type=jnp.float32)

        normed_two_grad = lax.psum_scatter(
            back_rows(jnp.int32(0), lax.axis_size("mp") * count).astype(jnp.bfloat16),
            "mp",
            scatter_dimension=0,
            tiled=True,
        ).astype(jnp.float32)
        _, norm_two_back = jax.vjp(layer_norm, middle, gains[1], shifts[1])
        middle_part, gain_two, shift_two = norm_two_back(normed_two_grad)
        middle_grad = grad + middle_part
        branch_grad = middle_grad.astype(jnp.bfloat16)
        attn_out_bias_grad = jnp.sum(branch_grad.astype(jnp.float32), axis=0)
        proj_grad = jnp.einsum(
            "nd,ne->de", attended, branch_grad, preferred_element_type=jnp.float32
        )
        attended_grad = jnp.einsum(
            "ne,de->nd", branch_grad, proj_full, preferred_element_type=jnp.float32
        ).astype(jnp.bfloat16)
        grad_heads = attended_grad.reshape(seqs, local, heads, HD)
        query_heads = query.reshape(seqs, local, heads, HD)
        key_heads = keys.reshape(seqs, length, heads, HD)
        value_heads = values.reshape(seqs, length, heads, HD)
        query_grad, key_grad, value_grad = lax.map(
            attend_back, (query_heads, key_heads, value_heads, grad_heads, logsum)
        )
        key_part, value_part = (
            lax.psum_scatter(
                key_grad.astype(jnp.bfloat16), "mp", scatter_dimension=1, tiled=True
            ).astype(jnp.float32),
            lax.psum_scatter(
                value_grad.astype(jnp.bfloat16), "mp", scatter_dimension=1, tiled=True
            ).astype(jnp.float32),
        )
        query_round = query_grad.reshape(count, width).astype(jnp.bfloat16)
        key_round = key_part.reshape(count, width).astype(jnp.bfloat16)
        value_round = value_part.reshape(count, width).astype(jnp.bfloat16)
        mixed_grad = jnp.concatenate([query_round, key_round, value_round], axis=1)
        bias_in_grad = jnp.stack(
            [
                jnp.sum(query_round.astype(jnp.float32), axis=0),
                jnp.sum(value_round.astype(jnp.float32), axis=0),
            ]
        )
        qkv_grad = jnp.einsum("nd,ne->de", normed, mixed_grad, preferred_element_type=jnp.float32)
        normed_grad = jnp.einsum(
            "ne,de->nd", mixed_grad, qkv_full, preferred_element_type=jnp.float32
        )
        _, norm_one_back = jax.vjp(layer_norm, hidden_in, gains[0], shifts[0])
        hidden_part, gain_one, shift_one = norm_one_back(normed_grad)
        grad = middle_grad + hidden_part
        gain_grad = jnp.stack([gain_one, gain_two])
        shift_grad = jnp.stack([shift_one, shift_two])
        bias_out_grad = jnp.stack([attn_out_bias_grad, mlp_bias_grad])
        shards = (
            lax.psum_scatter(
                qkv_grad.astype(jnp.bfloat16), "dp", scatter_dimension=0, tiled=True
            ).astype(jnp.float32),
            lax.psum_scatter(
                proj_grad.astype(jnp.bfloat16), "dp", scatter_dimension=0, tiled=True
            ).astype(jnp.float32),
            lax.psum_scatter(
                fc_grad.astype(jnp.bfloat16), "dp", scatter_dimension=0, tiled=True
            ).astype(jnp.float32),
            lax.psum_scatter(
                fc2_grad.astype(jnp.bfloat16), "dp", scatter_dimension=1, tiled=True
            ).astype(jnp.float32),
            lax.psum_scatter(
                fc_bias_grad.astype(jnp.bfloat16), "dp", scatter_dimension=0, tiled=True
            ).astype(jnp.float32),
            lax.psum_scatter(
                gain_grad.astype(jnp.bfloat16), "dp", scatter_dimension=1, tiled=True
            ).astype(jnp.float32),
            lax.psum_scatter(
                shift_grad.astype(jnp.bfloat16), "dp", scatter_dimension=1, tiled=True
            ).astype(jnp.float32),
            lax.psum_scatter(
                bias_in_grad.astype(jnp.bfloat16), "dp", scatter_dimension=1, tiled=True
            ).astype(jnp.float32),
            lax.psum_scatter(
                bias_out_grad.astype(jnp.bfloat16), "dp", scatter_dimension=1, tiled=True
            ).astype(jnp.float32),
        )
        projections = (
            lax.psum_scatter(
                shards[0].astype(jnp.bfloat16), "mp", scatter_dimension=1, tiled=True
            ).astype(jnp.float32),
            lax.psum_scatter(
                shards[1].astype(jnp.bfloat16), "mp", scatter_dimension=1, tiled=True
            ).astype(jnp.float32),
        )
        smaller = lax.psum((shards[5], shards[6], shards[7], shards[8]), "mp")
        factor = 1.0 / data_size
        collected.append(
            (
                projections[0] * factor,
                projections[1] * factor,
                shards[2] * factor,
                shards[3] * factor,
                shards[4] * factor,
                smaller[0] * factor,
                smaller[1] * factor,
                smaller[2] * factor,
                smaller[3] * factor,
            )
        )
    collected = collected[::-1]
    stacked = tuple((jnp.stack([entry[index] for entry in collected]) for index in range(9)))
    input_grad = grad.reshape(seqs, local, width)
    return (
        outputs,
        input_grad,
        stacked[0],
        stacked[1],
        stacked[2],
        stacked[3],
        stacked[4],
        stacked[5],
        stacked[6],
        stacked[7],
        stacked[8],
    )


def grid_index(mesh):
    shape = dict(mesh.shape)
    return shape["dp"] // 2, shape["mp"]


def spots(planes):
    return [(z, c, y, x) for z in range(planes) for c in range(2) for y in range(2) for x in range(2)]


def flat(z, c, y, x):
    return (z * 2 + c) * 4 + y * 2 + x


def pairs_of(planes, move):
    both = [(flat(*spot), flat(*move(*spot))) for spot in spots(planes)]
    return [pair for pair in both if pair[0] != pair[1]]


AXES = ("dp", "mp")
LANES = 128


def nt(a, b):
    return lax.dot_general(a, b, (((1,), (1,)), ((), ())), preferred_element_type=jnp.float32)


def tn(a, b):
    return lax.dot_general(a, b, (((0,), (0,)), ((), ())), preferred_element_type=jnp.float32)


def nn(a, b):
    return jnp.dot(a, b, preferred_element_type=jnp.float32)


def sort_keys(slot_ref, blocks, ok, own_ref, other_ref, cat, put):
    half = blocks * LANES // 2
    cat[:half] = jnp.where(ok, own_ref[...], 0)
    cat[half:] = jnp.where(ok, other_ref[...], 0)
    for j in range(blocks):
        start = pl.multiple_of(slot_ref[j] * LANES, LANES)
        put(j, cat[pl.ds(start, LANES), :])


def two_heads(rows, first):
    zero = jnp.zeros_like(rows)
    return jnp.concatenate([jnp.where(first, rows, zero), jnp.where(first, zero, rows)], axis=0)


def attend_kernel(width, blocks, qblocks, place_ref, slot_ref, q_ref, ko_ref, ks_ref, vo_ref, vs_ref,
                  o_ref, lse_ref, cat, ksort, vturn):
    lane = lax.broadcasted_iota(jnp.int32, (1, LANES), 1)
    ok = lane + pl.program_id(0) * LANES < width
    first = lane < HD

    def put_k(j, rows):
        ksort[j * LANES:(j + 1) * LANES, :] = rows

    def put_v(j, rows):
        vturn[:, j * LANES:(j + 1) * LANES] = rows.astype(jnp.float32).T.astype(jnp.bfloat16)

    sort_keys(slot_ref, blocks, ok, ko_ref, ks_ref, cat, put_k)
    sort_keys(slot_ref, blocks, ok, vo_ref, vs_ref, cat, put_v)

    def one(b, carry):
        place = place_ref[b]
        here = pl.ds(pl.multiple_of(b * LANES, LANES), LANES)
        rows = (jnp.where(ok, q_ref[here, :], 0) * (HD ** -0.5)).astype(jnp.bfloat16)
        q2 = two_heads(rows, first)
        for n in range(1, blocks // 2 + 1):
            @pl.when(place // 2 == n - 1)
            def _(n=n):
                keys = 2 * LANES * n
                s = nt(ksort[:keys, :], q2)
                row = lax.broadcasted_iota(jnp.int32, (2 * LANES, 2 * LANES), 0) + (keys - 2 * LANES)
                col = lax.broadcasted_iota(jnp.int32, (2 * LANES, 2 * LANES), 1) % LANES + place * LANES
                tail = jnp.where(row <= col, s[keys - 2 * LANES:], -1e30)
                s = tail if n == 1 else jnp.concatenate([s[:keys - 2 * LANES], tail], axis=0)
                top = jnp.max(s, axis=0, keepdims=True)
                e = jnp.exp(s - top)
                total = jnp.sum(e, axis=0, keepdims=True)
                turned = nn(vturn[:, :keys], e.astype(jnp.bfloat16)) / total
                joined = jnp.concatenate([turned[:HD, :LANES], turned[HD:, LANES:]], axis=0)
                o_ref[here, :] = joined.T.astype(jnp.bfloat16)
                lse = top + jnp.log(total)
                lse_ref[0, 0:1, here] = lse[:, :LANES]
                lse_ref[0, 1:2, here] = lse[:, LANES:]
        return carry

    lax.fori_loop(0, qblocks, one, 0)


def attend_back_kernel(width, blocks, qblocks, place_ref, slot_ref, q_ref, ko_ref, ks_ref, vo_ref, vs_ref,
                       do_ref, o_ref, lse_ref, dq_ref, dko_ref, dks_ref, dvo_ref, dvs_ref,
                       cat, ksort, kturn, vsort, dk, dv, loose):
    lane = lax.broadcasted_iota(jnp.int32, (1, LANES), 1)
    ok = lane + pl.program_id(0) * LANES < width
    first = lane < HD

    def put_k(j, rows):
        ksort[j * LANES:(j + 1) * LANES, :] = rows
        kturn[:, j * LANES:(j + 1) * LANES] = rows.astype(jnp.float32).T.astype(jnp.bfloat16)

    def put_v(j, rows):
        vsort[j * LANES:(j + 1) * LANES, :] = rows

    sort_keys(slot_ref, blocks, ok, ko_ref, ks_ref, cat, put_k)
    sort_keys(slot_ref, blocks, ok, vo_ref, vs_ref, cat, put_v)
    dk[...] = jnp.zeros_like(dk)
    dv[...] = jnp.zeros_like(dv)

    def one(b, carry):
        place = place_ref[b]
        here = pl.ds(pl.multiple_of(b * LANES, LANES), LANES)
        rows = (jnp.where(ok, q_ref[here, :], 0) * (HD ** -0.5)).astype(jnp.bfloat16)
        q2 = two_heads(rows, first)
        do = jnp.where(ok, do_ref[here, :], 0)
        do2 = two_heads(do, first)
        both = (do.astype(jnp.float32) * jnp.where(ok, o_ref[here, :], 0).astype(jnp.float32)).T
        delta = jnp.concatenate(
            [jnp.sum(both[:HD], axis=0, keepdims=True), jnp.sum(both[HD:], axis=0, keepdims=True)], axis=1
        )
        lse = jnp.concatenate([lse_ref[0, 0:1, here], lse_ref[0, 1:2, here]], axis=1)
        for n in range(1, blocks // 2 + 1):
            @pl.when(place // 2 == n - 1)
            def _(n=n):
                keys = 2 * LANES * n
                s = nt(ksort[:keys, :], q2)
                row = lax.broadcasted_iota(jnp.int32, (2 * LANES, 2 * LANES), 0) + (keys - 2 * LANES)
                col = lax.broadcasted_iota(jnp.int32, (2 * LANES, 2 * LANES), 1) % LANES + place * LANES
                tail = jnp.where(row <= col, s[keys - 2 * LANES:], -1e30)
                s = tail if n == 1 else jnp.concatenate([s[:keys - 2 * LANES], tail], axis=0)
                p = jnp.exp(s - lse)
                dp = nt(vsort[:keys, :], do2)
                ds = (p * (dp - delta)).astype(jnp.bfloat16)
                dv[:keys, :] += nn(p.astype(jnp.bfloat16), do2)
                dk[:keys, :] += nn(ds, q2)
                turned = nn(kturn[:, :keys], ds) * (HD ** -0.5)
                joined = jnp.concatenate([turned[:HD, :LANES], turned[HD:, LANES:]], axis=0)
                dq_ref[here, :] = joined.T.astype(jnp.bfloat16)
        return carry

    lax.fori_loop(0, qblocks, one, 0)
    half = blocks * LANES // 2
    for source, mine, theirs in ((dk, dko_ref, dks_ref), (dv, dvo_ref, dvs_ref)):
        for j in range(blocks):
            start = pl.multiple_of(slot_ref[j] * LANES, LANES)
            loose[pl.ds(start, LANES), :] = source[j * LANES:(j + 1) * LANES, :]
        mine[...] = loose[:half]
        theirs[...] = loose[half:].astype(jnp.bfloat16)


def attention_specs(rows):
    tall = pl.BlockSpec((rows, LANES), lambda i, *_: (0, i))
    stat = pl.BlockSpec((1, 2, rows), lambda i, *_: (i, 0, 0))
    return tall, stat


def attention(place, slot, q, ko, ks, vo, vs):
    rows, width = q.shape
    steps = -(-width // LANES)
    blocks, keys = slot.shape[0], slot.shape[0] * LANES
    tall, stat = attention_specs(rows)
    elems = rows * keys * steps * 2
    return pl.pallas_call(
        functools.partial(attend_kernel, width, blocks, place.shape[0]),
        grid_spec=pltpu.PrefetchScalarGridSpec(
            num_scalar_prefetch=2,
            grid=(steps,),
            in_specs=[tall] * 5,
            out_specs=[tall, stat],
            scratch_shapes=[
                pltpu.VMEM((keys, LANES), jnp.bfloat16),
                pltpu.VMEM((keys, LANES), jnp.bfloat16),
                pltpu.VMEM((LANES, keys), jnp.bfloat16),
            ],
        ),
        out_shape=[
            jax.ShapeDtypeStruct((rows, width), jnp.bfloat16),
            jax.ShapeDtypeStruct((steps, 2, rows), jnp.float32),
        ],
        cost_estimate=pl.CostEstimate(flops=elems * HD * 8, bytes_accessed=rows * width * 12, transcendentals=elems),
        compiler_params=pltpu.CompilerParams(vmem_limit_bytes=40 * 2 ** 20),
        name="attention",
    )(place, slot, q, ko, ks, vo, vs)


def attention_back(place, slot, q, ko, ks, vo, vs, do, o, lse):
    rows, width = q.shape
    steps = -(-width // LANES)
    blocks, keys = slot.shape[0], slot.shape[0] * LANES
    tall, stat = attention_specs(rows)
    elems = rows * keys * steps * 2
    wide = jax.ShapeDtypeStruct((rows, width), jnp.float32)
    thin = jax.ShapeDtypeStruct((rows, width), jnp.bfloat16)
    return pl.pallas_call(
        functools.partial(attend_back_kernel, width, blocks, place.shape[0]),
        grid_spec=pltpu.PrefetchScalarGridSpec(
            num_scalar_prefetch=2,
            grid=(steps,),
            in_specs=[tall] * 7 + [stat],
            out_specs=[tall] * 5,
            scratch_shapes=[
                pltpu.VMEM((keys, LANES), jnp.bfloat16),
                pltpu.VMEM((keys, LANES), jnp.bfloat16),
                pltpu.VMEM((LANES, keys), jnp.bfloat16),
                pltpu.VMEM((keys, LANES), jnp.bfloat16),
                pltpu.VMEM((keys, LANES), jnp.float32),
                pltpu.VMEM((keys, LANES), jnp.float32),
                pltpu.VMEM((keys, LANES), jnp.float32),
            ],
        ),
        out_shape=[thin, wide, thin, wide, thin],
        cost_estimate=pl.CostEstimate(flops=elems * HD * 20, bytes_accessed=rows * width * 30, transcendentals=elems),
        compiler_params=pltpu.CompilerParams(vmem_limit_bytes=40 * 2 ** 20),
        name="attention_back",
    )(place, slot, q, ko, ks, vo, vs, do, o, lse)


def bf(value):
    return value.astype(jnp.bfloat16)


def f32(value):
    return value.astype(jnp.float32)


def norm_parts(value):
    mean = jnp.mean(value, axis=-1, keepdims=True)
    centred = value - mean
    spread = jnp.mean(centred * centred, axis=-1, keepdims=True)
    return centred, lax.rsqrt(spread + eps)


def norm_back(grad, value, gain):
    centred, rate = norm_parts(value)
    hat = centred * rate
    scaled = grad * gain
    inner = scaled - jnp.mean(scaled, axis=-1, keepdims=True) - hat * jnp.mean(scaled * hat, axis=-1, keepdims=True)
    return inner * rate, jnp.sum(grad * hat, axis=0), jnp.sum(grad, axis=0)


def quick_body(
    planes,
    tokens,
    cotangent,
    block_order,
    qkv_weight,
    proj_weight,
    fc_weight,
    fc2_weight,
    fc_bias,
    norm_gain,
    norm_shift,
    attn_bias,
    out_bias,
):
    seqs, local, width = tokens.shape
    slots = local // LANES
    dp_rank = lax.axis_index("dp")
    mp_rank = lax.axis_index("mp")
    core, row, col = dp_rank % 2, mp_rank // 2, mp_rank % 2
    over_x = pairs_of(planes, lambda z, c, y, x: (z, c, y, 1 - x))
    over_y = pairs_of(planes, lambda z, c, y, x: (z, c, 1 - y, x))
    over_c = pairs_of(planes, lambda z, c, y, x: (z, 1 - c, y, x))
    swap_yc = pairs_of(planes, lambda z, c, y, x: (z, y, c, x))
    swap_xc = pairs_of(planes, lambda z, c, y, x: (z, x, y, c))

    along_z = [
        [flat(z, c, y, x) for z in range(planes)] for c in range(2) for y in range(2) for x in range(2)
    ]

    def go(value, pairs):
        return lax.ppermute(value, AXES, pairs)

    def turn_yc(value):
        return jnp.where(row == core, value, go(value, swap_yc))

    def turn_xc(value):
        return jnp.where(col == core, value, go(value, swap_xc))

    def sum_z(value):
        return lax.psum_scatter(value, AXES, axis_index_groups=along_z, scatter_dimension=0, tiled=True)

    def spread_in(value):
        mine = lax.dynamic_index_in_dim(value, col, 0, keepdims=False)
        theirs = lax.dynamic_index_in_dim(value, 1 - col, 0, keepdims=False)
        return jnp.concatenate([turn_yc(mine), turn_yc(go(theirs, over_x))], axis=0)

    def spread_out(value):
        mine = turn_yc(value[:local])
        theirs = go(turn_yc(value[local:]), over_x)
        front = jnp.where(col == 0, mine, theirs)
        back = jnp.where(col == 0, theirs, mine)
        return f32(jnp.stack([front, back]))

    ranks = jnp.stack([2 * core + col, 2 * core + 1 - col])
    others = jnp.stack([2 * (1 - core) + col, 2 * (1 - core) + 1 - col])

    def places(which):
        return block_order.reshape(-1, slots)[which].reshape(-1)

    place = places(ranks)
    keyed = jnp.concatenate([place, places(others)])
    blocks = keyed.shape[0]
    order = jnp.arange(blocks, dtype=jnp.int32)
    slot = jnp.sum(jnp.where(keyed[None, :] == order[:, None], order[None, :], 0), axis=1).astype(jnp.int32)

    def add_pair(a, b):
        return bf(f32(a) + f32(b))

    def core_columns(value, which):
        parts = value.reshape(value.shape[0], planes, 2, -1)
        return lax.dynamic_index_in_dim(parts, which, 2, keepdims=False).reshape(value.shape[0], -1)

    def gather_dp(piece):
        return lax.all_gather(piece, "dp", axis=0, tiled=True)

    def group(value):
        beside = go(value, over_c)
        across = go(value, over_y)
        return jnp.concatenate([value, beside, across, go(across, over_c)], axis=0)

    def ungroup(multiply, rows):
        far = multiply(rows // 2, rows // 2)
        near = multiply(0, rows // 2)
        quarter = rows // 4
        sent = far[:quarter] + f32(go(bf(far[quarter:]), over_c))
        back = go(bf(sent), over_y)
        return near[:quarter] + f32(go(bf(near[quarter:]), over_c)) + f32(back)

    small = jnp.concatenate(
        [norm_gain, norm_shift, attn_bias, out_bias, fc_bias[:, None, :]], axis=1
    )
    small = lax.all_gather(small, "dp", axis=0)
    small = jnp.transpose(small, (1, 2, 0, 3)).reshape(LAYERS, 9, width)
    units_bias = turn_xc(small[:, 8])
    small = f32(small)

    fetched = []
    for layer in range(LAYERS):
        qkv = qkv_weight[layer]
        fetched.append(
            dict(
                k=gather_dp(qkv[:, width:2 * width]),
                v=gather_dp(qkv[:, 2 * width:]),
                q=gather_dp(qkv[:, :width]),
                proj=gather_dp(proj_weight[layer]),
                fc=turn_xc(gather_dp(fc_weight[layer])),
                fc2=turn_xc(gather_dp(fc2_weight[layer].T)),
                gain=small[layer, 0:2],
                shift=small[layer, 2:4],
                bias_in=small[layer, 4:6],
                bias_out=small[layer, 6:8],
                fc_b=f32(units_bias[layer]),
            )
        )

    hidden = f32(spread_in(tokens))
    grad_in = spread_in(cotangent)
    saved = []
    for layer in range(LAYERS):
        w = fetched[layer]
        centred, rate = norm_parts(hidden)
        normed = bf(centred * rate * w["gain"][0] + w["shift"][0])
        key = bf(nn(normed, w["k"]))
        key_other = go(key, over_c)
        value = bf(nn(normed, w["v"]) + w["bias_in"][1])
        value_other = go(value, over_c)
        query = bf(nn(normed, w["q"]) + w["bias_in"][0])
        attended, lse = attention(place, slot, query, key, key_other, value, value_other)
        middle = hidden + nn(attended, w["proj"]) + w["bias_out"][0]
        centred, rate = norm_parts(middle)
        normed_two = bf(centred * rate * w["gain"][1] + w["shift"][1])
        rows_in = group(normed_two)
        inner = nn(rows_in, w["fc"]) + w["fc_b"]
        active = bf(jax.nn.gelu(inner, approximate=True))

        def down(start, rows, active=active, w=w):
            return nt(active[start:start + rows], w["fc2"])

        output = middle + ungroup(down, rows_in.shape[0]) + w["bias_out"][1]
        saved.append((hidden, normed, query, key, key_other, value, value_other, attended, lse, middle, rows_in, inner, active))
        hidden = output
    outputs = spread_out(bf(hidden))

    grad = f32(grad_in)
    factor = 1.0 / lax.axis_size("dp")
    third, fourth = 3 * width // 4, width // 4
    results = [None] * LAYERS
    for layer in reversed(range(LAYERS)):
        w = fetched[layer]
        (hidden, normed, query, key, key_other, value, value_other, attended, lse, middle, rows_in, inner, active) = saved[layer]
        out_grad = bf(grad)
        mlp_bias_grad = jnp.sum(f32(out_grad), axis=0)
        rows_grad = group(out_grad)
        _, gelu_back = jax.vjp(lambda v: jax.nn.gelu(v, approximate=True), inner)
        inner_grad = bf(gelu_back(nn(rows_grad, w["fc2"]))[0])

        def up(start, rows, inner_grad=inner_grad, w=w):
            return nt(inner_grad[start:start + rows], w["fc"])

        normed_two_grad = ungroup(up, rows_in.shape[0])
        fc2_grad = bf(tn(rows_grad, active))
        fc_grad = bf(tn(rows_in, inner_grad))
        units_grad = jnp.sum(f32(inner_grad), axis=0)
        part, gain_two, shift_two = norm_back(normed_two_grad, middle, w["gain"][1])
        middle_grad = grad + part
        branch_grad = bf(middle_grad)
        attn_out_grad = jnp.sum(f32(branch_grad), axis=0)
        attended_grad = bf(nt(branch_grad, w["proj"]))
        dq, dk_mine, dk_theirs, dv_mine, dv_theirs = attention_back(
            place, slot, query, key, key_other, value, value_other, attended_grad, attended, lse
        )
        dk = bf(dk_mine + f32(go(dk_theirs, over_c)))
        dv = bf(dv_mine + f32(go(dv_theirs, over_c)))
        bias_in_grad = jnp.stack([jnp.sum(f32(dq), axis=0), jnp.sum(f32(dv), axis=0)])
        normed_grad = nt(dq, w["q"]) + nt(dk, w["k"]) + nt(dv, w["v"])
        part, gain_one, shift_one = norm_back(normed_grad, hidden, w["gain"][0])
        grad = middle_grad + part

        mixed = jnp.concatenate([dq, dk, dv], axis=1)
        keep_cols = core_columns(normed, core), core_columns(attended, core)
        send_cols = core_columns(normed, 1 - core), core_columns(attended, 1 - core)

        def column(cols, near_y, near_x):
            index = 2 * (row if near_y else 1 - row) + (col if near_x else 1 - col)
            first = lax.dynamic_slice_in_dim(mixed, index * third, third, axis=1)
            second = lax.dynamic_slice_in_dim(branch_grad, index * fourth, fourth, axis=1)
            return bf(jnp.concatenate([tn(cols[0], first), tn(cols[1], second)], axis=1))

        def chip_sum(near_y, near_x):
            return add_pair(column(keep_cols, near_y, near_x), go(column(send_cols, near_y, near_x), over_c))

        def row_sum(near_x):
            return add_pair(chip_sum(True, near_x), go(chip_sum(False, near_x), over_y))

        far_side = go(row_sum(False), over_x)
        attn_part = sum_z(add_pair(row_sum(True), far_side))

        def units_sum(value):
            quarters = value.reshape(planes, 2, -1, width)
            kept = lax.dynamic_index_in_dim(quarters, col, 1, keepdims=False)
            sent = lax.dynamic_index_in_dim(quarters, 1 - col, 1, keepdims=False)
            part = add_pair(kept, go(sent, over_x)).reshape(-1, width)
            return turn_xc(sum_z(part))

        fc2_part = units_sum(fc2_grad)
        fc_part = units_sum(fc_grad)
        sums = jnp.concatenate(
            [
                jnp.stack([gain_one, gain_two, shift_one, shift_two]),
                bias_in_grad,
                jnp.stack([attn_out_grad, mlp_bias_grad]),
            ],
            axis=0,
        )
        results[layer] = (attn_part, fc_part, fc2_part, sums, units_grad)

    input_grad = spread_out(bf(grad))
    sums = jnp.stack([entry[3] for entry in results])
    sums = sums + go(sums, over_x)
    sums = sums + go(sums, over_y)
    units = turn_xc(jnp.stack([entry[4] for entry in results]))
    sums = jnp.concatenate([sums, units[:, None, :]], axis=1)
    sums = lax.psum_scatter(sums, "dp", scatter_dimension=2, tiled=True) * factor
    attn_part = jnp.stack([f32(entry[0]) for entry in results]) * factor
    return (
        outputs,
        input_grad,
        attn_part[:, :, :third],
        attn_part[:, :, third:],
        jnp.stack([f32(entry[1]) for entry in results]) * factor,
        jnp.stack([f32(entry[2]).T for entry in results]) * factor,
        sums[:, 8],
        sums[:, 0:2],
        sums[:, 2:4],
        sums[:, 4:6],
        sums[:, 6:8],
    )


def solution(mesh):
    planes = mesh.shape["dp"] // 2
    if mesh.shape["mp"] == 4:
        body = functools.partial(quick_body, planes)
    else:
        body = general_body
    return jax.shard_map(
        body,
        mesh=mesh,
        in_specs=(
            P("dp", "mp", None),
            P("dp", "mp", None),
            P(),
            P(None, "dp", None),
            P(None, "dp", None),
            P(None, "dp", "mp"),
            P(None, "mp", "dp"),
            P(None, ("mp", "dp")),
            P(None, None, "dp"),
            P(None, None, "dp"),
            P(None, None, "dp"),
            P(None, None, "dp"),
        ),
        out_specs=(
            P("dp", "mp", None),
            P("dp", "mp", None),
            P(None, "dp", "mp"),
            P(None, "dp", "mp"),
            P(None, "dp", "mp"),
            P(None, "mp", "dp"),
            P(None, ("mp", "dp")),
            P(None, None, "dp"),
            P(None, None, "dp"),
            P(None, None, "dp"),
            P(None, None, "dp"),
        ),
        check_vma=False,
    )
```

```python
import functools

import jax
import jax.numpy as jnp
from jax import lax
from jax.experimental import pallas as pl
from jax.experimental.pallas import tpu as pltpu
from jax.sharding import PartitionSpec as P

HD = 64
LAYERS = 2


eps = 1e-05


def layer_norm(value, gain, shift):
    mean = jnp.mean(value, axis=-1, keepdims=True)
    centred = value - mean
    spread = jnp.mean(centred * centred, axis=-1, keepdims=True)
    return centred * lax.rsqrt(spread + eps) * gain + shift


def fetch_params(weights, layer):
    pieces = tuple((w[layer] for w in weights))
    return (
        lax.all_gather(pieces[0], "dp", axis=0, tiled=True),
        lax.all_gather(pieces[1], "dp", axis=0, tiled=True),
        lax.all_gather(pieces[2], "dp", axis=0, tiled=True),
        lax.all_gather(pieces[3], "dp", axis=1, tiled=True),
        lax.all_gather(pieces[4], "dp", axis=0, tiled=True),
        lax.all_gather(pieces[5], "dp", axis=1, tiled=True),
        lax.all_gather(pieces[6], "dp", axis=1, tiled=True),
        lax.all_gather(pieces[7], "dp", axis=1, tiled=True),
        lax.all_gather(pieces[8], "dp", axis=1, tiled=True),
    )


def fetch_again(weights, layer):
    pieces = tuple((w[layer] for w in weights))
    return (
        lax.all_gather(pieces[0], "dp", axis=0, tiled=True),
        lax.all_gather(pieces[1], "dp", axis=0, tiled=True),
        lax.all_gather(pieces[2], "dp", axis=0, tiled=True),
        lax.all_gather(pieces[3], "dp", axis=1, tiled=True),
        lax.all_gather(pieces[4], "dp", axis=0, tiled=True),
        lax.all_gather(pieces[5], "dp", axis=1, tiled=True),
        lax.all_gather(pieces[6], "dp", axis=1, tiled=True),
        lax.all_gather(pieces[7], "dp", axis=1, tiled=True),
        lax.all_gather(pieces[8], "dp", axis=1, tiled=True),
    )


def scores_of(query_heads, key_heads, visible, scale):
    scores = (
        jnp.einsum("qhd,khd->hqk", query_heads, key_heads, preferred_element_type=jnp.float32)
        * scale
    )
    return jnp.where(visible, scores, -1e30)


def general_body(
    tokens,
    cotangent,
    block_order,
    qkv_weight,
    proj_weight,
    fc_weight,
    fc2_weight,
    fc_bias,
    norm_gain,
    norm_shift,
    attn_bias,
    out_bias,
):
    weights = (
        qkv_weight,
        proj_weight,
        fc_weight,
        fc2_weight,
        fc_bias,
        norm_gain,
        norm_shift,
        attn_bias,
        out_bias,
    )
    seqs, local, width = tokens.shape
    heads = width // HD
    scale = HD ** (-0.5)
    model_size = lax.axis_size("mp")
    data_size = lax.axis_size("dp")
    length = local * model_size
    half = local // 2
    rank = lax.axis_index("mp")
    owned = lax.dynamic_slice_in_dim(block_order, 2 * rank, 2)
    offsets = jnp.arange(local, dtype=jnp.int32)
    query_place = jnp.where(offsets < half, owned[0], owned[1]) * half + offsets % half
    every = jnp.arange(length, dtype=jnp.int32)
    key_place = jnp.repeat(block_order, half) * half + every % half
    visible = key_place[None, :] <= query_place[:, None]
    count = seqs * local

    def attend_one(pack):
        query_heads, key_heads, value_heads = pack
        scores = scores_of(query_heads, key_heads, visible, scale)
        top = jnp.max(scores, axis=-1, keepdims=True)
        expo = jnp.exp(scores - top)
        total = jnp.sum(expo, axis=-1, keepdims=True)
        probs = (expo / total).astype(jnp.bfloat16)
        logsum = top + jnp.log(total)
        attended = jnp.einsum(
            "hqk,khd->qhd", probs, value_heads, preferred_element_type=jnp.float32
        )
        return (attended.reshape(local, width).astype(jnp.bfloat16), logsum)

    def attend_back(pack):
        query_heads, key_heads, value_heads, grad_heads, logsum = pack
        scores = scores_of(query_heads, key_heads, visible, scale)
        probs = jnp.exp(scores - logsum)
        prob_grad = jnp.einsum(
            "qhd,khd->hqk", grad_heads, value_heads, preferred_element_type=jnp.float32
        )
        value_grad = jnp.einsum(
            "hqk,qhd->khd",
            probs.astype(jnp.bfloat16),
            grad_heads,
            preferred_element_type=jnp.float32,
        )
        score_grad = (
            probs * (prob_grad - jnp.sum(probs * prob_grad, axis=-1, keepdims=True))
        ).astype(jnp.bfloat16)
        query_grad = (
            jnp.einsum("hqk,khd->qhd", score_grad, key_heads, preferred_element_type=jnp.float32)
            * scale
        )
        key_grad = (
            jnp.einsum("hqk,qhd->khd", score_grad, query_heads, preferred_element_type=jnp.float32)
            * scale
        )
        return (
            query_grad.reshape(local, width),
            key_grad.reshape(length, width),
            value_grad.reshape(length, width),
        )

    hidden = tokens.reshape(count, width).astype(jnp.float32)
    saved = []
    for layer in range(LAYERS):
        params = fetch_params(weights, layer)
        qkv_full, proj_full, fc_full, fc2_full, fc_b = (
            params[0],
            params[1],
            params[2],
            params[3],
            params[4],
        )
        gains = params[5].astype(jnp.float32)
        shifts = params[6].astype(jnp.float32)
        bias_in = params[7].astype(jnp.float32)
        bias_out = params[8].astype(jnp.float32)
        normed = layer_norm(hidden, gains[0], shifts[0]).astype(jnp.bfloat16)
        mixed = jnp.dot(normed, qkv_full, preferred_element_type=jnp.float32)
        query = (mixed[:, :width] + bias_in[0]).astype(jnp.bfloat16)
        key = mixed[:, width : 2 * width].astype(jnp.bfloat16)
        value = (mixed[:, 2 * width :] + bias_in[1]).astype(jnp.bfloat16)
        keys, values = (
            lax.all_gather(key.reshape(seqs, local, width), "mp", axis=1, tiled=True),
            lax.all_gather(value.reshape(seqs, local, width), "mp", axis=1, tiled=True),
        )
        query_heads = query.reshape(seqs, local, heads, HD)
        key_heads = keys.reshape(seqs, length, heads, HD)
        value_heads = values.reshape(seqs, length, heads, HD)
        attended, logsum = lax.map(attend_one, (query_heads, key_heads, value_heads))
        attended = attended.reshape(count, width)
        middle = (
            hidden + jnp.dot(attended, proj_full, preferred_element_type=jnp.float32) + bias_out[0]
        )
        normed_two = layer_norm(middle, gains[1], shifts[1]).astype(jnp.bfloat16)
        group_rows = lax.all_gather(normed_two, "mp", axis=0, tiled=True)
        inner = jnp.dot(group_rows, fc_full, preferred_element_type=jnp.float32) + fc_b.astype(
            jnp.float32
        )
        active = jax.nn.gelu(inner, approximate=True).astype(jnp.bfloat16)

        def down_rows(start, rows, active=active, fc2_full=fc2_full):
            return jnp.dot(active, fc2_full, preferred_element_type=jnp.float32)

        reduced = lax.psum_scatter(
            down_rows(jnp.int32(0), lax.axis_size("mp") * count).astype(jnp.bfloat16),
            "mp",
            scatter_dimension=0,
            tiled=True,
        ).astype(jnp.float32)
        output = middle + reduced + bias_out[1]
        kept_params = None
        kept_pairs = None
        saved.append(
            (
                hidden,
                normed,
                query,
                key,
                value,
                logsum,
                attended,
                middle,
                group_rows,
                inner,
                kept_params,
                kept_pairs,
            )
        )
        hidden = output
    outputs = hidden.reshape(seqs, local, width)
    grad = cotangent.reshape(count, width).astype(jnp.float32)
    collected = []
    for layer in reversed(range(LAYERS)):
        (
            hidden_in,
            normed,
            query,
            key,
            value,
            logsum,
            attended,
            middle,
            group_rows,
            inner,
            kept_params,
            kept_pairs,
        ) = saved[layer]
        params = fetch_again(weights, layer)
        keys, values = (
            lax.all_gather(key.reshape(seqs, local, width), "mp", axis=1, tiled=True),
            lax.all_gather(value.reshape(seqs, local, width), "mp", axis=1, tiled=True),
        )
        qkv_full, proj_full, fc_full, fc2_full = (params[0], params[1], params[2], params[3])
        gains = params[5].astype(jnp.float32)
        shifts = params[6].astype(jnp.float32)
        out_grad = grad.astype(jnp.bfloat16)
        mlp_bias_grad = jnp.sum(out_grad.astype(jnp.float32), axis=0)
        group_grad = lax.all_gather(out_grad, "mp", axis=0, tiled=True)
        active = jax.nn.gelu(inner, approximate=True).astype(jnp.bfloat16)
        fc2_grad = jnp.einsum("nf,nd->fd", active, group_grad, preferred_element_type=jnp.float32)
        active_grad = jnp.einsum(
            "nd,fd->nf", group_grad, fc2_full, preferred_element_type=jnp.float32
        )
        _, gelu_back = jax.vjp(lambda v: jax.nn.gelu(v, approximate=True), inner)
        inner_grad = gelu_back(active_grad)[0].astype(jnp.bfloat16)
        fc_bias_grad = jnp.sum(inner_grad.astype(jnp.float32), axis=0)
        fc_grad = jnp.einsum(
            "nd,nf->df", group_rows, inner_grad, preferred_element_type=jnp.float32
        )

        def back_rows(start, rows, inner_grad=inner_grad, fc_full=fc_full):
            return jnp.einsum("nf,df->nd", inner_grad, fc_full, preferred_element_type=jnp.float32)

        normed_two_grad = lax.psum_scatter(
            back_rows(jnp.int32(0), lax.axis_size("mp") * count).astype(jnp.bfloat16),
            "mp",
            scatter_dimension=0,
            tiled=True,
        ).astype(jnp.float32)
        _, norm_two_back = jax.vjp(layer_norm, middle, gains[1], shifts[1])
        middle_part, gain_two, shift_two = norm_two_back(normed_two_grad)
        middle_grad = grad + middle_part
        branch_grad = middle_grad.astype(jnp.bfloat16)
        attn_out_bias_grad = jnp.sum(branch_grad.astype(jnp.float32), axis=0)
        proj_grad = jnp.einsum(
            "nd,ne->de", attended, branch_grad, preferred_element_type=jnp.float32
        )
        attended_grad = jnp.einsum(
            "ne,de->nd", branch_grad, proj_full, preferred_element_type=jnp.float32
        ).astype(jnp.bfloat16)
        grad_heads = attended_grad.reshape(seqs, local, heads, HD)
        query_heads = query.reshape(seqs, local, heads, HD)
        key_heads = keys.reshape(seqs, length, heads, HD)
        value_heads = values.reshape(seqs, length, heads, HD)
        query_grad, key_grad, value_grad = lax.map(
            attend_back, (query_heads, key_heads, value_heads, grad_heads, logsum)
        )
        key_part, value_part = (
            lax.psum_scatter(
                key_grad.astype(jnp.bfloat16), "mp", scatter_dimension=1, tiled=True
            ).astype(jnp.float32),
            lax.psum_scatter(
                value_grad.astype(jnp.bfloat16), "mp", scatter_dimension=1, tiled=True
            ).astype(jnp.float32),
        )
        query_round = query_grad.reshape(count, width).astype(jnp.bfloat16)
        key_round = key_part.reshape(count, width).astype(jnp.bfloat16)
        value_round = value_part.reshape(count, width).astype(jnp.bfloat16)
        mixed_grad = jnp.concatenate([query_round, key_round, value_round], axis=1)
        bias_in_grad = jnp.stack(
            [
                jnp.sum(query_round.astype(jnp.float32), axis=0),
                jnp.sum(value_round.astype(jnp.float32), axis=0),
            ]
        )
        qkv_grad = jnp.einsum("nd,ne->de", normed, mixed_grad, preferred_element_type=jnp.float32)
        normed_grad = jnp.einsum(
            "ne,de->nd", mixed_grad, qkv_full, preferred_element_type=jnp.float32
        )
        _, norm_one_back = jax.vjp(layer_norm, hidden_in, gains[0], shifts[0])
        hidden_part, gain_one, shift_one = norm_one_back(normed_grad)
        grad = middle_grad + hidden_part
        gain_grad = jnp.stack([gain_one, gain_two])
        shift_grad = jnp.stack([shift_one, shift_two])
        bias_out_grad = jnp.stack([attn_out_bias_grad, mlp_bias_grad])
        shards = (
            lax.psum_scatter(
                qkv_grad.astype(jnp.bfloat16), "dp", scatter_dimension=0, tiled=True
            ).astype(jnp.float32),
            lax.psum_scatter(
                proj_grad.astype(jnp.bfloat16), "dp", scatter_dimension=0, tiled=True
            ).astype(jnp.float32),
            lax.psum_scatter(
                fc_grad.astype(jnp.bfloat16), "dp", scatter_dimension=0, tiled=True
            ).astype(jnp.float32),
            lax.psum_scatter(
                fc2_grad.astype(jnp.bfloat16), "dp", scatter_dimension=1, tiled=True
            ).astype(jnp.float32),
            lax.psum_scatter(
                fc_bias_grad.astype(jnp.bfloat16), "dp", scatter_dimension=0, tiled=True
            ).astype(jnp.float32),
            lax.psum_scatter(
                gain_grad.astype(jnp.bfloat16), "dp", scatter_dimension=1, tiled=True
            ).astype(jnp.float32),
            lax.psum_scatter(
                shift_grad.astype(jnp.bfloat16), "dp", scatter_dimension=1, tiled=True
            ).astype(jnp.float32),
            lax.psum_scatter(
                bias_in_grad.astype(jnp.bfloat16), "dp", scatter_dimension=1, tiled=True
            ).astype(jnp.float32),
            lax.psum_scatter(
                bias_out_grad.astype(jnp.bfloat16), "dp", scatter_dimension=1, tiled=True
            ).astype(jnp.float32),
        )
        projections = (
            lax.psum_scatter(
                shards[0].astype(jnp.bfloat16), "mp", scatter_dimension=1, tiled=True
            ).astype(jnp.float32),
            lax.psum_scatter(
                shards[1].astype(jnp.bfloat16), "mp", scatter_dimension=1, tiled=True
            ).astype(jnp.float32),
        )
        smaller = lax.psum((shards[5], shards[6], shards[7], shards[8]), "mp")
        factor = 1.0 / data_size
        collected.append(
            (
                projections[0] * factor,
                projections[1] * factor,
                shards[2] * factor,
                shards[3] * factor,
                shards[4] * factor,
                smaller[0] * factor,
                smaller[1] * factor,
                smaller[2] * factor,
                smaller[3] * factor,
            )
        )
    collected = collected[::-1]
    stacked = tuple((jnp.stack([entry[index] for entry in collected]) for index in range(9)))
    input_grad = grad.reshape(seqs, local, width)
    return (
        outputs,
        input_grad,
        stacked[0],
        stacked[1],
        stacked[2],
        stacked[3],
        stacked[4],
        stacked[5],
        stacked[6],
        stacked[7],
        stacked[8],
    )


def grid_index(mesh):
    shape = dict(mesh.shape)
    return shape["dp"] // 2, shape["mp"]


def spots(planes):
    return [(z, c, y, x) for z in range(planes) for c in range(2) for y in range(2) for x in range(2)]


def flat(z, c, y, x):
    return (z * 2 + c) * 4 + y * 2 + x


def pairs_of(planes, move):
    both = [(flat(*spot), flat(*move(*spot))) for spot in spots(planes)]
    return [pair for pair in both if pair[0] != pair[1]]


AXES = ("dp", "mp")
LANES = 128


def nt(a, b):
    return lax.dot_general(a, b, (((1,), (1,)), ((), ())), preferred_element_type=jnp.float32)


def tn(a, b):
    return lax.dot_general(a, b, (((0,), (0,)), ((), ())), preferred_element_type=jnp.float32)


def nn(a, b):
    return jnp.dot(a, b, preferred_element_type=jnp.float32)


def sort_keys(slot_ref, blocks, ok, own_ref, other_ref, cat, put):
    half = blocks * LANES // 2
    cat[:half] = jnp.where(ok, own_ref[...], 0)
    cat[half:] = jnp.where(ok, other_ref[...], 0)
    for j in range(blocks):
        start = pl.multiple_of(slot_ref[j] * LANES, LANES)
        put(j, cat[pl.ds(start, LANES), :])


def two_heads(rows, first):
    zero = jnp.zeros_like(rows)
    return jnp.concatenate([jnp.where(first, rows, zero), jnp.where(first, zero, rows)], axis=0)


def attend_kernel(width, blocks, qblocks, place_ref, slot_ref, q_ref, ko_ref, ks_ref, vo_ref, vs_ref,
                  o_ref, lse_ref, cat, ksort, vturn):
    lane = lax.broadcasted_iota(jnp.int32, (1, LANES), 1)
    ok = lane + pl.program_id(0) * LANES < width
    first = lane < HD

    def put_k(j, rows):
        ksort[j * LANES:(j + 1) * LANES, :] = rows

    def put_v(j, rows):
        vturn[:, j * LANES:(j + 1) * LANES] = rows.astype(jnp.float32).T.astype(jnp.bfloat16)

    sort_keys(slot_ref, blocks, ok, ko_ref, ks_ref, cat, put_k)
    sort_keys(slot_ref, blocks, ok, vo_ref, vs_ref, cat, put_v)

    def one(b, carry):
        place = place_ref[b]
        here = pl.ds(pl.multiple_of(b * LANES, LANES), LANES)
        rows = (jnp.where(ok, q_ref[here, :], 0) * (HD ** -0.5)).astype(jnp.bfloat16)
        q2 = two_heads(rows, first)
        for n in range(1, blocks // 2 + 1):
            @pl.when(place // 2 == n - 1)
            def _(n=n):
                keys = 2 * LANES * n
                s = nt(ksort[:keys, :], q2)
                row = lax.broadcasted_iota(jnp.int32, (2 * LANES, 2 * LANES), 0) + (keys - 2 * LANES)
                col = lax.broadcasted_iota(jnp.int32, (2 * LANES, 2 * LANES), 1) % LANES + place * LANES
                tail = jnp.where(row <= col, s[keys - 2 * LANES:], -1e30)
                s = tail if n == 1 else jnp.concatenate([s[:keys - 2 * LANES], tail], axis=0)
                top = jnp.max(s, axis=0, keepdims=True)
                e = jnp.exp(s - top)
                total = jnp.sum(e, axis=0, keepdims=True)
                turned = nn(vturn[:, :keys], e.astype(jnp.bfloat16)) / total
                joined = jnp.concatenate([turned[:HD, :LANES], turned[HD:, LANES:]], axis=0)
                o_ref[here, :] = joined.T.astype(jnp.bfloat16)
                lse = top + jnp.log(total)
                lse_ref[0, 0:1, here] = lse[:, :LANES]
                lse_ref[0, 1:2, here] = lse[:, LANES:]
        return carry

    lax.fori_loop(0, qblocks, one, 0)


def attend_back_kernel(width, blocks, qblocks, place_ref, slot_ref, q_ref, ko_ref, ks_ref, vo_ref, vs_ref,
                       do_ref, o_ref, lse_ref, dq_ref, dko_ref, dks_ref, dvo_ref, dvs_ref,
                       cat, ksort, kturn, vsort, dk, dv, loose):
    lane = lax.broadcasted_iota(jnp.int32, (1, LANES), 1)
    ok = lane + pl.program_id(0) * LANES < width
    first = lane < HD

    def put_k(j, rows):
        ksort[j * LANES:(j + 1) * LANES, :] = rows
        kturn[:, j * LANES:(j + 1) * LANES] = rows.astype(jnp.float32).T.astype(jnp.bfloat16)

    def put_v(j, rows):
        vsort[j * LANES:(j + 1) * LANES, :] = rows

    sort_keys(slot_ref, blocks, ok, ko_ref, ks_ref, cat, put_k)
    sort_keys(slot_ref, blocks, ok, vo_ref, vs_ref, cat, put_v)
    dk[...] = jnp.zeros_like(dk)
    dv[...] = jnp.zeros_like(dv)

    def one(b, carry):
        place = place_ref[b]
        here = pl.ds(pl.multiple_of(b * LANES, LANES), LANES)
        rows = (jnp.where(ok, q_ref[here, :], 0) * (HD ** -0.5)).astype(jnp.bfloat16)
        q2 = two_heads(rows, first)
        do = jnp.where(ok, do_ref[here, :], 0)
        do2 = two_heads(do, first)
        both = (do.astype(jnp.float32) * jnp.where(ok, o_ref[here, :], 0).astype(jnp.float32)).T
        delta = jnp.concatenate(
            [jnp.sum(both[:HD], axis=0, keepdims=True), jnp.sum(both[HD:], axis=0, keepdims=True)], axis=1
        )
        lse = jnp.concatenate([lse_ref[0, 0:1, here], lse_ref[0, 1:2, here]], axis=1)
        for n in range(1, blocks // 2 + 1):
            @pl.when(place // 2 == n - 1)
            def _(n=n):
                keys = 2 * LANES * n
                s = nt(ksort[:keys, :], q2)
                row = lax.broadcasted_iota(jnp.int32, (2 * LANES, 2 * LANES), 0) + (keys - 2 * LANES)
                col = lax.broadcasted_iota(jnp.int32, (2 * LANES, 2 * LANES), 1) % LANES + place * LANES
                tail = jnp.where(row <= col, s[keys - 2 * LANES:], -1e30)
                s = tail if n == 1 else jnp.concatenate([s[:keys - 2 * LANES], tail], axis=0)
                p = jnp.exp(s - lse)
                dp = nt(vsort[:keys, :], do2)
                ds = (p * (dp - delta)).astype(jnp.bfloat16)
                dv[:keys, :] += nn(p.astype(jnp.bfloat16), do2)
                dk[:keys, :] += nn(ds, q2)
                turned = nn(kturn[:, :keys], ds) * (HD ** -0.5)
                joined = jnp.concatenate([turned[:HD, :LANES], turned[HD:, LANES:]], axis=0)
                dq_ref[here, :] = joined.T.astype(jnp.bfloat16)
        return carry

    lax.fori_loop(0, qblocks, one, 0)
    half = blocks * LANES // 2
    for source, mine, theirs in ((dk, dko_ref, dks_ref), (dv, dvo_ref, dvs_ref)):
        for j in range(blocks):
            start = pl.multiple_of(slot_ref[j] * LANES, LANES)
            loose[pl.ds(start, LANES), :] = source[j * LANES:(j + 1) * LANES, :]
        mine[...] = loose[:half]
        theirs[...] = loose[half:].astype(jnp.bfloat16)


def attention_specs(rows):
    tall = pl.BlockSpec((rows, LANES), lambda i, *_: (0, i))
    stat = pl.BlockSpec((1, 2, rows), lambda i, *_: (i, 0, 0))
    return tall, stat


def attention(place, slot, q, ko, ks, vo, vs):
    rows, width = q.shape
    steps = -(-width // LANES)
    blocks, keys = slot.shape[0], slot.shape[0] * LANES
    tall, stat = attention_specs(rows)
    elems = rows * keys * steps * 2
    return pl.pallas_call(
        functools.partial(attend_kernel, width, blocks, place.shape[0]),
        grid_spec=pltpu.PrefetchScalarGridSpec(
            num_scalar_prefetch=2,
            grid=(steps,),
            in_specs=[tall] * 5,
            out_specs=[tall, stat],
            scratch_shapes=[
                pltpu.VMEM((keys, LANES), jnp.bfloat16),
                pltpu.VMEM((keys, LANES), jnp.bfloat16),
                pltpu.VMEM((LANES, keys), jnp.bfloat16),
            ],
        ),
        out_shape=[
            jax.ShapeDtypeStruct((rows, width), jnp.bfloat16),
            jax.ShapeDtypeStruct((steps, 2, rows), jnp.float32),
        ],
        cost_estimate=pl.CostEstimate(flops=elems * HD * 8, bytes_accessed=rows * width * 12, transcendentals=elems),
        compiler_params=pltpu.CompilerParams(vmem_limit_bytes=40 * 2 ** 20),
        name="attention",
    )(place, slot, q, ko, ks, vo, vs)


def attention_back(place, slot, q, ko, ks, vo, vs, do, o, lse):
    rows, width = q.shape
    steps = -(-width // LANES)
    blocks, keys = slot.shape[0], slot.shape[0] * LANES
    tall, stat = attention_specs(rows)
    elems = rows * keys * steps * 2
    wide = jax.ShapeDtypeStruct((rows, width), jnp.float32)
    thin = jax.ShapeDtypeStruct((rows, width), jnp.bfloat16)
    return pl.pallas_call(
        functools.partial(attend_back_kernel, width, blocks, place.shape[0]),
        grid_spec=pltpu.PrefetchScalarGridSpec(
            num_scalar_prefetch=2,
            grid=(steps,),
            in_specs=[tall] * 7 + [stat],
            out_specs=[tall] * 5,
            scratch_shapes=[
                pltpu.VMEM((keys, LANES), jnp.bfloat16),
                pltpu.VMEM((keys, LANES), jnp.bfloat16),
                pltpu.VMEM((LANES, keys), jnp.bfloat16),
                pltpu.VMEM((keys, LANES), jnp.bfloat16),
                pltpu.VMEM((keys, LANES), jnp.float32),
                pltpu.VMEM((keys, LANES), jnp.float32),
                pltpu.VMEM((keys, LANES), jnp.float32),
            ],
        ),
        out_shape=[thin, wide, thin, wide, thin],
        cost_estimate=pl.CostEstimate(flops=elems * HD * 20, bytes_accessed=rows * width * 30, transcendentals=elems),
        compiler_params=pltpu.CompilerParams(vmem_limit_bytes=40 * 2 ** 20),
        name="attention_back",
    )(place, slot, q, ko, ks, vo, vs, do, o, lse)


def gather_kernel(planes, piece_ref, small_ref, token_ref, cot_ref, out_ref, small_out, token_out, cot_out,
                  send_sem, recv_sem, small_send, small_recv, swap_send, swap_recv, own_sem):
    dp, mp = lax.axis_index("dp"), lax.axis_index("mp")
    z, c = dp // 2, dp % 2
    y, x = mp // 2, mp % 2
    side = mp + 1 - 2 * x
    across = mp + 2 - 4 * y
    corner = 3 - mp
    to_x, to_y, to_c = (dp, side), (dp, across), (dp + 1 - 2 * c, mp)
    to_z = [(lax.rem(z + k, planes) * 2 + c, mp) for k in range(1, planes)]
    same, turned = (z * 2 + y, c * 2 + x), (z * 2 + y, c * 2 + 1 - x)
    barrier = pltpu.get_barrier_semaphore()
    for peer in (to_x, to_y, to_c, *to_z, turned):
        pl.semaphore_signal(barrier, inc=1, device_id=peer, device_id_type=pl.DeviceIdType.MESH)

    @pl.when(y != c)
    def _():
        pl.semaphore_signal(barrier, inc=1, device_id=same, device_id_type=pl.DeviceIdType.MESH)

    pl.semaphore_wait(barrier, 4 + len(to_z) + (y - c) * (y - c))

    locals_ = [
        pltpu.make_async_copy(piece_ref, out_ref.at[mp, dp], own_sem.at[0]),
        pltpu.make_async_copy(small_ref, small_out.at[dp], own_sem.at[1]),
    ]
    for copy in locals_:
        copy.start()
    sent = []

    def remote(source, target, sems, peer):
        copy = pltpu.make_async_remote_copy(
            src_ref=source,
            dst_ref=target,
            send_sem=sems[0],
            recv_sem=sems[1],
            device_id=peer,
            device_id_type=pl.DeviceIdType.MESH,
        )
        copy.start()
        return copy

    def send(source, index, row, peer):
        sent.append(remote(source, out_ref.at[index, row], (send_sem.at[len(sent)], recv_sem.at[index, row]), peer))

    def arrived(index, row):
        pltpu.make_async_copy(out_ref.at[index, row], out_ref.at[index, row], recv_sem.at[index, row]).wait()
        return out_ref.at[index, row]

    def swap(source, target, which):
        moved = remote(source.at[1 - x], target.at[1], (swap_send.at[which, 1], swap_recv.at[which, 1]), turned)
        kept = pltpu.make_async_copy(source.at[x], target.at[0], own_sem.at[2 + which])
        pair = (source.at[x], target.at[0], (swap_send.at[which, 0], swap_recv.at[which, 0]), same)

        @pl.when(y == c)
        def _():
            kept.start()

        @pl.when(y != c)
        def _():
            remote(*pair)

        def finish():
            moved.wait()

            @pl.when(y == c)
            def _():
                kept.wait()

            @pl.when(y != c)
            def _():
                pltpu.make_async_remote_copy(
                    src_ref=pair[0],
                    dst_ref=pair[1],
                    send_sem=pair[2][0],
                    recv_sem=pair[2][1],
                    device_id=same,
                    device_id_type=pl.DeviceIdType.MESH,
                ).wait()

        return finish

    rows = [lax.rem(z - k + planes, planes) * 2 + c for k in range(planes)]
    little = []

    def send_small(source, row, peer):
        little.append(
            remote(source, small_out.at[row], (small_send.at[len(little)], small_recv.at[row]), peer)
        )

    def small_arrived(row):
        pltpu.make_async_copy(small_out.at[row], small_out.at[row], small_recv.at[row]).wait()
        return small_out.at[row]

    for peer in (*to_z, to_c):
        send_small(small_ref, dp, peer)
    for peer in to_z:
        send(piece_ref, mp, dp, peer)
    for peer in (to_x, to_y, to_c):
        send(piece_ref, mp, dp, peer)
    finishes = [swap(token_ref, token_out, 0)]
    for k in range(planes):
        if k > 0:
            send_small(small_arrived(rows[k]), rows[k], to_c)
            block = arrived(mp, rows[k])
            for peer in (to_x, to_y, to_c):
                send(block, mp, rows[k], peer)
            send(arrived(corner, rows[k - 1]), corner, rows[k - 1], to_c)
        block = arrived(side, rows[k])
        if k % 2 == 0:
            send(block, side, rows[k], to_y)
        send(block, side, rows[k], to_c)
        block = arrived(across, rows[k])
        if k % 2 == 1:
            send(block, across, rows[k], to_x)
        send(block, across, rows[k], to_c)
    finishes.append(swap(cot_ref, cot_out, 1))
    send(arrived(corner, rows[-1]), corner, rows[-1], to_c)
    for k in range(planes):
        beside = rows[k] + 1 - 2 * c
        small_arrived(beside)
        for index in (mp, side, across, corner):
            arrived(index, beside)
    for copy in sent + little:
        copy.wait_send()
    for finish in finishes:
        finish()
    for copy in locals_:
        copy.wait()


def gather_four(planes, piece, small, tokens, cotangent):
    count = (planes - 1) + 3 * planes + planes + 3 * planes
    anywhere = pl.BlockSpec(memory_space=pl.ANY)
    return pl.pallas_call(
        functools.partial(gather_kernel, planes),
        in_specs=[anywhere] * 4,
        out_specs=[anywhere] * 4,
        out_shape=[
            jax.ShapeDtypeStruct((4, 2 * planes) + piece.shape, piece.dtype),
            jax.ShapeDtypeStruct((2 * planes,) + small.shape, small.dtype),
            jax.ShapeDtypeStruct(tokens.shape, tokens.dtype),
            jax.ShapeDtypeStruct(cotangent.shape, cotangent.dtype),
        ],
        scratch_shapes=[
            pltpu.SemaphoreType.DMA((count,)),
            pltpu.SemaphoreType.DMA((4, 2 * planes)),
            pltpu.SemaphoreType.DMA((2 * planes,)),
            pltpu.SemaphoreType.DMA((2 * planes,)),
            pltpu.SemaphoreType.DMA((2, 2)),
            pltpu.SemaphoreType.DMA((2, 2)),
            pltpu.SemaphoreType.DMA((4,)),
        ],
        cost_estimate=pl.CostEstimate(flops=0, bytes_accessed=300 * 2 ** 20, transcendentals=0),
        compiler_params=pltpu.CompilerParams(collective_id=0, has_side_effects=True),
        name="gather_four",
    )(piece, small, tokens, cotangent)


GROUPS, PARTS = 4, 2


def tiles(width, body):
    whole = width // 256

    def step(j, carry):
        body(pl.multiple_of(j * 256, 256), 256)
        return carry

    lax.fori_loop(0, whole, step, 0)
    if width % 256:
        body(whole * 256, width % 256)


def units_kernel(back, *refs):
    if back:
        (x_ref, wa_ref, wb_ref, slope_ref, out_ref, rows_ref, left_ref, sums_ref, *scratch) = refs
    else:
        (x_ref, wa_ref, wb_ref, bias_ref, out_ref, rows_ref, left_ref, slope_ref, *scratch) = refs
    (wa, wb, rows, own, far, beside, corner, got_c, got_f, give, got_y, left, slope,
     in_sem, send_sem, recv_sem, out_sem) = scratch
    width = wa.shape[1]
    part = rows.shape[2]
    dp, mp = lax.axis_index("dp"), lax.axis_index("mp")
    to_c = (dp + 1 - 2 * (dp % 2), mp)
    to_y = (dp, mp + 2 - 4 * (mp // 2))
    loads = [
        pltpu.make_async_copy(x_ref.at[pl.ds(h * part, part)], rows.at[0, h], in_sem.at[h]) for h in range(PARTS)
    ]
    loads += [pltpu.make_async_copy(wa_ref, wa, in_sem.at[2]), pltpu.make_async_copy(wb_ref, wb, in_sem.at[3])]
    for load in loads:
        load.start()
    barrier = pltpu.get_barrier_semaphore()
    for peer in (to_c, to_y):
        pl.semaphore_signal(barrier, inc=1, device_id=peer, device_id_type=pl.DeviceIdType.MESH)
    pl.semaphore_wait(barrier, 2)
    sent = []

    def send(source, target, slot, peer):
        copy = pltpu.make_async_remote_copy(
            src_ref=source,
            dst_ref=target,
            send_sem=send_sem.at[slot],
            recv_sem=recv_sem.at[slot],
            device_id=peer,
            device_id_type=pl.DeviceIdType.MESH,
        )
        copy.start()
        sent.append(copy)
        return copy

    kinds = {name: i for i, name in enumerate(("y", "c", "f", "beside", "corner", "give"))}

    def slot_of(kind, h):
        return kinds[kind] * PARTS + h

    arrivals = {}
    for h in range(PARTS):
        loads[h].wait()
        arrivals["y", h] = send(rows.at[0, h], rows.at[2, h], slot_of("y", h), to_y)
        arrivals["c", h] = send(rows.at[0, h], rows.at[1, h], slot_of("c", h), to_c)
    stores = []
    busy = [[], []]
    order = [(0, 0), (0, 1), (1, 0), (1, 1), (2, 0), (3, 0), (2, 1), (3, 1)]

    def place(index):
        group, h = order[index]
        return pl.ds((group * PARTS + h) * part, part)

    def fetch(index):
        copy = pltpu.make_async_copy(slope_ref.at[place(index)], slope.at[index % 2], in_sem.at[4 + index % 2])
        copy.start()
        return copy

    def store(source, target, index, kind):
        copy = pltpu.make_async_copy(source, target, out_sem.at[kind, index])
        copy.start()
        return copy

    fetched = {}
    if back:
        sums_ref[...] = jnp.zeros_like(sums_ref)
        fetched[0] = fetch(0)
    loads[2].wait()
    loads[3].wait()

    def work(index, target):
        group, h = order[index]
        side = index % 2
        for copy in busy[side]:
            copy.wait()
        busy[side] = []
        source = rows.at[group, h]
        if back:
            fetched[index].wait()
            if index + 1 < len(order):
                fetched[index + 1] = fetch(index + 1)

        def first(at, size):
            span = pl.ds(at, size)
            value = nn(source[...], wa[:, span])
            if back:
                value = bf(value * f32(slope[side, :, span]))
                left[side, :, span] = value
                sums_ref[:, span] += jnp.sum(f32(value), axis=0, keepdims=True)
            else:
                value = value + bias_ref[:, span]
                square = value * value
                bend = jnp.tanh(0.7978845608028654 * value * (1.0 + 0.044715 * square))
                half = 0.5 * (1.0 + bend)
                left[side, :, span] = bf(value * half)
                slope[side, :, span] = bf(
                    half + 0.5 * value * (1.0 - bend * bend) * 0.7978845608028654 * (1.0 + 0.134145 * square)
                )

        tiles(width, first)
        busy[side].append(store(left.at[side], left_ref.at[place(index)], index, 0))
        if not back:
            busy[side].append(store(slope.at[side], slope_ref.at[place(index)], index, 1))
        stores.append(store(source, rows_ref.at[place(index)], index, 2))

        def second(at, size):
            span = pl.ds(at, size)
            target[:, span] = nt(left[side], wb[span, :]).astype(target.dtype)

        tiles(width, second)

    def combine(h):
        arrivals["corner", h].wait_recv()
        give[h] = bf(far[h] + f32(got_f[h]))
        arrivals["give", h] = send(give.at[h], got_y.at[h], slot_of("give", h), to_y)

    work(0, own.at[0])
    work(1, own.at[1])
    for h in range(PARTS):
        arrivals["c", h].wait_recv()
        work(2 + h, beside.at[h])
        arrivals["beside", h] = send(beside.at[h], got_c.at[h], slot_of("beside", h), to_c)
    for h in range(PARTS):
        arrivals["y", h].wait_recv()
        arrivals["f", h] = send(rows.at[2, h], rows.at[3, h], slot_of("f", h), to_c)
        work(4 + 2 * h, far.at[h])
        arrivals["f", h].wait_recv()
        work(5 + 2 * h, corner.at[h])
        arrivals["corner", h] = send(corner.at[h], got_f.at[h], slot_of("corner", h), to_c)
        combine(h)
    for h in range(PARTS):
        arrivals["beside", h].wait_recv()
        arrivals["give", h].wait_recv()
        out_ref[pl.ds(h * part, part), :] = own[h] + f32(got_c[h]) + f32(got_y[h])
    for copy in sent:
        copy.wait_send()
    for copy in stores + busy[0] + busy[1]:
        copy.wait()


def units(back, x, wa, wb, extra):
    rows, width = x.shape
    part = rows // PARTS
    half = jax.ShapeDtypeStruct((GROUPS * rows, width), jnp.bfloat16)
    anywhere = pl.BlockSpec(memory_space=pl.ANY)
    inside = pl.BlockSpec(memory_space=pltpu.VMEM)
    thin, wide = pltpu.VMEM((PARTS, part, width), jnp.bfloat16), pltpu.VMEM((PARTS, part, width), jnp.float32)
    count = 6 * PARTS
    return pl.pallas_call(
        functools.partial(units_kernel, back),
        in_specs=[anywhere, anywhere, anywhere, anywhere if back else inside],
        out_specs=[inside, anywhere, anywhere, inside if back else anywhere],
        out_shape=[
            jax.ShapeDtypeStruct((rows, width), jnp.float32),
            half,
            half,
            jax.ShapeDtypeStruct((1, width), jnp.float32) if back else half,
        ],
        scratch_shapes=[
            pltpu.VMEM(wa.shape, jnp.bfloat16),
            pltpu.VMEM(wb.shape, jnp.bfloat16),
            pltpu.VMEM((GROUPS, PARTS, part, width), jnp.bfloat16),
            wide, wide, thin, thin, thin, thin, thin, thin, thin, thin,
            pltpu.SemaphoreType.DMA((6,)),
            pltpu.SemaphoreType.DMA((count,)),
            pltpu.SemaphoreType.DMA((count,)),
            pltpu.SemaphoreType.DMA((3, GROUPS * PARTS)),
        ],
        cost_estimate=pl.CostEstimate(
            flops=60 * 10 ** 9, bytes_accessed=60 * 2 ** 20, transcendentals=0
        ),
        compiler_params=pltpu.CompilerParams(
            collective_id=2 if back else 1, has_side_effects=True, vmem_limit_bytes=56 * 2 ** 20
        ),
        name="units_back" if back else "units",
    )(x, wa, wb, extra)


def settle_kernel(planes, keep_ref, send_ref, piece_ref, out_ref, pieces, outgo, income, total, from_y, from_x, to_give,
                  final, from_z, load_sem, c_send, c_recv, xy_send, xy_recv, z_send, z_recv):
    dp, mp = lax.axis_index("dp"), lax.axis_index("mp")
    z, c = dp // 2, dp % 2
    y, x = mp // 2, mp % 2
    to_x, to_y = (dp, mp + 1 - 2 * x), (dp, mp + 2 - 4 * y)
    to_c = (dp + 1 - 2 * c, mp)
    others = [lax.rem(z + k, planes) for k in range(1, planes)]
    barrier = pltpu.get_barrier_semaphore()
    for peer in (to_x, to_y, to_c, *[(other * 2 + c, mp) for other in others]):
        pl.semaphore_signal(barrier, inc=1, device_id=peer, device_id_type=pl.DeviceIdType.MESH)
    loads = []
    for k, (far_y, far_x) in enumerate(((1, 1), (1, 0), (0, 1), (0, 0))):
        index = 2 * (1 - y if far_y else y) + (1 - x if far_x else x)
        loads.append(pltpu.make_async_copy(piece_ref.at[index], pieces.at[k], load_sem.at[k]))
        loads[-1].start()
    pl.semaphore_wait(barrier, 3 + len(others))
    width = pieces.shape[2]
    tall = keep_ref.shape[0] // planes
    half = planes // 2

    def remote(source, target, sems, slot, peer):
        copy = pltpu.make_async_remote_copy(
            src_ref=source,
            dst_ref=target,
            send_sem=sems[0].at[slot],
            recv_sem=sems[1].at[slot],
            device_id=peer,
            device_id_type=pl.DeviceIdType.MESH,
        )
        copy.start()
        return copy

    def product(left_ref, k, write):
        def body(at, size):
            span = pl.ds(at, size)
            value = nn(left_ref[...], pieces[k, :, span])
            for block in range(planes):
                write(block, span, value[block * tall:(block + 1) * tall])

        tiles(width, body)

    crossing = []
    for k in range(4):
        loads[k].wait()

        def put(block, span, value, k=k):
            outgo[k, block, :, span] = bf(value)

        product(send_ref, k, put)
        crossing.append(remote(outgo.at[k], income.at[k], (c_send, c_recv), k, to_c))
    first, second = pl.ds(0, half), pl.ds(half, half)
    sent = []

    def chip(k):
        crossing[k].wait_recv()

        def put(block, span, value, k=k):
            total[k, block, :, span] = bf(value + f32(income[k, block, :, span]))

        product(keep_ref, k, put)

    def add(target, base, extras):
        for block in range(half):
            value = f32(base[block])
            for extra in extras:
                value = value + f32(extra[block])
            target[block] = value.astype(target.dtype)

    sems = (xy_send, xy_recv)
    chip(0)
    y0 = remote(total.at[0, first], from_y.at[0], sems, 0, to_y)
    x0 = remote(total.at[0, second], from_x.at[0], sems, 1, to_x)
    chip(1)
    y1 = remote(total.at[1, first], from_y.at[1], sems, 2, to_y)
    chip(2)
    x1 = remote(total.at[2, second], from_x.at[1], sems, 3, to_x)
    chip(3)
    y0.wait_recv()
    add(to_give.at[0], total.at[2, first], [from_y.at[0]])
    x2 = remote(to_give.at[0], from_x.at[2], sems, 4, to_x)
    x0.wait_recv()
    add(to_give.at[1], total.at[1, second], [from_x.at[0]])
    y2 = remote(to_give.at[1], from_y.at[2], sems, 5, to_y)
    y1.wait_recv()
    x2.wait_recv()
    add(final.at[first], total.at[3, first], [from_y.at[1], from_x.at[2]])
    x1.wait_recv()
    y2.wait_recv()
    add(final.at[second], total.at[3, second], [from_x.at[1], from_y.at[2]])
    leaving = []
    for k, other in enumerate(others):
        leaving.append(remote(final.at[other], from_z.at[k], (z_send, z_recv), k, (other * 2 + c, mp)))
    value = f32(final[z])
    for k in range(len(others)):
        leaving[k].wait_recv()
        value = value + f32(from_z[k])
    out_ref[...] = value * (1.0 / (2 * planes))
    for copy in (*crossing, y0, x0, y1, x1, x2, y2, *leaving):
        copy.wait_send()


def settle_columns(planes, keep, send, pieces):
    rows, width = keep.shape[0], pieces.shape[2]
    tall = rows // planes
    half = planes // 2
    low = lambda *shape: pltpu.VMEM((*shape, tall, width), jnp.bfloat16)
    inside = pl.BlockSpec(memory_space=pltpu.VMEM)
    return pl.pallas_call(
        functools.partial(settle_kernel, planes),
        in_specs=[inside, inside, pl.BlockSpec(memory_space=pl.ANY)],
        out_specs=inside,
        out_shape=jax.ShapeDtypeStruct((tall, width), jnp.float32),
        scratch_shapes=[
            pltpu.VMEM(pieces.shape, jnp.bfloat16),
            low(4, planes), low(4, planes), low(4, planes),
            low(3, half), low(3, half), low(2, half), low(planes), low(planes - 1),
            pltpu.SemaphoreType.DMA((4,)),
            pltpu.SemaphoreType.DMA((4,)), pltpu.SemaphoreType.DMA((4,)),
            pltpu.SemaphoreType.DMA((6,)), pltpu.SemaphoreType.DMA((6,)),
            pltpu.SemaphoreType.DMA((planes - 1,)), pltpu.SemaphoreType.DMA((planes - 1,)),
        ],
        cost_estimate=pl.CostEstimate(flops=16 * 10 ** 9, bytes_accessed=60 * 2 ** 20, transcendentals=0),
        compiler_params=pltpu.CompilerParams(
            collective_id=3, has_side_effects=True, vmem_limit_bytes=58 * 2 ** 20
        ),
        name="settle_columns",
    )(keep, send, pieces)


def bf(value):
    return value.astype(jnp.bfloat16)


def f32(value):
    return value.astype(jnp.float32)


def norm_parts(value):
    mean = jnp.mean(value, axis=-1, keepdims=True)
    centred = value - mean
    spread = jnp.mean(centred * centred, axis=-1, keepdims=True)
    return centred, lax.rsqrt(spread + eps)


def norm_back(grad, value, gain):
    centred, rate = norm_parts(value)
    hat = centred * rate
    scaled = grad * gain
    inner = scaled - jnp.mean(scaled, axis=-1, keepdims=True) - hat * jnp.mean(scaled * hat, axis=-1, keepdims=True)
    return inner * rate, jnp.sum(grad * hat, axis=0), jnp.sum(grad, axis=0)


def quick_body(
    planes,
    tokens,
    cotangent,
    block_order,
    qkv_weight,
    proj_weight,
    fc_weight,
    fc2_weight,
    fc_bias,
    norm_gain,
    norm_shift,
    attn_bias,
    out_bias,
):
    seqs, local, width = tokens.shape
    slots = local // LANES
    dp_rank = lax.axis_index("dp")
    mp_rank = lax.axis_index("mp")
    core, row, col = dp_rank % 2, mp_rank // 2, mp_rank % 2
    over_x = pairs_of(planes, lambda z, c, y, x: (z, c, y, 1 - x))
    over_y = pairs_of(planes, lambda z, c, y, x: (z, c, 1 - y, x))
    over_c = pairs_of(planes, lambda z, c, y, x: (z, 1 - c, y, x))
    swap_yc = pairs_of(planes, lambda z, c, y, x: (z, y, c, x))
    swap_xc = pairs_of(planes, lambda z, c, y, x: (z, x, y, c))

    along_z = [
        [flat(z, c, y, x) for z in range(planes)] for c in range(2) for y in range(2) for x in range(2)
    ]

    def go(value, pairs):
        return lax.ppermute(value, AXES, pairs)

    def turn_yc(value):
        return jnp.where(row == core, value, go(value, swap_yc))

    def turn_xc(value):
        return jnp.where(col == core, value, go(value, swap_xc))

    def sum_z(value):
        return lax.psum_scatter(value, AXES, axis_index_groups=along_z, scatter_dimension=0, tiled=True)

    ranks = jnp.stack([2 * core + col, 2 * core + 1 - col])
    others = jnp.stack([2 * (1 - core) + col, 2 * (1 - core) + 1 - col])

    def places(which):
        return block_order.reshape(-1, slots)[which].reshape(-1)

    place = places(ranks)
    keyed = jnp.concatenate([place, places(others)])
    blocks = keyed.shape[0]
    order = jnp.arange(blocks, dtype=jnp.int32)
    slot = jnp.sum(jnp.where(keyed[None, :] == order[:, None], order[None, :], 0), axis=1).astype(jnp.int32)

    def add_pair(a, b):
        return bf(f32(a) + f32(b))

    def core_columns(value, which):
        parts = value.reshape(value.shape[0], planes, 2, -1)
        return lax.dynamic_index_in_dim(parts, which, 2, keepdims=False).reshape(value.shape[0], -1)

    def chip_sums(left, right):
        keep, send = core_columns(left, core), core_columns(left, 1 - core)
        size = right.shape[1] // 4

        def one(near_y, near_x):
            index = 2 * (row if near_y else 1 - row) + (col if near_x else 1 - col)
            piece = lax.dynamic_slice_in_dim(right, index * size, size, axis=1)
            return add_pair(tn(keep, piece), go(bf(tn(send, piece)), over_c))

        return one(False, False), one(False, True), one(True, False), one(True, True)

    def gather_dp(piece):
        return lax.all_gather(piece, "dp", axis=0, tiled=True)

    def after(values, *done):
        return lax.optimization_barrier((values, done))[0]

    def fence(*values):
        return lax.optimization_barrier(values)

    def stacked(layer):
        qkv = qkv_weight[layer]
        return jnp.stack([qkv[:, :width], qkv[:, width:2 * width], qkv[:, 2 * width:], proj_weight[layer]])

    small = f32(jnp.concatenate([norm_gain, norm_shift, attn_bias, out_bias, fc_bias[:, None, :]], axis=1))
    count = small.shape[0] * small.shape[1]
    small = jnp.pad(small.reshape(count, -1), ((0, -count % 8), (0, 0)))
    piece = lax.dynamic_index_in_dim(stacked(0), mp_rank, 0, keepdims=False)
    full, small, token_rows, cot_rows = gather_four(planes, piece, small, tokens, cotangent)
    first_four = full.reshape(4, width, width)
    small = jnp.transpose(small[:, :count].reshape(-1, LAYERS, 9, width // (2 * planes)), (1, 2, 0, 3))
    small = small.reshape(LAYERS, 9, width)
    units_bias = turn_xc(small[:, 8])

    fc_slice = [None] * LAYERS
    fc2_slice = [None] * LAYERS
    fc_slice[0] = gather_dp(fc_weight[0])
    fc2_slice[0] = gather_dp(fc2_weight[0].T)
    qkv1 = qkv_weight[1]
    pair_one = gather_dp(after(jnp.where(row == 0, qkv1[:, :width], qkv1[:, width:2 * width]), small))
    pair_two = gather_dp(after(jnp.where(col == 0, qkv1[:, 2 * width:], proj_weight[1]), small))

    def pair_send(whole, over):
        tall = whole.shape[0] // 2
        return go(lax.dynamic_slice_in_dim(whole, core * tall, tall, axis=0), over)

    def pair_join(whole, got, beside, bit):
        other = jnp.concatenate([jnp.where(core == 0, got, beside), jnp.where(core == 0, beside, got)], axis=0)
        return jnp.where(bit == 0, whole, other), jnp.where(bit == 0, other, whole)

    def turned_weight(slice_, moved):
        return jnp.where(col == core, slice_, moved)

    def normal(value, layer, which):
        centred, rate = norm_parts(value)
        return bf(centred * rate * small[layer, which] + small[layer, 2 + which])

    def attend(layer, hidden, w):
        normed = normal(hidden, layer, 0)
        key = bf(nn(normed, w["k"]))
        key_other = go(key, over_c)
        value = bf(nn(normed, w["v"]) + small[layer, 5])
        value_other = go(value, over_c)
        query = bf(nn(normed, w["q"]) + small[layer, 4])
        return normed, query, key, key_other, value, value_other

    def project(layer, hidden, attended, w):
        middle = hidden + nn(attended, w["proj"]) + small[layer, 6]
        return middle, normal(middle, layer, 1)

    saved = []
    hidden = f32(token_rows.reshape(-1, width))
    w = dict(q=first_four[0], k=first_four[1], v=first_four[2], proj=first_four[3])
    parts = attend(0, hidden, w)
    moved_fc = go(after(fc_slice[0], units_bias), swap_xc)
    *parts, moved_fc, fc2_now, pair_one = fence(*parts, moved_fc, fc2_slice[0], pair_one)
    normed, query, key, key_other, value, value_other = parts
    fc_slice[1] = gather_dp(after(fc_weight[1], normed))
    moved_fc2 = go(fc2_now, swap_xc)
    got_one = pair_send(pair_one, over_y)
    attended, lse = attention(place, slot, query, key, key_other, value, value_other)
    attended, lse, moved_fc2, got_one = fence(attended, lse, moved_fc2, got_one)
    fc2_slice[1] = gather_dp(after(fc2_weight[1].T, attended))
    middle, normed_two = project(0, hidden, attended, w)
    w["fc"] = turned_weight(fc_slice[0], moved_fc)
    w["fc2"] = turned_weight(fc2_now, moved_fc2)
    beside_one = go(got_one, over_c)
    middle, normed_two, w["fc"], w["fc2"], beside_one, pair_two = fence(
        middle, normed_two, w["fc"], w["fc2"], beside_one, pair_two
    )
    got_two = pair_send(pair_two, over_x)
    ff_out, rows_in, active, slope = units(False, normed_two, w["fc"], w["fc2"], units_bias[0:1])
    ff_out, rows_in, active, slope, got_two, fc_now = fence(ff_out, rows_in, active, slope, got_two, fc_slice[1])
    saved.append((hidden, *parts, attended, lse, middle, rows_in, active, slope, w))
    moved_fc = go(fc_now, swap_xc)
    beside_two = go(got_two, over_c)
    w = dict()
    w["q"], w["k"] = pair_join(pair_one, got_one, beside_one, row)
    w["v"], w["proj"] = pair_join(pair_two, got_two, beside_two, col)
    hidden = middle + ff_out + small[0, 7]
    *parts, moved_fc, fc2_now = fence(*attend(1, hidden, w), moved_fc, fc2_slice[1])
    normed, query, key, key_other, value, value_other = parts
    moved_fc2 = go(fc2_now, swap_xc)
    attended, lse = attention(place, slot, query, key, key_other, value, value_other)
    attended, lse, moved_fc2 = fence(attended, lse, moved_fc2)
    middle, normed_two = project(1, hidden, attended, w)
    w["fc"] = turned_weight(fc_now, moved_fc)
    w["fc2"] = turned_weight(fc2_now, moved_fc2)
    middle, normed_two, w["fc"], w["fc2"] = fence(middle, normed_two, w["fc"], w["fc2"])
    ff_out, rows_in, active, slope = units(False, normed_two, w["fc"], w["fc2"], units_bias[1:2])
    saved.append((hidden, *parts, attended, lse, middle, rows_in, active, slope, w))
    final = bf(middle + ff_out + small[1, 7])

    factor = 1.0 / lax.axis_size("dp")
    results = [None] * LAYERS

    def units_split(value):
        halves = value.reshape(2, -1, width)
        kept = lax.dynamic_index_in_dim(halves, col, 0, keepdims=False)
        return kept, lax.dynamic_index_in_dim(halves, 1 - col, 0, keepdims=False)

    def mlp_back(layer, out_grad, *held):
        (*_, active, slope, w) = saved[layer]
        return units(True, out_grad, w["fc2"], w["fc"], slope)

    def middle_back(layer, grad, da2):
        middle, w = saved[layer][9], saved[layer][-1]
        part, gain, shift = norm_back(da2, middle, small[layer, 1])
        middle_grad = grad + part
        branch = bf(middle_grad)
        return middle_grad, branch, bf(nt(branch, w["proj"])), gain, shift, jnp.sum(f32(branch), axis=0)

    def heads_back(layer, attended_grad):
        hidden, normed, query, key, key_other, value, value_other, attended, lse = saved[layer][:9]
        return attention_back(place, slot, query, key, key_other, value, value_other, attended_grad, attended, lse)

    def input_back(layer, middle_grad, dq, dk, dv):
        hidden, w = saved[layer][0], saved[layer][-1]
        normed_grad = nt(dq, w["q"]) + nt(dk, w["k"]) + nt(dv, w["v"])
        part, gain, shift = norm_back(normed_grad, hidden, small[layer, 0])
        return middle_grad + part, gain, shift

    def mixed_of(dq, dkm, dkt, dvm, dvt):
        dk = bf(dkm + f32(go(dkt, over_c)))
        dv = bf(dvm + f32(go(dvt, over_c)))
        return dq, dk, dv

    def last_sum(parts, away, side):
        return bf(f32(parts[3]) + f32(away) + f32(side))

    turn_far = pairs_of(planes, lambda z, c, y, x: (z, y, c, 1 - x))

    def regroup(value):
        return go(value[:local], swap_yc), go(value[local:], turn_far)

    def settle(value, mine, theirs):
        mine = jnp.where(row == core, value[:local], mine)
        return f32(jnp.stack([jnp.where(col == 0, mine, theirs), jnp.where(col == 0, theirs, mine)]))

    def bias_sums(gains, shifts, dq, dv, branch_sum, out_grad):
        return jnp.stack(
            [*gains, *shifts, jnp.sum(f32(dq), axis=0), jnp.sum(f32(dv), axis=0), branch_sum, jnp.sum(f32(out_grad), axis=0)]
        )

    def row_parts(left):
        columns = jnp.transpose(left).reshape(planes, 2, -1, left.shape[0])
        keep = lax.dynamic_index_in_dim(columns, core, 1, keepdims=False)
        send = lax.dynamic_index_in_dim(columns, 1 - core, 1, keepdims=False)
        return keep.reshape(-1, left.shape[0]), send.reshape(-1, left.shape[0])

    grad = f32(cot_rows.reshape(-1, width))
    out_grad = cot_rows.reshape(-1, width)
    final, out_grad = fence(final, out_grad)
    da2, rows_grad, inner_grad, units_sum = mlp_back(1, out_grad)
    final, da2, rows_grad, inner_grad, units_sum = fence(final, da2, rows_grad, inner_grad, units_sum)
    fc2_grad = bf(tn(rows_grad, saved[1][11]))
    fc2_grad, rows_in = fence(fc2_grad, saved[1][10])
    fc2_sum = sum_z(fc2_grad)
    fc_grad = bf(tn(rows_in, inner_grad))
    middle_grad, branch, attended_grad, gain_two, shift_two, attn_out_grad = middle_back(1, grad, da2)
    proj_parts = chip_sums(saved[1][7], branch)
    fc_grad, middle_grad, branch, attended_grad, *proj_parts = fence(
        fc_grad, middle_grad, branch, attended_grad, *proj_parts
    )
    fc_sum = sum_z(fc_grad)
    proj_far = go(proj_parts[0], over_y)
    proj_near = go(proj_parts[1], over_y)
    final_moved = regroup(final)
    back = fence(*heads_back(1, attended_grad), fc2_sum, proj_far, proj_near, *final_moved)
    fc2_sum, proj_far, proj_near, *final_moved = back[5:]
    dq, dk, dv = mixed_of(*back[:5])
    dq, dk, dv = fence(dq, dk, dv)
    below, gain_one, shift_one = input_back(1, middle_grad, dq, dk, dv)
    out_grad_low = bf(below)
    sums_one = bias_sums((gain_one, gain_two), (shift_one, shift_two), dq, dv, attn_out_grad, out_grad)
    out_grad_low, below, dq, dk, dv, sums_one = fence(out_grad_low, below, dq, dk, dv, sums_one)
    parts = chip_sums(saved[1][1], jnp.concatenate([dq, dk, dv], axis=1))
    out_grad_low, *parts = fence(out_grad_low, *parts)
    side_far = go(parts[0], over_x)
    side_near = go(parts[2], over_x)
    proj_side = go(add_pair(proj_parts[2], proj_far), over_x)
    fc2_kept, fc2_sent = units_split(fc2_sum)
    fc2_away = go(fc2_sent, over_x)
    da2, rows_grad, inner_grad, units_low = mlp_back(0, out_grad_low)
    da2, rows_grad, inner_grad, units_low, side_far, side_near, fc_sum, proj_side, fc2_away = fence(
        da2, rows_grad, inner_grad, units_low, side_far, side_near, fc_sum, proj_side, fc2_away
    )
    proj_sum = sum_z(last_sum(proj_parts, proj_near, proj_side))
    fc2_high = add_pair(fc2_kept, fc2_away)
    fc_kept, fc_sent = units_split(fc_sum)
    side_far = add_pair(parts[1], side_far)
    fc2_grad = bf(tn(rows_grad, saved[0][11]))
    fc2_grad, rows_in = fence(fc2_grad, saved[0][10])
    fc2_sum = sum_z(fc2_grad)
    fc_grad = bf(tn(rows_in, inner_grad))
    middle_grad, branch, attended_grad, gain_two, shift_two, attn_out_grad = middle_back(0, below, da2)
    low_parts = chip_sums(saved[0][7], branch)
    fc_sent, fc_grad, middle_grad, branch, attended_grad, side_far, *low_parts = fence(
        fc_sent, fc_grad, middle_grad, branch, attended_grad, side_far, *low_parts
    )
    away = go(side_far, over_y)
    fc_away = go(fc_sent, over_x)
    fc_sum = sum_z(fc_grad)
    low_far = go(low_parts[0], over_y)
    low_near = go(low_parts[1], over_y)
    back = fence(*heads_back(0, attended_grad), fc_away, low_far, low_near, away, proj_sum, fc2_sum)
    fc_away, low_far, low_near, away, proj_sum, fc2_sum = back[5:]
    results_one = [add_pair(fc_kept, fc_away), fc2_high, proj_sum]
    dq, dk, dv = mixed_of(*back[:5])
    qkv_joined = bf(f32(parts[3]) + f32(side_near) + f32(away))
    dq, dk, dv, qkv_joined = fence(dq, dk, dv, qkv_joined)
    qkv_sum = sum_z(qkv_joined)
    lowest, gain_one, shift_one = input_back(0, middle_grad, dq, dk, dv)
    sums_zero = bias_sums((gain_one, gain_two), (shift_one, shift_two), dq, dv, attn_out_grad, out_grad_low)
    low = bf(lowest)
    third = 3 * width // 4
    mixed = jnp.concatenate([dq, dk, dv], axis=1)
    pieces = jnp.stack([mixed[:, i * third:(i + 1) * third] for i in range(4)])
    keep, send = row_parts(saved[0][1])
    spread = (jnp.arange(4) == 2 * row + core).astype(jnp.float32)
    sums = jnp.concatenate(
        [
            sums_zero,
            sums_one,
            (spread[None, :, None] * jnp.concatenate([units_low, units_sum], axis=0)[:, None, :]).reshape(2 * 4, width),
        ]
    )
    fc2_kept, fc2_sent = units_split(fc2_sum)
    low, sums, pieces, keep, send, fc2_sent, results_one = fence(low, sums, pieces, keep, send, fc2_sent, results_one)
    results_one[0] = turn_xc(results_one[0])
    results_one[1] = turn_xc(results_one[1])
    low_moved = regroup(low)
    fc2_away = go(fc2_sent, over_x)
    low_side = go(add_pair(low_parts[2], low_far), over_x)
    sums = lax.psum(sums, AXES)
    qkv_low = settle_columns(planes, keep, send, pieces)
    qkv_low, fc2_away, low_side, sums, fc_sum, qkv_sum, results_one, *low_moved = fence(
        qkv_low, fc2_away, low_side, sums, fc_sum, qkv_sum, results_one, *low_moved
    )
    proj_low = sum_z(last_sum(low_parts, low_near, low_side))
    fc_kept, fc_sent = units_split(fc_sum)
    results_zero = [
        turn_xc(add_pair(fc_kept, go(fc_sent, over_x))),
        turn_xc(add_pair(fc2_kept, fc2_away)),
        proj_low,
    ]
    outputs = settle(final, *final_moved)
    input_grad = settle(low, *low_moved)
    held = width // (2 * planes)
    sums = lax.dynamic_slice_in_dim(sums, dp_rank * held, held, axis=1) * factor
    unit_rows = lax.dynamic_index_in_dim(sums[16:].reshape(2, 4, held), mp_rank, 1, keepdims=False)
    sums = sums[:16].reshape(2, 8, held)
    qkv_high = f32(qkv_sum) * factor
    results = [results_zero, results_one]
    return (
        outputs,
        input_grad,
        jnp.stack([qkv_low, qkv_high]),
        jnp.stack([f32(entry[2]) for entry in results]) * factor,
        jnp.stack([f32(entry[0]) for entry in results]) * factor,
        jnp.stack([f32(entry[1]).T for entry in results]) * factor,
        unit_rows,
        sums[:, 0:2],
        sums[:, 2:4],
        sums[:, 4:6],
        sums[:, 6:8],
    )


def solution(mesh):
    planes = mesh.shape["dp"] // 2
    if mesh.shape["mp"] == 4:
        body = functools.partial(quick_body, planes)
    else:
        body = general_body
    return jax.shard_map(
        body,
        mesh=mesh,
        in_specs=(
            P("dp", "mp", None),
            P("dp", "mp", None),
            P(),
            P(None, "dp", None),
            P(None, "dp", None),
            P(None, "dp", "mp"),
            P(None, "mp", "dp"),
            P(None, ("mp", "dp")),
            P(None, None, "dp"),
            P(None, None, "dp"),
            P(None, None, "dp"),
            P(None, None, "dp"),
        ),
        out_specs=(
            P("dp", "mp", None),
            P("dp", "mp", None),
            P(None, "dp", "mp"),
            P(None, "dp", "mp"),
            P(None, "dp", "mp"),
            P(None, "mp", "dp"),
            P(None, ("mp", "dp")),
            P(None, None, "dp"),
            P(None, None, "dp"),
            P(None, None, "dp"),
            P(None, None, "dp"),
        ),
        check_vma=False,
    )
```

```python
import functools

import jax
import jax.numpy as jnp
from jax import lax
from jax.experimental import pallas as pl
from jax.experimental.pallas import tpu as pltpu
from jax.sharding import PartitionSpec as P

HD = 64
LAYERS = 2


eps = 1e-05


def layer_norm(value, gain, shift):
    mean = jnp.mean(value, axis=-1, keepdims=True)
    centred = value - mean
    spread = jnp.mean(centred * centred, axis=-1, keepdims=True)
    return centred * lax.rsqrt(spread + eps) * gain + shift


def fetch_params(weights, layer):
    pieces = tuple((w[layer] for w in weights))
    return (
        lax.all_gather(pieces[0], "dp", axis=0, tiled=True),
        lax.all_gather(pieces[1], "dp", axis=0, tiled=True),
        lax.all_gather(pieces[2], "dp", axis=0, tiled=True),
        lax.all_gather(pieces[3], "dp", axis=1, tiled=True),
        lax.all_gather(pieces[4], "dp", axis=0, tiled=True),
        lax.all_gather(pieces[5], "dp", axis=1, tiled=True),
        lax.all_gather(pieces[6], "dp", axis=1, tiled=True),
        lax.all_gather(pieces[7], "dp", axis=1, tiled=True),
        lax.all_gather(pieces[8], "dp", axis=1, tiled=True),
    )


def fetch_again(weights, layer):
    pieces = tuple((w[layer] for w in weights))
    return (
        lax.all_gather(pieces[0], "dp", axis=0, tiled=True),
        lax.all_gather(pieces[1], "dp", axis=0, tiled=True),
        lax.all_gather(pieces[2], "dp", axis=0, tiled=True),
        lax.all_gather(pieces[3], "dp", axis=1, tiled=True),
        lax.all_gather(pieces[4], "dp", axis=0, tiled=True),
        lax.all_gather(pieces[5], "dp", axis=1, tiled=True),
        lax.all_gather(pieces[6], "dp", axis=1, tiled=True),
        lax.all_gather(pieces[7], "dp", axis=1, tiled=True),
        lax.all_gather(pieces[8], "dp", axis=1, tiled=True),
    )


def scores_of(query_heads, key_heads, visible, scale):
    scores = (
        jnp.einsum("qhd,khd->hqk", query_heads, key_heads, preferred_element_type=jnp.float32)
        * scale
    )
    return jnp.where(visible, scores, -1e30)


def general_body(
    tokens,
    cotangent,
    block_order,
    qkv_weight,
    proj_weight,
    fc_weight,
    fc2_weight,
    fc_bias,
    norm_gain,
    norm_shift,
    attn_bias,
    out_bias,
):
    weights = (
        qkv_weight,
        proj_weight,
        fc_weight,
        fc2_weight,
        fc_bias,
        norm_gain,
        norm_shift,
        attn_bias,
        out_bias,
    )
    seqs, local, width = tokens.shape
    heads = width // HD
    scale = HD ** (-0.5)
    model_size = lax.axis_size("mp")
    data_size = lax.axis_size("dp")
    length = local * model_size
    half = local // 2
    rank = lax.axis_index("mp")
    owned = lax.dynamic_slice_in_dim(block_order, 2 * rank, 2)
    offsets = jnp.arange(local, dtype=jnp.int32)
    query_place = jnp.where(offsets < half, owned[0], owned[1]) * half + offsets % half
    every = jnp.arange(length, dtype=jnp.int32)
    key_place = jnp.repeat(block_order, half) * half + every % half
    visible = key_place[None, :] <= query_place[:, None]
    count = seqs * local

    def attend_one(pack):
        query_heads, key_heads, value_heads = pack
        scores = scores_of(query_heads, key_heads, visible, scale)
        top = jnp.max(scores, axis=-1, keepdims=True)
        expo = jnp.exp(scores - top)
        total = jnp.sum(expo, axis=-1, keepdims=True)
        probs = (expo / total).astype(jnp.bfloat16)
        logsum = top + jnp.log(total)
        attended = jnp.einsum(
            "hqk,khd->qhd", probs, value_heads, preferred_element_type=jnp.float32
        )
        return (attended.reshape(local, width).astype(jnp.bfloat16), logsum)

    def attend_back(pack):
        query_heads, key_heads, value_heads, grad_heads, logsum = pack
        scores = scores_of(query_heads, key_heads, visible, scale)
        probs = jnp.exp(scores - logsum)
        prob_grad = jnp.einsum(
            "qhd,khd->hqk", grad_heads, value_heads, preferred_element_type=jnp.float32
        )
        value_grad = jnp.einsum(
            "hqk,qhd->khd",
            probs.astype(jnp.bfloat16),
            grad_heads,
            preferred_element_type=jnp.float32,
        )
        score_grad = (
            probs * (prob_grad - jnp.sum(probs * prob_grad, axis=-1, keepdims=True))
        ).astype(jnp.bfloat16)
        query_grad = (
            jnp.einsum("hqk,khd->qhd", score_grad, key_heads, preferred_element_type=jnp.float32)
            * scale
        )
        key_grad = (
            jnp.einsum("hqk,qhd->khd", score_grad, query_heads, preferred_element_type=jnp.float32)
            * scale
        )
        return (
            query_grad.reshape(local, width),
            key_grad.reshape(length, width),
            value_grad.reshape(length, width),
        )

    hidden = tokens.reshape(count, width).astype(jnp.float32)
    saved = []
    for layer in range(LAYERS):
        params = fetch_params(weights, layer)
        qkv_full, proj_full, fc_full, fc2_full, fc_b = (
            params[0],
            params[1],
            params[2],
            params[3],
            params[4],
        )
        gains = params[5].astype(jnp.float32)
        shifts = params[6].astype(jnp.float32)
        bias_in = params[7].astype(jnp.float32)
        bias_out = params[8].astype(jnp.float32)
        normed = layer_norm(hidden, gains[0], shifts[0]).astype(jnp.bfloat16)
        mixed = jnp.dot(normed, qkv_full, preferred_element_type=jnp.float32)
        query = (mixed[:, :width] + bias_in[0]).astype(jnp.bfloat16)
        key = mixed[:, width : 2 * width].astype(jnp.bfloat16)
        value = (mixed[:, 2 * width :] + bias_in[1]).astype(jnp.bfloat16)
        keys, values = (
            lax.all_gather(key.reshape(seqs, local, width), "mp", axis=1, tiled=True),
            lax.all_gather(value.reshape(seqs, local, width), "mp", axis=1, tiled=True),
        )
        query_heads = query.reshape(seqs, local, heads, HD)
        key_heads = keys.reshape(seqs, length, heads, HD)
        value_heads = values.reshape(seqs, length, heads, HD)
        attended, logsum = lax.map(attend_one, (query_heads, key_heads, value_heads))
        attended = attended.reshape(count, width)
        middle = (
            hidden + jnp.dot(attended, proj_full, preferred_element_type=jnp.float32) + bias_out[0]
        )
        normed_two = layer_norm(middle, gains[1], shifts[1]).astype(jnp.bfloat16)
        group_rows = lax.all_gather(normed_two, "mp", axis=0, tiled=True)
        inner = jnp.dot(group_rows, fc_full, preferred_element_type=jnp.float32) + fc_b.astype(
            jnp.float32
        )
        active = jax.nn.gelu(inner, approximate=True).astype(jnp.bfloat16)

        def down_rows(start, rows, active=active, fc2_full=fc2_full):
            return jnp.dot(active, fc2_full, preferred_element_type=jnp.float32)

        reduced = lax.psum_scatter(
            down_rows(jnp.int32(0), lax.axis_size("mp") * count).astype(jnp.bfloat16),
            "mp",
            scatter_dimension=0,
            tiled=True,
        ).astype(jnp.float32)
        output = middle + reduced + bias_out[1]
        kept_params = None
        kept_pairs = None
        saved.append(
            (
                hidden,
                normed,
                query,
                key,
                value,
                logsum,
                attended,
                middle,
                group_rows,
                inner,
                kept_params,
                kept_pairs,
            )
        )
        hidden = output
    outputs = hidden.reshape(seqs, local, width)
    grad = cotangent.reshape(count, width).astype(jnp.float32)
    collected = []
    for layer in reversed(range(LAYERS)):
        (
            hidden_in,
            normed,
            query,
            key,
            value,
            logsum,
            attended,
            middle,
            group_rows,
            inner,
            kept_params,
            kept_pairs,
        ) = saved[layer]
        params = fetch_again(weights, layer)
        keys, values = (
            lax.all_gather(key.reshape(seqs, local, width), "mp", axis=1, tiled=True),
            lax.all_gather(value.reshape(seqs, local, width), "mp", axis=1, tiled=True),
        )
        qkv_full, proj_full, fc_full, fc2_full = (params[0], params[1], params[2], params[3])
        gains = params[5].astype(jnp.float32)
        shifts = params[6].astype(jnp.float32)
        out_grad = grad.astype(jnp.bfloat16)
        mlp_bias_grad = jnp.sum(out_grad.astype(jnp.float32), axis=0)
        group_grad = lax.all_gather(out_grad, "mp", axis=0, tiled=True)
        active = jax.nn.gelu(inner, approximate=True).astype(jnp.bfloat16)
        fc2_grad = jnp.einsum("nf,nd->fd", active, group_grad, preferred_element_type=jnp.float32)
        active_grad = jnp.einsum(
            "nd,fd->nf", group_grad, fc2_full, preferred_element_type=jnp.float32
        )
        _, gelu_back = jax.vjp(lambda v: jax.nn.gelu(v, approximate=True), inner)
        inner_grad = gelu_back(active_grad)[0].astype(jnp.bfloat16)
        fc_bias_grad = jnp.sum(inner_grad.astype(jnp.float32), axis=0)
        fc_grad = jnp.einsum(
            "nd,nf->df", group_rows, inner_grad, preferred_element_type=jnp.float32
        )

        def back_rows(start, rows, inner_grad=inner_grad, fc_full=fc_full):
            return jnp.einsum("nf,df->nd", inner_grad, fc_full, preferred_element_type=jnp.float32)

        normed_two_grad = lax.psum_scatter(
            back_rows(jnp.int32(0), lax.axis_size("mp") * count).astype(jnp.bfloat16),
            "mp",
            scatter_dimension=0,
            tiled=True,
        ).astype(jnp.float32)
        _, norm_two_back = jax.vjp(layer_norm, middle, gains[1], shifts[1])
        middle_part, gain_two, shift_two = norm_two_back(normed_two_grad)
        middle_grad = grad + middle_part
        branch_grad = middle_grad.astype(jnp.bfloat16)
        attn_out_bias_grad = jnp.sum(branch_grad.astype(jnp.float32), axis=0)
        proj_grad = jnp.einsum(
            "nd,ne->de", attended, branch_grad, preferred_element_type=jnp.float32
        )
        attended_grad = jnp.einsum(
            "ne,de->nd", branch_grad, proj_full, preferred_element_type=jnp.float32
        ).astype(jnp.bfloat16)
        grad_heads = attended_grad.reshape(seqs, local, heads, HD)
        query_heads = query.reshape(seqs, local, heads, HD)
        key_heads = keys.reshape(seqs, length, heads, HD)
        value_heads = values.reshape(seqs, length, heads, HD)
        query_grad, key_grad, value_grad = lax.map(
            attend_back, (query_heads, key_heads, value_heads, grad_heads, logsum)
        )
        key_part, value_part = (
            lax.psum_scatter(
                key_grad.astype(jnp.bfloat16), "mp", scatter_dimension=1, tiled=True
            ).astype(jnp.float32),
            lax.psum_scatter(
                value_grad.astype(jnp.bfloat16), "mp", scatter_dimension=1, tiled=True
            ).astype(jnp.float32),
        )
        query_round = query_grad.reshape(count, width).astype(jnp.bfloat16)
        key_round = key_part.reshape(count, width).astype(jnp.bfloat16)
        value_round = value_part.reshape(count, width).astype(jnp.bfloat16)
        mixed_grad = jnp.concatenate([query_round, key_round, value_round], axis=1)
        bias_in_grad = jnp.stack(
            [
                jnp.sum(query_round.astype(jnp.float32), axis=0),
                jnp.sum(value_round.astype(jnp.float32), axis=0),
            ]
        )
        qkv_grad = jnp.einsum("nd,ne->de", normed, mixed_grad, preferred_element_type=jnp.float32)
        normed_grad = jnp.einsum(
            "ne,de->nd", mixed_grad, qkv_full, preferred_element_type=jnp.float32
        )
        _, norm_one_back = jax.vjp(layer_norm, hidden_in, gains[0], shifts[0])
        hidden_part, gain_one, shift_one = norm_one_back(normed_grad)
        grad = middle_grad + hidden_part
        gain_grad = jnp.stack([gain_one, gain_two])
        shift_grad = jnp.stack([shift_one, shift_two])
        bias_out_grad = jnp.stack([attn_out_bias_grad, mlp_bias_grad])
        shards = (
            lax.psum_scatter(
                qkv_grad.astype(jnp.bfloat16), "dp", scatter_dimension=0, tiled=True
            ).astype(jnp.float32),
            lax.psum_scatter(
                proj_grad.astype(jnp.bfloat16), "dp", scatter_dimension=0, tiled=True
            ).astype(jnp.float32),
            lax.psum_scatter(
                fc_grad.astype(jnp.bfloat16), "dp", scatter_dimension=0, tiled=True
            ).astype(jnp.float32),
            lax.psum_scatter(
                fc2_grad.astype(jnp.bfloat16), "dp", scatter_dimension=1, tiled=True
            ).astype(jnp.float32),
            lax.psum_scatter(
                fc_bias_grad.astype(jnp.bfloat16), "dp", scatter_dimension=0, tiled=True
            ).astype(jnp.float32),
            lax.psum_scatter(
                gain_grad.astype(jnp.bfloat16), "dp", scatter_dimension=1, tiled=True
            ).astype(jnp.float32),
            lax.psum_scatter(
                shift_grad.astype(jnp.bfloat16), "dp", scatter_dimension=1, tiled=True
            ).astype(jnp.float32),
            lax.psum_scatter(
                bias_in_grad.astype(jnp.bfloat16), "dp", scatter_dimension=1, tiled=True
            ).astype(jnp.float32),
            lax.psum_scatter(
                bias_out_grad.astype(jnp.bfloat16), "dp", scatter_dimension=1, tiled=True
            ).astype(jnp.float32),
        )
        projections = (
            lax.psum_scatter(
                shards[0].astype(jnp.bfloat16), "mp", scatter_dimension=1, tiled=True
            ).astype(jnp.float32),
            lax.psum_scatter(
                shards[1].astype(jnp.bfloat16), "mp", scatter_dimension=1, tiled=True
            ).astype(jnp.float32),
        )
        smaller = lax.psum((shards[5], shards[6], shards[7], shards[8]), "mp")
        factor = 1.0 / data_size
        collected.append(
            (
                projections[0] * factor,
                projections[1] * factor,
                shards[2] * factor,
                shards[3] * factor,
                shards[4] * factor,
                smaller[0] * factor,
                smaller[1] * factor,
                smaller[2] * factor,
                smaller[3] * factor,
            )
        )
    collected = collected[::-1]
    stacked = tuple((jnp.stack([entry[index] for entry in collected]) for index in range(9)))
    input_grad = grad.reshape(seqs, local, width)
    return (
        outputs,
        input_grad,
        stacked[0],
        stacked[1],
        stacked[2],
        stacked[3],
        stacked[4],
        stacked[5],
        stacked[6],
        stacked[7],
        stacked[8],
    )


def grid_index(mesh):
    shape = dict(mesh.shape)
    return shape["dp"] // 2, shape["mp"]


def spots(planes):
    return [(z, c, y, x) for z in range(planes) for c in range(2) for y in range(2) for x in range(2)]


def flat(z, c, y, x):
    return (z * 2 + c) * 4 + y * 2 + x


def pairs_of(planes, move):
    both = [(flat(*spot), flat(*move(*spot))) for spot in spots(planes)]
    return [pair for pair in both if pair[0] != pair[1]]


AXES = ("dp", "mp")
LANES = 128


def nt(a, b):
    return lax.dot_general(a, b, (((1,), (1,)), ((), ())), preferred_element_type=jnp.float32)


def tn(a, b):
    return lax.dot_general(a, b, (((0,), (0,)), ((), ())), preferred_element_type=jnp.float32)


def nn(a, b):
    return jnp.dot(a, b, preferred_element_type=jnp.float32)


def sort_keys(slot_ref, blocks, ok, own_ref, other_ref, cat, put):
    half = blocks * LANES // 2
    cat[:half] = jnp.where(ok, own_ref[...], 0)
    cat[half:] = jnp.where(ok, other_ref[...], 0)
    for j in range(blocks):
        start = pl.multiple_of(slot_ref[j] * LANES, LANES)
        put(j, cat[pl.ds(start, LANES), :])


def two_heads(rows, first):
    zero = jnp.zeros_like(rows)
    return jnp.concatenate([jnp.where(first, rows, zero), jnp.where(first, zero, rows)], axis=0)


def attend_kernel(width, blocks, qblocks, place_ref, slot_ref, q_ref, ko_ref, ks_ref, vo_ref, vs_ref,
                  o_ref, lse_ref, cat, ksort, vturn):
    lane = lax.broadcasted_iota(jnp.int32, (1, LANES), 1)
    ok = lane + pl.program_id(0) * LANES < width
    first = lane < HD

    def put_k(j, rows):
        ksort[j * LANES:(j + 1) * LANES, :] = rows

    def put_v(j, rows):
        vturn[:, j * LANES:(j + 1) * LANES] = rows.astype(jnp.float32).T.astype(jnp.bfloat16)

    sort_keys(slot_ref, blocks, ok, ko_ref, ks_ref, cat, put_k)
    sort_keys(slot_ref, blocks, ok, vo_ref, vs_ref, cat, put_v)

    def one(b, carry):
        place = place_ref[b]
        here = pl.ds(pl.multiple_of(b * LANES, LANES), LANES)
        rows = (jnp.where(ok, q_ref[here, :], 0) * (HD ** -0.5)).astype(jnp.bfloat16)
        q2 = two_heads(rows, first)
        for n in range(1, blocks // 2 + 1):
            @pl.when(place // 2 == n - 1)
            def _(n=n):
                keys = 2 * LANES * n
                s = nt(ksort[:keys, :], q2)
                row = lax.broadcasted_iota(jnp.int32, (2 * LANES, 2 * LANES), 0) + (keys - 2 * LANES)
                col = lax.broadcasted_iota(jnp.int32, (2 * LANES, 2 * LANES), 1) % LANES + place * LANES
                tail = jnp.where(row <= col, s[keys - 2 * LANES:], -1e30)
                s = tail if n == 1 else jnp.concatenate([s[:keys - 2 * LANES], tail], axis=0)
                top = jnp.max(s, axis=0, keepdims=True)
                e = jnp.exp(s - top)
                total = jnp.sum(e, axis=0, keepdims=True)
                turned = nn(vturn[:, :keys], e.astype(jnp.bfloat16)) / total
                joined = jnp.concatenate([turned[:HD, :LANES], turned[HD:, LANES:]], axis=0)
                o_ref[here, :] = joined.T.astype(jnp.bfloat16)
                lse = top + jnp.log(total)
                lse_ref[0, 0:1, here] = lse[:, :LANES]
                lse_ref[0, 1:2, here] = lse[:, LANES:]
        return carry

    lax.fori_loop(0, qblocks, one, 0)


def attend_back_kernel(width, blocks, qblocks, place_ref, slot_ref, q_ref, ko_ref, ks_ref, vo_ref, vs_ref,
                       do_ref, o_ref, lse_ref, dq_ref, dko_ref, dks_ref, dvo_ref, dvs_ref,
                       cat, ksort, kturn, vsort, dk, dv, loose):
    lane = lax.broadcasted_iota(jnp.int32, (1, LANES), 1)
    ok = lane + pl.program_id(0) * LANES < width
    first = lane < HD

    def put_k(j, rows):
        ksort[j * LANES:(j + 1) * LANES, :] = rows
        kturn[:, j * LANES:(j + 1) * LANES] = rows.astype(jnp.float32).T.astype(jnp.bfloat16)

    def put_v(j, rows):
        vsort[j * LANES:(j + 1) * LANES, :] = rows

    sort_keys(slot_ref, blocks, ok, ko_ref, ks_ref, cat, put_k)
    sort_keys(slot_ref, blocks, ok, vo_ref, vs_ref, cat, put_v)
    dk[...] = jnp.zeros_like(dk)
    dv[...] = jnp.zeros_like(dv)

    def one(b, carry):
        place = place_ref[b]
        here = pl.ds(pl.multiple_of(b * LANES, LANES), LANES)
        rows = (jnp.where(ok, q_ref[here, :], 0) * (HD ** -0.5)).astype(jnp.bfloat16)
        q2 = two_heads(rows, first)
        do = jnp.where(ok, do_ref[here, :], 0)
        do2 = two_heads(do, first)
        both = (do.astype(jnp.float32) * jnp.where(ok, o_ref[here, :], 0).astype(jnp.float32)).T
        delta = jnp.concatenate(
            [jnp.sum(both[:HD], axis=0, keepdims=True), jnp.sum(both[HD:], axis=0, keepdims=True)], axis=1
        )
        lse = jnp.concatenate([lse_ref[0, 0:1, here], lse_ref[0, 1:2, here]], axis=1)
        for n in range(1, blocks // 2 + 1):
            @pl.when(place // 2 == n - 1)
            def _(n=n):
                keys = 2 * LANES * n
                s = nt(ksort[:keys, :], q2)
                row = lax.broadcasted_iota(jnp.int32, (2 * LANES, 2 * LANES), 0) + (keys - 2 * LANES)
                col = lax.broadcasted_iota(jnp.int32, (2 * LANES, 2 * LANES), 1) % LANES + place * LANES
                tail = jnp.where(row <= col, s[keys - 2 * LANES:], -1e30)
                s = tail if n == 1 else jnp.concatenate([s[:keys - 2 * LANES], tail], axis=0)
                p = jnp.exp(s - lse)
                dp = nt(vsort[:keys, :], do2)
                ds = (p * (dp - delta)).astype(jnp.bfloat16)
                dv[:keys, :] += nn(p.astype(jnp.bfloat16), do2)
                dk[:keys, :] += nn(ds, q2)
                turned = nn(kturn[:, :keys], ds) * (HD ** -0.5)
                joined = jnp.concatenate([turned[:HD, :LANES], turned[HD:, LANES:]], axis=0)
                dq_ref[here, :] = joined.T.astype(jnp.bfloat16)
        return carry

    lax.fori_loop(0, qblocks, one, 0)
    half = blocks * LANES // 2
    for source, mine, theirs in ((dk, dko_ref, dks_ref), (dv, dvo_ref, dvs_ref)):
        for j in range(blocks):
            start = pl.multiple_of(slot_ref[j] * LANES, LANES)
            loose[pl.ds(start, LANES), :] = source[j * LANES:(j + 1) * LANES, :]
        mine[...] = loose[:half]
        theirs[...] = loose[half:].astype(jnp.bfloat16)


def attention_specs(rows):
    tall = pl.BlockSpec((rows, LANES), lambda i, *_: (0, i))
    stat = pl.BlockSpec((1, 2, rows), lambda i, *_: (i, 0, 0))
    return tall, stat


def attention(place, slot, q, ko, ks, vo, vs):
    rows, width = q.shape
    steps = -(-width // LANES)
    blocks, keys = slot.shape[0], slot.shape[0] * LANES
    tall, stat = attention_specs(rows)
    elems = rows * keys * steps * 2
    return pl.pallas_call(
        functools.partial(attend_kernel, width, blocks, place.shape[0]),
        grid_spec=pltpu.PrefetchScalarGridSpec(
            num_scalar_prefetch=2,
            grid=(steps,),
            in_specs=[tall] * 5,
            out_specs=[tall, stat],
            scratch_shapes=[
                pltpu.VMEM((keys, LANES), jnp.bfloat16),
                pltpu.VMEM((keys, LANES), jnp.bfloat16),
                pltpu.VMEM((LANES, keys), jnp.bfloat16),
            ],
        ),
        out_shape=[
            jax.ShapeDtypeStruct((rows, width), jnp.bfloat16),
            jax.ShapeDtypeStruct((steps, 2, rows), jnp.float32),
        ],
        cost_estimate=pl.CostEstimate(flops=elems * HD * 8, bytes_accessed=rows * width * 12, transcendentals=elems),
        compiler_params=pltpu.CompilerParams(vmem_limit_bytes=40 * 2 ** 20),
        name="attention",
    )(place, slot, q, ko, ks, vo, vs)


def attention_back(place, slot, q, ko, ks, vo, vs, do, o, lse):
    rows, width = q.shape
    steps = -(-width // LANES)
    blocks, keys = slot.shape[0], slot.shape[0] * LANES
    tall, stat = attention_specs(rows)
    elems = rows * keys * steps * 2
    wide = jax.ShapeDtypeStruct((rows, steps * LANES), jnp.float32)
    thin = jax.ShapeDtypeStruct((rows, steps * LANES), jnp.bfloat16)
    narrow = jax.ShapeDtypeStruct((rows, width), jnp.bfloat16)
    return pl.pallas_call(
        functools.partial(attend_back_kernel, width, blocks, place.shape[0]),
        grid_spec=pltpu.PrefetchScalarGridSpec(
            num_scalar_prefetch=2,
            grid=(steps,),
            in_specs=[tall] * 7 + [stat],
            out_specs=[tall] * 5,
            scratch_shapes=[
                pltpu.VMEM((keys, LANES), jnp.bfloat16),
                pltpu.VMEM((keys, LANES), jnp.bfloat16),
                pltpu.VMEM((LANES, keys), jnp.bfloat16),
                pltpu.VMEM((keys, LANES), jnp.bfloat16),
                pltpu.VMEM((keys, LANES), jnp.float32),
                pltpu.VMEM((keys, LANES), jnp.float32),
                pltpu.VMEM((keys, LANES), jnp.float32),
            ],
        ),
        out_shape=[narrow, wide, thin, wide, thin],
        cost_estimate=pl.CostEstimate(flops=elems * HD * 20, bytes_accessed=rows * width * 30, transcendentals=elems),
        compiler_params=pltpu.CompilerParams(vmem_limit_bytes=40 * 2 ** 20),
        name="attention_back",
    )(place, slot, q, ko, ks, vo, vs, do, o, lse)


def gather_kernel(planes, piece_ref, small_ref, token_ref, out_ref, small_out, token_out,
                  send_sem, recv_sem, small_send, small_recv, swap_send, swap_recv, own_sem):
    dp, mp = lax.axis_index("dp"), lax.axis_index("mp")
    z, c = dp // 2, dp % 2
    y, x = mp // 2, mp % 2
    side = mp + 1 - 2 * x
    across = mp + 2 - 4 * y
    corner = 3 - mp
    to_x, to_y, to_c = (dp, side), (dp, across), (dp + 1 - 2 * c, mp)
    to_z = [(lax.rem(z + k, planes) * 2 + c, mp) for k in range(1, planes)]
    same, turned = (z * 2 + y, c * 2 + x), (z * 2 + y, c * 2 + 1 - x)
    barrier = pltpu.get_barrier_semaphore()
    for peer in (to_x, to_y, to_c, *to_z, turned):
        pl.semaphore_signal(barrier, inc=1, device_id=peer, device_id_type=pl.DeviceIdType.MESH)

    @pl.when(y != c)
    def _():
        pl.semaphore_signal(barrier, inc=1, device_id=same, device_id_type=pl.DeviceIdType.MESH)

    pl.semaphore_wait(barrier, 4 + len(to_z) + (y - c) * (y - c))

    locals_ = [
        pltpu.make_async_copy(piece_ref, out_ref.at[mp, dp], own_sem.at[0]),
        pltpu.make_async_copy(small_ref, small_out.at[dp], own_sem.at[1]),
    ]
    for copy in locals_:
        copy.start()
    sent = []

    def remote(source, target, sems, peer):
        copy = pltpu.make_async_remote_copy(
            src_ref=source,
            dst_ref=target,
            send_sem=sems[0],
            recv_sem=sems[1],
            device_id=peer,
            device_id_type=pl.DeviceIdType.MESH,
        )
        copy.start()
        return copy

    def send(source, index, row, peer):
        sent.append(remote(source, out_ref.at[index, row], (send_sem.at[len(sent)], recv_sem.at[index, row]), peer))

    def arrived(index, row):
        pltpu.make_async_copy(out_ref.at[index, row], out_ref.at[index, row], recv_sem.at[index, row]).wait()
        return out_ref.at[index, row]

    def swap(source, target, which):
        moved = remote(source.at[1 - x], target.at[1], (swap_send.at[which, 1], swap_recv.at[which, 1]), turned)
        kept = pltpu.make_async_copy(source.at[x], target.at[0], own_sem.at[2 + which])
        pair = (source.at[x], target.at[0], (swap_send.at[which, 0], swap_recv.at[which, 0]), same)

        @pl.when(y == c)
        def _():
            kept.start()

        @pl.when(y != c)
        def _():
            remote(*pair)

        def finish():
            moved.wait()

            @pl.when(y == c)
            def _():
                kept.wait()

            @pl.when(y != c)
            def _():
                pltpu.make_async_remote_copy(
                    src_ref=pair[0],
                    dst_ref=pair[1],
                    send_sem=pair[2][0],
                    recv_sem=pair[2][1],
                    device_id=same,
                    device_id_type=pl.DeviceIdType.MESH,
                ).wait()

        return finish

    rows = [lax.rem(z - k + planes, planes) * 2 + c for k in range(planes)]
    little = []

    def send_small(source, row, peer):
        little.append(
            remote(source, small_out.at[row], (small_send.at[len(little)], small_recv.at[row]), peer)
        )

    def small_arrived(row):
        pltpu.make_async_copy(small_out.at[row], small_out.at[row], small_recv.at[row]).wait()
        return small_out.at[row]

    for peer in (*to_z, to_c):
        send_small(small_ref, dp, peer)
    for peer in to_z:
        send(piece_ref, mp, dp, peer)
    for peer in (to_x, to_y, to_c):
        send(piece_ref, mp, dp, peer)
    finishes = [swap(token_ref, token_out, 0)]
    for k in range(planes):
        if k > 0:
            send_small(small_arrived(rows[k]), rows[k], to_c)
            block = arrived(mp, rows[k])
            for peer in (to_x, to_y, to_c):
                send(block, mp, rows[k], peer)
            send(arrived(corner, rows[k - 1]), corner, rows[k - 1], to_c)
        block = arrived(side, rows[k])
        if k % 2 == 0:
            send(block, side, rows[k], to_y)
        send(block, side, rows[k], to_c)
        block = arrived(across, rows[k])
        if k % 2 == 1:
            send(block, across, rows[k], to_x)
        send(block, across, rows[k], to_c)
    send(arrived(corner, rows[-1]), corner, rows[-1], to_c)
    for k in range(planes):
        beside = rows[k] + 1 - 2 * c
        small_arrived(beside)
        for index in (mp, side, across, corner):
            arrived(index, beside)
    for copy in sent + little:
        copy.wait_send()
    for finish in finishes:
        finish()
    for copy in locals_:
        copy.wait()


def gather_four(planes, piece, small, tokens):
    count = (planes - 1) + 3 * planes + planes + 3 * planes
    anywhere = pl.BlockSpec(memory_space=pl.ANY)
    return pl.pallas_call(
        functools.partial(gather_kernel, planes),
        in_specs=[anywhere] * 3,
        out_specs=[anywhere] * 3,
        out_shape=[
            jax.ShapeDtypeStruct((4, 2 * planes) + piece.shape, piece.dtype),
            jax.ShapeDtypeStruct((2 * planes,) + small.shape, small.dtype),
            jax.ShapeDtypeStruct(tokens.shape, tokens.dtype),
        ],
        scratch_shapes=[
            pltpu.SemaphoreType.DMA((count,)),
            pltpu.SemaphoreType.DMA((4, 2 * planes)),
            pltpu.SemaphoreType.DMA((2 * planes,)),
            pltpu.SemaphoreType.DMA((2 * planes,)),
            pltpu.SemaphoreType.DMA((2, 2)),
            pltpu.SemaphoreType.DMA((2, 2)),
            pltpu.SemaphoreType.DMA((4,)),
        ],
        cost_estimate=pl.CostEstimate(flops=0, bytes_accessed=300 * 2 ** 20, transcendentals=0),
        compiler_params=pltpu.CompilerParams(collective_id=0, has_side_effects=True),
        name="gather_four",
    )(piece, small, tokens)


GROUPS, PARTS = 4, 2


def tiles(width, body):
    whole = width // 256

    def step(j, carry):
        body(pl.multiple_of(j * 256, 256), 256)
        return carry

    lax.fori_loop(0, whole, step, 0)
    if width % 256:
        body(whole * 256, width % 256)


def units_kernel(back, counts, *refs):
    x_ref, wa_own, wb_own, *refs = refs
    (*wa_moved,), refs = refs[:counts[0]], refs[counts[0]:]
    (*wb_moved,), refs = refs[:counts[1]], refs[counts[1]:]
    if back:
        (slope_ref, act_ref, out_ref, rows_ref, left_ref, sums_ref, grad_ref, act, grad, *scratch) = refs
    else:
        (bias_ref, out_ref, rows_ref, left_ref, slope_ref, *scratch) = refs
    (wa, wb, rows, own, far, beside, corner, got_c, got_f, give, got_y, left, slope,
     in_sem, send_sem, recv_sem, out_sem) = scratch
    width = wa.shape[1]
    part = rows.shape[2]
    dp, mp = lax.axis_index("dp"), lax.axis_index("mp")
    to_c = (dp + 1 - 2 * (dp % 2), mp)
    to_y = (dp, mp + 2 - 4 * (mp // 2))
    loads = [
        pltpu.make_async_copy(x_ref.at[pl.ds(h * part, part)], rows.at[0, h], in_sem.at[h]) for h in range(PARTS)
    ]
    moved = []
    for slot, (own_ref, moved_refs, target) in enumerate(((wa_own, wa_moved, wa), (wb_own, wb_moved, wb))):
        tall = wa.shape[0] // len(moved_refs)
        for side, part_ref in enumerate(moved_refs):
            span = pl.ds(side * tall, tall)
            sem = in_sem.at[6 + 2 * slot + side]
            loads.append(pltpu.make_async_copy(own_ref.at[span], target.at[span], sem))
            moved.append(pltpu.make_async_copy(part_ref, target.at[span], sem))
    for load in loads[:PARTS]:
        load.start()

    @pl.when(mp % 2 == dp % 2)
    def _():
        for load in loads[PARTS:]:
            load.start()

    @pl.when(mp % 2 != dp % 2)
    def _():
        for load in moved:
            load.start()

    barrier = pltpu.get_barrier_semaphore()
    for peer in (to_c, to_y):
        pl.semaphore_signal(barrier, inc=1, device_id=peer, device_id_type=pl.DeviceIdType.MESH)
    pl.semaphore_wait(barrier, 2)
    sent = []

    def send(source, target, slot, peer):
        copy = pltpu.make_async_remote_copy(
            src_ref=source,
            dst_ref=target,
            send_sem=send_sem.at[slot],
            recv_sem=recv_sem.at[slot],
            device_id=peer,
            device_id_type=pl.DeviceIdType.MESH,
        )
        copy.start()
        sent.append(copy)
        return copy

    kinds = {name: i for i, name in enumerate(("y", "c", "f", "beside", "corner", "give"))}

    def slot_of(kind, h):
        return kinds[kind] * PARTS + h

    arrivals = {}
    for h in range(PARTS):
        loads[h].wait()
        arrivals["y", h] = send(rows.at[0, h], rows.at[2, h], slot_of("y", h), to_y)
        arrivals["c", h] = send(rows.at[0, h], rows.at[1, h], slot_of("c", h), to_c)
    stores = []
    busy = [[], []]
    order = [(0, 0), (0, 1), (1, 0), (1, 1), (2, 0), (3, 0), (2, 1), (3, 1)]

    def place(index):
        group, h = order[index]
        return pl.ds((group * PARTS + h) * part, part)

    def fetch(index):
        copy = pltpu.make_async_copy(slope_ref.at[place(index)], slope.at[index % 2], in_sem.at[4 + index % 2])
        copy.start()
        return copy

    def store(source, target, index, kind):
        copy = pltpu.make_async_copy(source, target, out_sem.at[kind, index])
        copy.start()
        return copy

    fetched = {}
    if back:
        sums_ref[...] = jnp.zeros_like(sums_ref)
        fetched[0] = fetch(0)
        act_load = pltpu.make_async_copy(act_ref, act, in_sem.at[10])
        act_load.start()
    for load in loads[PARTS:]:
        load.wait()

    def work(index, target):
        group, h = order[index]
        side = index % 2
        for copy in busy[side]:
            copy.wait()
        busy[side] = []
        source = rows.at[group, h]
        if back:
            fetched[index].wait()
            if index + 1 < len(order):
                fetched[index + 1] = fetch(index + 1)

        def first(at, size):
            span = pl.ds(at, size)
            value = nn(source[...], wa[:, span])
            if back:
                value = bf(value * f32(slope[side, :, span]))
                left[side, :, span] = value
                sums_ref[:, span] += jnp.sum(f32(value), axis=0, keepdims=True)
            else:
                value = value + bias_ref[:, span]
                square = value * value
                bend = jnp.tanh(0.7978845608028654 * value * (1.0 + 0.044715 * square))
                half = 0.5 * (1.0 + bend)
                left[side, :, span] = bf(value * half)
                slope[side, :, span] = bf(
                    half + 0.5 * value * (1.0 - bend * bend) * 0.7978845608028654 * (1.0 + 0.134145 * square)
                )

        tiles(width, first)
        busy[side].append(store(left.at[side], left_ref.at[place(index)], index, 0))
        if not back:
            busy[side].append(store(slope.at[side], slope_ref.at[place(index)], index, 1))
        stores.append(store(source, rows_ref.at[place(index)], index, 2))

        def second(at, size):
            span = pl.ds(at, size)
            target[:, span] = nt(left[side], wb[span, :]).astype(target.dtype)

        tiles(width, second)

    def combine(h):
        arrivals["corner", h].wait_recv()
        give[h] = bf(far[h] + f32(got_f[h]))
        arrivals["give", h] = send(give.at[h], got_y.at[h], slot_of("give", h), to_y)

    work(0, own.at[0])
    work(1, own.at[1])
    for h in range(PARTS):
        arrivals["c", h].wait_recv()
        work(2 + h, beside.at[h])
        arrivals["beside", h] = send(beside.at[h], got_c.at[h], slot_of("beside", h), to_c)
    for h in range(PARTS):
        arrivals["y", h].wait_recv()
        arrivals["f", h] = send(rows.at[2, h], rows.at[3, h], slot_of("f", h), to_c)
        work(4 + 2 * h, far.at[h])
        arrivals["f", h].wait_recv()
        work(5 + 2 * h, corner.at[h])
        arrivals["corner", h] = send(corner.at[h], got_f.at[h], slot_of("corner", h), to_c)
        combine(h)
    if back:
        act_load.wait()
        leaving = {}
        for j in range(-(-width // 256)):
            at, size, side = j * 256, min(256, width - j * 256), j % 2
            if j >= 2:
                leaving[j - 2].wait()

            def column(first, length, at=at, size=size, side=side):
                span = pl.ds(first, length)
                value = None
                for group in range(GROUPS):
                    for h in range(PARTS):
                        here = pl.ds((group * PARTS + h) * part, part)
                        term = tn(rows[group, h, :, at:at + size], act[here, span])
                        value = term if value is None else value + term
                grad[side, :size, span] = bf(value)

            tiles(width, column)
            leaving[j] = pltpu.make_async_copy(
                grad.at[side, pl.ds(0, size)], grad_ref.at[pl.ds(at, size)], in_sem.at[11 + side]
            )
            leaving[j].start()
        for j in list(leaving)[-2:]:
            leaving[j].wait()
    for h in range(PARTS):
        arrivals["beside", h].wait_recv()
        arrivals["give", h].wait_recv()
        out_ref[pl.ds(h * part, part), :] = own[h] + f32(got_c[h]) + f32(got_y[h])
    for copy in sent:
        copy.wait_send()
    for copy in stores + busy[0] + busy[1]:
        copy.wait()


def units(back, x, wa, wb, *extra):
    rows, width = x.shape
    part = rows // PARTS
    half = jax.ShapeDtypeStruct((GROUPS * rows, width), jnp.bfloat16)
    anywhere = pl.BlockSpec(memory_space=pl.ANY)
    inside = pl.BlockSpec(memory_space=pltpu.VMEM)
    thin, wide = pltpu.VMEM((PARTS, part, width), jnp.bfloat16), pltpu.VMEM((PARTS, part, width), jnp.float32)
    count = 6 * PARTS
    moved = (*wa[1:], *wb[1:])
    square = wa[0].shape
    work = []
    if back:
        work = [pltpu.VMEM((GROUPS * rows, width), jnp.bfloat16), pltpu.VMEM((2, 256, width), jnp.bfloat16)]
    return pl.pallas_call(
        functools.partial(units_kernel, back, (len(wa) - 1, len(wb) - 1)),
        in_specs=[anywhere] * (3 + len(moved)) + ([anywhere] * 2 if back else [inside]),
        out_specs=[inside, anywhere, anywhere] + ([inside, anywhere] if back else [anywhere]),
        out_shape=[jax.ShapeDtypeStruct((rows, width), jnp.float32), half, half]
        + ([jax.ShapeDtypeStruct((1, width), jnp.float32), jax.ShapeDtypeStruct(square, jnp.bfloat16)] if back else [half]),
        scratch_shapes=[
            *work,
            pltpu.VMEM(square, jnp.bfloat16),
            pltpu.VMEM(square, jnp.bfloat16),
            pltpu.VMEM((GROUPS, PARTS, part, width), jnp.bfloat16),
            wide, wide, thin, thin, thin, thin, thin, thin, thin, thin,
            pltpu.SemaphoreType.DMA((13,)),
            pltpu.SemaphoreType.DMA((count,)),
            pltpu.SemaphoreType.DMA((count,)),
            pltpu.SemaphoreType.DMA((3, GROUPS * PARTS)),
        ],
        cost_estimate=pl.CostEstimate(
            flops=60 * 10 ** 9, bytes_accessed=60 * 2 ** 20, transcendentals=0
        ),
        compiler_params=pltpu.CompilerParams(
            collective_id=2 if back else 1, has_side_effects=True, vmem_limit_bytes=58 * 2 ** 20
        ),
        name="units_back" if back else "units",
    )(x, wa[0], wb[0], *moved, *extra)


def settle_kernel(planes, keep_ref, send_ref, piece_ref, sum_ref, out_ref, sum_out, pieces, outgo, income, total, from_y, from_x, to_give,
                  final, from_z, sum_at, sum_from, load_sem, c_send, c_recv, xy_send, xy_recv, z_send, z_recv,
                  sum_send, sum_recv):
    dp, mp = lax.axis_index("dp"), lax.axis_index("mp")
    z, c = dp // 2, dp % 2
    y, x = mp // 2, mp % 2
    to_x, to_y = (dp, mp + 1 - 2 * x), (dp, mp + 2 - 4 * y)
    to_c = (dp + 1 - 2 * c, mp)
    others = [lax.rem(z + k, planes) for k in range(1, planes)]
    barrier = pltpu.get_barrier_semaphore()
    for peer in (to_x, to_y, to_c, *[(other * 2 + c, mp) for other in others]):
        pl.semaphore_signal(barrier, inc=1, device_id=peer, device_id_type=pl.DeviceIdType.MESH)
    loads = []
    for k, (far_y, far_x) in enumerate(((1, 1), (1, 0), (0, 1), (0, 0))):
        index = 2 * (1 - y if far_y else y) + (1 - x if far_x else x)
        loads.append(pltpu.make_async_copy(piece_ref.at[index], pieces.at[k], load_sem.at[k]))
        loads[-1].start()
    pl.semaphore_wait(barrier, 3 + len(others))
    width = pieces.shape[2]
    tall = keep_ref.shape[0] // planes
    half = planes // 2

    def remote(source, target, sems, slot, peer):
        copy = pltpu.make_async_remote_copy(
            src_ref=source,
            dst_ref=target,
            send_sem=sems[0].at[slot],
            recv_sem=sems[1].at[slot],
            device_id=peer,
            device_id_type=pl.DeviceIdType.MESH,
        )
        copy.start()
        return copy

    def product(left_ref, k, write):
        def body(at, size):
            span = pl.ds(at, size)
            value = nn(left_ref[...], pieces[k, :, span])
            for block in range(planes):
                write(block, span, value[block * tall:(block + 1) * tall])

        tiles(width, body)

    adding = [remote(sum_ref, sum_from.at[0], (sum_send, sum_recv), 0, to_c)]

    def sum_step(k, source, peer):
        adding[k].wait_recv()
        sum_at[k] = source[...] + sum_from[k]
        if peer is not None:
            adding.append(remote(sum_at.at[k], sum_from.at[k + 1], (sum_send, sum_recv), k + 1, peer))

    crossing = []
    for k in range(4):
        loads[k].wait()

        def put(block, span, value, k=k):
            outgo[k, block, :, span] = bf(value)

        product(send_ref, k, put)
        crossing.append(remote(outgo.at[k], income.at[k], (c_send, c_recv), k, to_c))
    first, second = pl.ds(0, half), pl.ds(half, half)
    sent = []

    def chip(k):
        crossing[k].wait_recv()

        def put(block, span, value, k=k):
            total[k, block, :, span] = bf(value + f32(income[k, block, :, span]))

        product(keep_ref, k, put)

    def add(target, base, extras):
        for block in range(half):
            value = f32(base[block])
            for extra in extras:
                value = value + f32(extra[block])
            target[block] = value.astype(target.dtype)

    sems = (xy_send, xy_recv)
    sum_step(0, sum_ref, to_x)
    chip(0)
    y0 = remote(total.at[0, first], from_y.at[0], sems, 0, to_y)
    x0 = remote(total.at[0, second], from_x.at[0], sems, 1, to_x)
    chip(1)
    y1 = remote(total.at[1, first], from_y.at[1], sems, 2, to_y)
    sum_step(1, sum_at.at[0], to_y)
    chip(2)
    x1 = remote(total.at[2, second], from_x.at[1], sems, 3, to_x)
    chip(3)
    sum_step(2, sum_at.at[1], None)
    for k, other in enumerate(others):
        adding.append(remote(sum_at.at[2], sum_from.at[3 + k], (sum_send, sum_recv), 3 + k, (other * 2 + c, mp)))
    y0.wait_recv()
    add(to_give.at[0], total.at[2, first], [from_y.at[0]])
    x2 = remote(to_give.at[0], from_x.at[2], sems, 4, to_x)
    x0.wait_recv()
    add(to_give.at[1], total.at[1, second], [from_x.at[0]])
    y2 = remote(to_give.at[1], from_y.at[2], sems, 5, to_y)
    y1.wait_recv()
    x2.wait_recv()
    add(final.at[first], total.at[3, first], [from_y.at[1], from_x.at[2]])
    x1.wait_recv()
    y2.wait_recv()
    add(final.at[second], total.at[3, second], [from_x.at[1], from_y.at[2]])
    leaving = []
    for k, other in enumerate(others):
        leaving.append(remote(final.at[other], from_z.at[k], (z_send, z_recv), k, (other * 2 + c, mp)))
    value = f32(final[z])
    for k in range(len(others)):
        leaving[k].wait_recv()
        value = value + f32(from_z[k])
    out_ref[...] = value * (1.0 / (2 * planes))
    value = sum_at[2]
    for k in range(len(others)):
        adding[3 + k].wait_recv()
        value = value + sum_from[3 + k]
    sum_out[...] = value
    for copy in (*crossing, y0, x0, y1, x1, x2, y2, *leaving, *adding):
        copy.wait_send()


def settle_columns(planes, keep, send, pieces, sums):
    rows, width = keep.shape[0], pieces.shape[2]
    tall = rows // planes
    half = planes // 2
    low = lambda *shape: pltpu.VMEM((*shape, tall, width), jnp.bfloat16)
    inside = pl.BlockSpec(memory_space=pltpu.VMEM)
    return pl.pallas_call(
        functools.partial(settle_kernel, planes),
        in_specs=[inside, inside, pl.BlockSpec(memory_space=pl.ANY), inside],
        out_specs=[inside, inside],
        out_shape=[
            jax.ShapeDtypeStruct((tall, width), jnp.float32),
            jax.ShapeDtypeStruct(sums.shape, jnp.float32),
        ],
        scratch_shapes=[
            pltpu.VMEM(pieces.shape, jnp.bfloat16),
            low(4, planes), low(4, planes), low(4, planes),
            low(3, half), low(3, half), low(2, half), low(planes), low(planes - 1),
            pltpu.VMEM((3, *sums.shape), jnp.float32),
            pltpu.VMEM((2 + planes, *sums.shape), jnp.float32),
            pltpu.SemaphoreType.DMA((4,)),
            pltpu.SemaphoreType.DMA((4,)), pltpu.SemaphoreType.DMA((4,)),
            pltpu.SemaphoreType.DMA((6,)), pltpu.SemaphoreType.DMA((6,)),
            pltpu.SemaphoreType.DMA((planes - 1,)), pltpu.SemaphoreType.DMA((planes - 1,)),
            pltpu.SemaphoreType.DMA((2 + planes,)), pltpu.SemaphoreType.DMA((2 + planes,)),
        ],
        cost_estimate=pl.CostEstimate(flops=16 * 10 ** 9, bytes_accessed=60 * 2 ** 20, transcendentals=0),
        compiler_params=pltpu.CompilerParams(
            collective_id=3, has_side_effects=True, vmem_limit_bytes=58 * 2 ** 20
        ),
        name="settle_columns",
    )(keep, send, pieces, sums)


def bf(value):
    return value.astype(jnp.bfloat16)


def f32(value):
    return value.astype(jnp.float32)


def norm_parts(value):
    mean = jnp.mean(value, axis=-1, keepdims=True)
    centred = value - mean
    spread = jnp.mean(centred * centred, axis=-1, keepdims=True)
    return centred, lax.rsqrt(spread + eps)


def norm_back(grad, value, gain):
    centred, rate = norm_parts(value)
    hat = centred * rate
    scaled = grad * gain
    inner = scaled - jnp.mean(scaled, axis=-1, keepdims=True) - hat * jnp.mean(scaled * hat, axis=-1, keepdims=True)
    return inner * rate, jnp.sum(grad * hat, axis=0), jnp.sum(grad, axis=0)


def quick_body(
    planes,
    tokens,
    cotangent,
    block_order,
    qkv_weight,
    proj_weight,
    fc_weight,
    fc2_weight,
    fc_bias,
    norm_gain,
    norm_shift,
    attn_bias,
    out_bias,
):
    seqs, local, width = tokens.shape
    slots = local // LANES
    dp_rank = lax.axis_index("dp")
    mp_rank = lax.axis_index("mp")
    core, row, col = dp_rank % 2, mp_rank // 2, mp_rank % 2
    over_x = pairs_of(planes, lambda z, c, y, x: (z, c, y, 1 - x))
    over_y = pairs_of(planes, lambda z, c, y, x: (z, c, 1 - y, x))
    over_xy = pairs_of(planes, lambda z, c, y, x: (z, c, 1 - y, 1 - x))
    over_c = pairs_of(planes, lambda z, c, y, x: (z, 1 - c, y, x))
    swap_yc = pairs_of(planes, lambda z, c, y, x: (z, y, c, x))
    swap_xc = pairs_of(planes, lambda z, c, y, x: (z, x, y, c))

    along_z = [
        [flat(z, c, y, x) for z in range(planes)] for c in range(2) for y in range(2) for x in range(2)
    ]

    along_dp = [[flat(z, c, y, x) for z in range(planes) for c in range(2)] for y in range(2) for x in range(2)]

    def go(value, pairs):
        return lax.ppermute(value, AXES, pairs)

    def turn_yc(value):
        return jnp.where(row == core, value, go(value, swap_yc))

    def turn_xc(value):
        return jnp.where(col == core, value, go(value, swap_xc))

    def sum_z(value):
        return lax.psum_scatter(value, AXES, axis_index_groups=along_z, scatter_dimension=0, tiled=True)

    ranks = jnp.stack([2 * core + col, 2 * core + 1 - col])
    others = jnp.stack([2 * (1 - core) + col, 2 * (1 - core) + 1 - col])

    def places(which):
        return block_order.reshape(-1, slots)[which].reshape(-1)

    place = places(ranks)
    keyed = jnp.concatenate([place, places(others)])
    blocks = keyed.shape[0]
    order = jnp.arange(blocks, dtype=jnp.int32)
    slot = jnp.sum(jnp.where(keyed[None, :] == order[:, None], order[None, :], 0), axis=1).astype(jnp.int32)

    def add_pair(a, b):
        return bf(f32(a) + f32(b))

    def core_columns(value, which):
        parts = value.reshape(value.shape[0], planes, 2, -1)
        return lax.dynamic_index_in_dim(parts, which, 2, keepdims=False).reshape(value.shape[0], -1)

    def chip_sums(left, right):
        keep, send = core_columns(left, core), core_columns(left, 1 - core)
        size = right.shape[1] // 4

        def one(near_y, near_x):
            index = 2 * (row if near_y else 1 - row) + (col if near_x else 1 - col)
            piece = lax.dynamic_slice_in_dim(right, index * size, size, axis=1)
            return add_pair(tn(keep, piece), go(bf(tn(send, piece)), over_c))

        return one(False, False), one(False, True), one(True, False), one(True, True)

    def gather_dp(piece):
        return lax.all_gather(piece, "dp", axis=0, tiled=True)

    def after(values, *done):
        return lax.optimization_barrier((values, done))[0]

    def fence(*values):
        return lax.optimization_barrier(values)

    def stacked(layer):
        qkv = qkv_weight[layer]
        return jnp.stack([qkv[:, :width], qkv[:, width:2 * width], qkv[:, 2 * width:], proj_weight[layer]])

    small = f32(jnp.concatenate([norm_gain, norm_shift, attn_bias, out_bias, fc_bias[:, None, :]], axis=1))
    count = small.shape[0] * small.shape[1]
    small = jnp.pad(small.reshape(count, -1), ((0, -count % 8), (0, 0)))
    piece = lax.dynamic_index_in_dim(stacked(0), mp_rank, 0, keepdims=False)
    full, small, token_rows = gather_four(planes, piece, small, tokens)
    first_four = full.reshape(4, width, width)
    small = jnp.transpose(small[:, :count].reshape(-1, LAYERS, 9, width // (2 * planes)), (1, 2, 0, 3))
    small = small.reshape(LAYERS, 9, width)
    units_bias = turn_xc(small[:, 8])

    fc_slice = [None] * LAYERS
    fc2_slice = [None] * LAYERS
    fc_slice[0] = gather_dp(fc_weight[0])
    fc2_slice[0] = gather_dp(fc2_weight[0].T)
    qkv1 = qkv_weight[1]
    pair = gather_dp(jnp.where(row == 0, qkv1[:, :width], qkv1[:, width:2 * width]))
    tall = width // 2

    def pair_join(whole, got, bit):
        got = jnp.concatenate(got, axis=0)
        beside = go(got, over_c)
        other = jnp.concatenate([jnp.where(core == 0, got, beside), jnp.where(core == 0, beside, got)], axis=0)
        return jnp.where(bit == 0, whole, other), jnp.where(bit == 0, other, whole)

    def halves(value):
        middle = value.shape[0] // 2
        return value[:middle], value[middle:]

    def padded(value):
        return jnp.pad(value, ((0, 0), (0, -width % LANES)))

    def normal(value, layer, which):
        centred, rate = norm_parts(value)
        return bf(centred * rate * small[layer, which] + small[layer, 2 + which])

    def attend(layer, hidden, w):
        normed = normal(hidden, layer, 0)
        key = padded(bf(nn(normed, w["k"])))
        key_other = go(key, over_c)
        value = padded(bf(nn(normed, w["v"]) + small[layer, 5]))
        value_other = go(value, over_c)
        query = bf(nn(normed, w["q"]) + small[layer, 4])
        return normed, query, key, key_other, value, value_other

    def project(layer, hidden, attended, w):
        middle = hidden + nn(attended, w["proj"]) + small[layer, 6]
        return middle, normal(middle, layer, 1)

    turn_far = pairs_of(planes, lambda z, c, y, x: (z, y, c, 1 - x))

    def cot_regroup():
        mine = lax.dynamic_index_in_dim(cotangent, col, 0, keepdims=False)
        theirs = lax.dynamic_index_in_dim(cotangent, 1 - col, 0, keepdims=False)
        return mine, go(mine, swap_yc), go(theirs, turn_far)

    saved = []
    hidden = f32(token_rows.reshape(-1, width))
    w = dict(q=first_four[0], k=first_four[1], v=first_four[2], proj=first_four[3])
    first_fc = after(fc_slice[0], units_bias)
    fc_moved = go(first_fc, swap_xc)
    fc_slice[1] = gather_dp(after(fc_weight[1], small))
    parts = attend(0, hidden, w)
    *parts, fc_moved, fc2_now, pair = fence(*parts, fc_moved, fc2_slice[0], pair)
    normed, query, key, key_other, value, value_other = parts
    v1 = gather_dp(after(qkv1[:, 2 * width:], normed))
    fc2_parts = halves(fc2_now)
    pair_parts = halves(lax.dynamic_slice_in_dim(pair, core * tall, tall, axis=0))
    fc2_top = go(fc2_parts[0], swap_xc)
    got = [go(pair_parts[0], over_y)]
    attended, lse = attention(place, slot, query, key, key_other, value, value_other)
    attended, lse, fc2_top, got[0] = fence(attended, lse, fc2_top, got[0])
    proj1 = gather_dp(after(proj_weight[1], attended))
    fc2_end = go(fc2_parts[1], swap_xc)
    got.append(go(pair_parts[1], over_y))
    middle, normed_two = project(0, hidden, attended, w)
    middle, normed_two, fc2_end, got[1], fc_now = fence(middle, normed_two, fc2_end, got[1], fc_slice[1])
    w["fc"] = (first_fc, fc_moved)
    w["fc2"] = (fc2_now, fc2_top, fc2_end)
    fc2_slice[1] = gather_dp(after(fc2_weight[1].T, middle))
    fc_moved = go(fc_now, swap_xc)
    ff_out, rows_in, active, slope = units(False, normed_two, w["fc"], w["fc2"], units_bias[0:1])
    ff_out, rows_in, active, slope, fc_moved, v1 = fence(ff_out, rows_in, active, slope, fc_moved, v1)
    saved.append((hidden, *parts, attended, lse, middle, rows_in, active, slope, w))
    w = dict(v=v1, proj=proj1, fc=(fc_now, fc_moved))
    w["q"], w["k"] = pair_join(pair, got, row)
    hidden = middle + ff_out + small[0, 7]
    cot_moved = cot_regroup()
    *parts, cot_moved, fc2_now = fence(*attend(1, hidden, w), cot_moved, fc2_slice[1])
    normed, query, key, key_other, value, value_other = parts
    fc2_parts = halves(fc2_now)
    fc2_top = go(fc2_parts[0], swap_xc)
    attended, lse = attention(place, slot, query, key, key_other, value, value_other)
    attended, lse, fc2_top = fence(attended, lse, fc2_top)
    fc2_end = go(fc2_parts[1], swap_xc)
    middle, normed_two = project(1, hidden, attended, w)
    w["fc2"] = (fc2_now, fc2_top, fc2_end)
    middle, normed_two, fc2_end = fence(middle, normed_two, fc2_end)
    w["fc2"] = (fc2_now, fc2_top, fc2_end)
    ff_out, rows_in, active, slope = units(False, normed_two, w["fc"], w["fc2"], units_bias[1:2])
    saved.append((hidden, *parts, attended, lse, middle, rows_in, active, slope, w))
    final = bf(middle + ff_out + small[1, 7])

    factor = 1.0 / lax.axis_size("dp")
    results = [None] * LAYERS

    def units_split(value):
        quarters = value.reshape(planes, 2, -1, width)
        kept = lax.dynamic_index_in_dim(quarters, col, 1, keepdims=False)
        return kept, lax.dynamic_index_in_dim(quarters, 1 - col, 1, keepdims=False)

    def halves_of(value):
        halves = value.reshape(2, -1, width)
        kept = lax.dynamic_index_in_dim(halves, col, 0, keepdims=False)
        return kept, lax.dynamic_index_in_dim(halves, 1 - col, 0, keepdims=False)

    def sum_dp(value):
        return lax.psum_scatter(value, AXES, axis_index_groups=along_dp, scatter_dimension=0, tiled=True)

    def mp_pieces(*values):
        def piece(y, x):
            parts = []
            for value in values:
                size = value.shape[1] // 4
                parts.append(lax.dynamic_slice_in_dim(value, (2 * y + x) * size, size, axis=1))
            return jnp.concatenate(parts, axis=1)

        return [
            piece(row, col),
            go(piece(row, 1 - col), over_x),
            go(piece(1 - row, col), over_y),
            go(piece(1 - row, 1 - col), over_xy),
        ]

    def total_of(pieces):
        return sum(f32(piece) for piece in pieces[1:]) + f32(pieces[0])

    def mlp_back(layer, out_grad, *held):
        (*_, active, slope, w) = saved[layer]
        return units(True, out_grad, w["fc2"], w["fc"], slope, active)

    def middle_back(layer, grad, da2):
        middle, w = saved[layer][9], saved[layer][-1]
        part, gain, shift = norm_back(da2, middle, small[layer, 1])
        middle_grad = grad + part
        branch = bf(middle_grad)
        return middle_grad, branch, bf(nt(branch, w["proj"])), gain, shift, jnp.sum(f32(branch), axis=0)

    def heads_back(layer, attended_grad):
        hidden, normed, query, key, key_other, value, value_other, attended, lse = saved[layer][:9]
        return attention_back(place, slot, query, key, key_other, value, value_other, attended_grad, attended, lse)

    def input_back(layer, middle_grad, dq, dk, dv):
        hidden, w = saved[layer][0], saved[layer][-1]
        normed_grad = nt(dq, w["q"]) + nt(dk, w["k"]) + nt(dv, w["v"])
        part, gain, shift = norm_back(normed_grad, hidden, small[layer, 0])
        return middle_grad + part, gain, shift

    def mixed_of(dq, dkm, dkt, dvm, dvt):
        dk = bf(dkm + f32(go(dkt, over_c)))[:, :width]
        dv = bf(dvm + f32(go(dvt, over_c)))[:, :width]
        return dq, dk, dv

    def last_sum(parts, away, side):
        return bf(f32(parts[3]) + f32(away) + f32(side))

    def regroup(value):
        value = padded(value)
        return go(value[:local], swap_yc), go(value[local:], turn_far)

    def settle(value, mine, theirs):
        mine, theirs = mine[:, :width], theirs[:, :width]
        mine = jnp.where(row == core, value[:local], mine)
        return f32(jnp.stack([jnp.where(col == 0, mine, theirs), jnp.where(col == 0, theirs, mine)]))

    def bias_sums(gains, shifts, dq, dv, branch_sum, out_grad):
        return jnp.stack(
            [*gains, *shifts, jnp.sum(f32(dq), axis=0), jnp.sum(f32(dv), axis=0), branch_sum, jnp.sum(f32(out_grad), axis=0)]
        )

    def row_parts(left):
        columns = jnp.transpose(left).reshape(planes, 2, -1, left.shape[0])
        keep = lax.dynamic_index_in_dim(columns, core, 1, keepdims=False)
        send = lax.dynamic_index_in_dim(columns, 1 - core, 1, keepdims=False)
        return keep.reshape(-1, left.shape[0]), send.reshape(-1, left.shape[0])

    out_grad = jnp.concatenate([jnp.where(row == core, cot_moved[0], cot_moved[1]), cot_moved[2]], axis=0)
    grad = f32(out_grad)
    final, out_grad = fence(final, out_grad)
    da2, rows_grad, inner_grad, units_sum, fc2_grad = mlp_back(1, out_grad)
    final, da2, inner_grad, units_sum, fc2_grad = fence(final, da2, inner_grad, units_sum, fc2_grad)
    fc2_sum = sum_z(fc2_grad)
    fc_kept, fc_sent = units_split(bf(tn(saved[1][10], inner_grad)))
    fc_kept, fc_top, fc_end, da2 = fence(fc_kept, fc_sent[:planes // 2], fc_sent[planes // 2:], da2)
    fc_away = [go(fc_top, over_x)]
    middle_grad, branch, attended_grad, gain_two, shift_two, attn_out_grad = middle_back(1, grad, da2)
    proj_grad = bf(tn(saved[1][7], branch))
    fc_away[0], fc_end, middle_grad, branch, attended_grad, proj_grad = fence(
        fc_away[0], fc_end, middle_grad, branch, attended_grad, proj_grad
    )
    proj_sum = sum_dp(proj_grad)
    fc_away.append(go(fc_end, over_x))
    final_moved = regroup(final)
    back = fence(*heads_back(1, attended_grad), fc2_sum, fc_away[1], *final_moved)
    fc2_sum, fc_away[1], *final_moved = back[5:]
    dq, dk, dv = mixed_of(*back[:5])
    dq_grad = bf(tn(saved[1][1], back[0]))
    dq, dk, dv, dq_grad = fence(dq, dk, dv, dq_grad)
    dq_sum = sum_dp(dq_grad)
    below, gain_one, shift_one = input_back(1, middle_grad, dq, dk, dv)
    out_grad_low = bf(below)
    sums_one = bias_sums((gain_one, gain_two), (shift_one, shift_two), dq, dv, attn_out_grad, out_grad)
    out_grad_low, below, dq, dk, dv, sums_one = fence(out_grad_low, below, dq, dk, dv, sums_one)
    dkv_grad = bf(tn(saved[1][1], jnp.concatenate([dk, dv], axis=1)))
    fc_joined = add_pair(fc_kept, jnp.concatenate(fc_away, axis=0))
    fc2_kept, fc2_sent = halves_of(fc2_sum)
    out_grad_low, dkv_grad, fc_joined, fc2_sent = fence(out_grad_low, dkv_grad, fc_joined, fc2_sent)
    dkv_sum = sum_dp(dkv_grad)
    fc_sum = sum_z(fc_joined.reshape(-1, width))
    fc2_away = go(fc2_sent, over_x)
    da2, rows_grad, inner_grad, units_low, fc2_grad = mlp_back(0, out_grad_low)
    da2, inner_grad, units_low, fc2_grad, fc2_away, proj_sum, dq_sum = fence(
        da2, inner_grad, units_low, fc2_grad, fc2_away, proj_sum, dq_sum
    )
    fc2_high = add_pair(fc2_kept, fc2_away)
    fc2_kept, fc2_sent = units_split(fc2_grad)
    top = planes // 2
    fc2_kept, fc2_top, fc2_end, da2, fc2_high = fence(fc2_kept, fc2_sent[:top], fc2_sent[top:], da2, fc2_high)
    fc2_away = [go(fc2_top, over_x)]
    fc_kept, fc_sent = units_split(bf(tn(saved[0][10], inner_grad)))
    fc2_away[0], fc2_end, fc_kept, fc_sent, da2 = fence(fc2_away[0], fc2_end, fc_kept, fc_sent, da2)
    fc2_away.append(go(fc2_end, over_x))
    middle_grad, branch, attended_grad, gain_two, shift_two, attn_out_grad = middle_back(0, below, da2)
    proj_grad = bf(tn(saved[0][7], branch))
    fc2_away[1], fc_sent, middle_grad, branch, attended_grad, proj_grad = fence(
        fc2_away[1], fc_sent, middle_grad, branch, attended_grad, proj_grad
    )
    fc_away = go(fc_sent, over_x)
    fc2_low = sum_z(add_pair(fc2_kept, jnp.concatenate(fc2_away, axis=0)).reshape(-1, width))
    back = fence(*heads_back(0, attended_grad), fc_away, dkv_sum)
    fc_away, dkv_sum = back[5:]
    dq, dk, dv = mixed_of(*back[:5])
    dq, dk, dv, proj_grad = fence(dq, dk, dv, proj_grad)
    proj_low = sum_dp(proj_grad)
    fc_low = sum_z(add_pair(fc_kept, fc_away).reshape(-1, width))
    lowest, gain_one, shift_one = input_back(0, middle_grad, dq, dk, dv)
    sums_zero = bias_sums((gain_one, gain_two), (shift_one, shift_two), dq, dv, attn_out_grad, out_grad_low)
    low = bf(lowest)
    third = 3 * width // 4
    mixed = jnp.concatenate([dq, dk, dv], axis=1)
    pieces = jnp.stack([mixed[:, i * third:(i + 1) * third] for i in range(4)])
    keep, send = row_parts(saved[0][1])
    spread = (jnp.arange(4) == 2 * row + core).astype(jnp.float32)
    sums = jnp.concatenate(
        [
            sums_zero,
            sums_one,
            (spread[None, :, None] * jnp.concatenate([units_low, units_sum], axis=0)[:, None, :]).reshape(2 * 4, width),
        ]
    )
    low, sums, pieces, keep, send, dq_sum, dkv_sum, proj_sum, fc_sum, fc2_low = fence(
        low, sums, pieces, keep, send, dq_sum, dkv_sum, proj_sum, fc_sum, fc2_low
    )
    held_rows = proj_sum.shape[0]
    turned = turn_xc(jnp.concatenate([fc_sum, fc2_high, fc2_low], axis=0))
    low_moved = regroup(low)
    columns = mp_pieces(jnp.concatenate([dq_sum, dkv_sum], axis=1), proj_sum)
    qkv_low, sums = settle_columns(planes, keep, send, pieces, sums)
    qkv_low, sums, fc_low, proj_low, turned, columns, low_moved = fence(
        qkv_low, sums, fc_low, proj_low, turned, columns, low_moved
    )
    columns = total_of(columns)
    turned = turned.reshape(3, held_rows, width)
    qkv_high = columns[:, :third]
    results_zero = [turn_xc(fc_low), turned[2], total_of(mp_pieces(proj_low))]
    results_one = [turned[0], turned[1], columns[:, third:]]
    outputs = settle(final, *final_moved)
    input_grad = settle(low, *low_moved)
    held = width // (2 * planes)
    sums = lax.dynamic_slice_in_dim(sums, dp_rank * held, held, axis=1) * factor
    unit_rows = lax.dynamic_index_in_dim(sums[16:].reshape(2, 4, held), mp_rank, 1, keepdims=False)
    sums = sums[:16].reshape(2, 8, held)
    qkv_high = qkv_high * factor
    results = [results_zero, results_one]
    return (
        outputs,
        input_grad,
        jnp.stack([qkv_low, qkv_high]),
        jnp.stack([f32(entry[2]) for entry in results]) * factor,
        jnp.stack([f32(entry[0]) for entry in results]) * factor,
        jnp.stack([f32(entry[1]).T for entry in results]) * factor,
        unit_rows,
        sums[:, 0:2],
        sums[:, 2:4],
        sums[:, 4:6],
        sums[:, 6:8],
    )


def solution(mesh):
    planes = mesh.shape["dp"] // 2
    if mesh.shape["mp"] == 4:
        body = functools.partial(quick_body, planes)
    else:
        body = general_body
    return jax.shard_map(
        body,
        mesh=mesh,
        in_specs=(
            P("dp", "mp", None),
            P("dp", "mp", None),
            P(),
            P(None, "dp", None),
            P(None, "dp", None),
            P(None, "dp", "mp"),
            P(None, "mp", "dp"),
            P(None, ("mp", "dp")),
            P(None, None, "dp"),
            P(None, None, "dp"),
            P(None, None, "dp"),
            P(None, None, "dp"),
        ),
        out_specs=(
            P("dp", "mp", None),
            P("dp", "mp", None),
            P(None, "dp", "mp"),
            P(None, "dp", "mp"),
            P(None, "dp", "mp"),
            P(None, "mp", "dp"),
            P(None, ("mp", "dp")),
            P(None, None, "dp"),
            P(None, None, "dp"),
            P(None, None, "dp"),
            P(None, None, "dp"),
        ),
        check_vma=False,
    )
```

```python
import functools

import jax
import jax.numpy as jnp
from jax import lax
from jax.experimental import pallas as pl
from jax.experimental.pallas import tpu as pltpu
from jax.sharding import PartitionSpec as P

HD = 64
LAYERS = 2


eps = 1e-05


def layer_norm(value, gain, shift):
    mean = jnp.mean(value, axis=-1, keepdims=True)
    centred = value - mean
    spread = jnp.mean(centred * centred, axis=-1, keepdims=True)
    return centred * lax.rsqrt(spread + eps) * gain + shift


def fetch_params(weights, layer):
    pieces = tuple((w[layer] for w in weights))
    return (
        lax.all_gather(pieces[0], "dp", axis=0, tiled=True),
        lax.all_gather(pieces[1], "dp", axis=0, tiled=True),
        lax.all_gather(pieces[2], "dp", axis=0, tiled=True),
        lax.all_gather(pieces[3], "dp", axis=1, tiled=True),
        lax.all_gather(pieces[4], "dp", axis=0, tiled=True),
        lax.all_gather(pieces[5], "dp", axis=1, tiled=True),
        lax.all_gather(pieces[6], "dp", axis=1, tiled=True),
        lax.all_gather(pieces[7], "dp", axis=1, tiled=True),
        lax.all_gather(pieces[8], "dp", axis=1, tiled=True),
    )


def fetch_again(weights, layer):
    pieces = tuple((w[layer] for w in weights))
    return (
        lax.all_gather(pieces[0], "dp", axis=0, tiled=True),
        lax.all_gather(pieces[1], "dp", axis=0, tiled=True),
        lax.all_gather(pieces[2], "dp", axis=0, tiled=True),
        lax.all_gather(pieces[3], "dp", axis=1, tiled=True),
        lax.all_gather(pieces[4], "dp", axis=0, tiled=True),
        lax.all_gather(pieces[5], "dp", axis=1, tiled=True),
        lax.all_gather(pieces[6], "dp", axis=1, tiled=True),
        lax.all_gather(pieces[7], "dp", axis=1, tiled=True),
        lax.all_gather(pieces[8], "dp", axis=1, tiled=True),
    )


def scores_of(query_heads, key_heads, visible, scale):
    scores = (
        jnp.einsum("qhd,khd->hqk", query_heads, key_heads, preferred_element_type=jnp.float32)
        * scale
    )
    return jnp.where(visible, scores, -1e30)


def general_body(
    tokens,
    cotangent,
    block_order,
    qkv_weight,
    proj_weight,
    fc_weight,
    fc2_weight,
    fc_bias,
    norm_gain,
    norm_shift,
    attn_bias,
    out_bias,
):
    weights = (
        qkv_weight,
        proj_weight,
        fc_weight,
        fc2_weight,
        fc_bias,
        norm_gain,
        norm_shift,
        attn_bias,
        out_bias,
    )
    seqs, local, width = tokens.shape
    heads = width // HD
    scale = HD ** (-0.5)
    model_size = lax.axis_size("mp")
    data_size = lax.axis_size("dp")
    length = local * model_size
    half = local // 2
    rank = lax.axis_index("mp")
    owned = lax.dynamic_slice_in_dim(block_order, 2 * rank, 2)
    offsets = jnp.arange(local, dtype=jnp.int32)
    query_place = jnp.where(offsets < half, owned[0], owned[1]) * half + offsets % half
    every = jnp.arange(length, dtype=jnp.int32)
    key_place = jnp.repeat(block_order, half) * half + every % half
    visible = key_place[None, :] <= query_place[:, None]
    count = seqs * local

    def attend_one(pack):
        query_heads, key_heads, value_heads = pack
        scores = scores_of(query_heads, key_heads, visible, scale)
        top = jnp.max(scores, axis=-1, keepdims=True)
        expo = jnp.exp(scores - top)
        total = jnp.sum(expo, axis=-1, keepdims=True)
        probs = (expo / total).astype(jnp.bfloat16)
        logsum = top + jnp.log(total)
        attended = jnp.einsum(
            "hqk,khd->qhd", probs, value_heads, preferred_element_type=jnp.float32
        )
        return (attended.reshape(local, width).astype(jnp.bfloat16), logsum)

    def attend_back(pack):
        query_heads, key_heads, value_heads, grad_heads, logsum = pack
        scores = scores_of(query_heads, key_heads, visible, scale)
        probs = jnp.exp(scores - logsum)
        prob_grad = jnp.einsum(
            "qhd,khd->hqk", grad_heads, value_heads, preferred_element_type=jnp.float32
        )
        value_grad = jnp.einsum(
            "hqk,qhd->khd",
            probs.astype(jnp.bfloat16),
            grad_heads,
            preferred_element_type=jnp.float32,
        )
        score_grad = (
            probs * (prob_grad - jnp.sum(probs * prob_grad, axis=-1, keepdims=True))
        ).astype(jnp.bfloat16)
        query_grad = (
            jnp.einsum("hqk,khd->qhd", score_grad, key_heads, preferred_element_type=jnp.float32)
            * scale
        )
        key_grad = (
            jnp.einsum("hqk,qhd->khd", score_grad, query_heads, preferred_element_type=jnp.float32)
            * scale
        )
        return (
            query_grad.reshape(local, width),
            key_grad.reshape(length, width),
            value_grad.reshape(length, width),
        )

    hidden = tokens.reshape(count, width).astype(jnp.float32)
    saved = []
    for layer in range(LAYERS):
        params = fetch_params(weights, layer)
        qkv_full, proj_full, fc_full, fc2_full, fc_b = (
            params[0],
            params[1],
            params[2],
            params[3],
            params[4],
        )
        gains = params[5].astype(jnp.float32)
        shifts = params[6].astype(jnp.float32)
        bias_in = params[7].astype(jnp.float32)
        bias_out = params[8].astype(jnp.float32)
        normed = layer_norm(hidden, gains[0], shifts[0]).astype(jnp.bfloat16)
        mixed = jnp.dot(normed, qkv_full, preferred_element_type=jnp.float32)
        query = (mixed[:, :width] + bias_in[0]).astype(jnp.bfloat16)
        key = mixed[:, width : 2 * width].astype(jnp.bfloat16)
        value = (mixed[:, 2 * width :] + bias_in[1]).astype(jnp.bfloat16)
        keys, values = (
            lax.all_gather(key.reshape(seqs, local, width), "mp", axis=1, tiled=True),
            lax.all_gather(value.reshape(seqs, local, width), "mp", axis=1, tiled=True),
        )
        query_heads = query.reshape(seqs, local, heads, HD)
        key_heads = keys.reshape(seqs, length, heads, HD)
        value_heads = values.reshape(seqs, length, heads, HD)
        attended, logsum = lax.map(attend_one, (query_heads, key_heads, value_heads))
        attended = attended.reshape(count, width)
        middle = (
            hidden + jnp.dot(attended, proj_full, preferred_element_type=jnp.float32) + bias_out[0]
        )
        normed_two = layer_norm(middle, gains[1], shifts[1]).astype(jnp.bfloat16)
        group_rows = lax.all_gather(normed_two, "mp", axis=0, tiled=True)
        inner = jnp.dot(group_rows, fc_full, preferred_element_type=jnp.float32) + fc_b.astype(
            jnp.float32
        )
        active = jax.nn.gelu(inner, approximate=True).astype(jnp.bfloat16)

        def down_rows(start, rows, active=active, fc2_full=fc2_full):
            return jnp.dot(active, fc2_full, preferred_element_type=jnp.float32)

        reduced = lax.psum_scatter(
            down_rows(jnp.int32(0), lax.axis_size("mp") * count).astype(jnp.bfloat16),
            "mp",
            scatter_dimension=0,
            tiled=True,
        ).astype(jnp.float32)
        output = middle + reduced + bias_out[1]
        kept_params = None
        kept_pairs = None
        saved.append(
            (
                hidden,
                normed,
                query,
                key,
                value,
                logsum,
                attended,
                middle,
                group_rows,
                inner,
                kept_params,
                kept_pairs,
            )
        )
        hidden = output
    outputs = hidden.reshape(seqs, local, width)
    grad = cotangent.reshape(count, width).astype(jnp.float32)
    collected = []
    for layer in reversed(range(LAYERS)):
        (
            hidden_in,
            normed,
            query,
            key,
            value,
            logsum,
            attended,
            middle,
            group_rows,
            inner,
            kept_params,
            kept_pairs,
        ) = saved[layer]
        params = fetch_again(weights, layer)
        keys, values = (
            lax.all_gather(key.reshape(seqs, local, width), "mp", axis=1, tiled=True),
            lax.all_gather(value.reshape(seqs, local, width), "mp", axis=1, tiled=True),
        )
        qkv_full, proj_full, fc_full, fc2_full = (params[0], params[1], params[2], params[3])
        gains = params[5].astype(jnp.float32)
        shifts = params[6].astype(jnp.float32)
        out_grad = grad.astype(jnp.bfloat16)
        mlp_bias_grad = jnp.sum(out_grad.astype(jnp.float32), axis=0)
        group_grad = lax.all_gather(out_grad, "mp", axis=0, tiled=True)
        active = jax.nn.gelu(inner, approximate=True).astype(jnp.bfloat16)
        fc2_grad = jnp.einsum("nf,nd->fd", active, group_grad, preferred_element_type=jnp.float32)
        active_grad = jnp.einsum(
            "nd,fd->nf", group_grad, fc2_full, preferred_element_type=jnp.float32
        )
        _, gelu_back = jax.vjp(lambda v: jax.nn.gelu(v, approximate=True), inner)
        inner_grad = gelu_back(active_grad)[0].astype(jnp.bfloat16)
        fc_bias_grad = jnp.sum(inner_grad.astype(jnp.float32), axis=0)
        fc_grad = jnp.einsum(
            "nd,nf->df", group_rows, inner_grad, preferred_element_type=jnp.float32
        )

        def back_rows(start, rows, inner_grad=inner_grad, fc_full=fc_full):
            return jnp.einsum("nf,df->nd", inner_grad, fc_full, preferred_element_type=jnp.float32)

        normed_two_grad = lax.psum_scatter(
            back_rows(jnp.int32(0), lax.axis_size("mp") * count).astype(jnp.bfloat16),
            "mp",
            scatter_dimension=0,
            tiled=True,
        ).astype(jnp.float32)
        _, norm_two_back = jax.vjp(layer_norm, middle, gains[1], shifts[1])
        middle_part, gain_two, shift_two = norm_two_back(normed_two_grad)
        middle_grad = grad + middle_part
        branch_grad = middle_grad.astype(jnp.bfloat16)
        attn_out_bias_grad = jnp.sum(branch_grad.astype(jnp.float32), axis=0)
        proj_grad = jnp.einsum(
            "nd,ne->de", attended, branch_grad, preferred_element_type=jnp.float32
        )
        attended_grad = jnp.einsum(
            "ne,de->nd", branch_grad, proj_full, preferred_element_type=jnp.float32
        ).astype(jnp.bfloat16)
        grad_heads = attended_grad.reshape(seqs, local, heads, HD)
        query_heads = query.reshape(seqs, local, heads, HD)
        key_heads = keys.reshape(seqs, length, heads, HD)
        value_heads = values.reshape(seqs, length, heads, HD)
        query_grad, key_grad, value_grad = lax.map(
            attend_back, (query_heads, key_heads, value_heads, grad_heads, logsum)
        )
        key_part, value_part = (
            lax.psum_scatter(
                key_grad.astype(jnp.bfloat16), "mp", scatter_dimension=1, tiled=True
            ).astype(jnp.float32),
            lax.psum_scatter(
                value_grad.astype(jnp.bfloat16), "mp", scatter_dimension=1, tiled=True
            ).astype(jnp.float32),
        )
        query_round = query_grad.reshape(count, width).astype(jnp.bfloat16)
        key_round = key_part.reshape(count, width).astype(jnp.bfloat16)
        value_round = value_part.reshape(count, width).astype(jnp.bfloat16)
        mixed_grad = jnp.concatenate([query_round, key_round, value_round], axis=1)
        bias_in_grad = jnp.stack(
            [
                jnp.sum(query_round.astype(jnp.float32), axis=0),
                jnp.sum(value_round.astype(jnp.float32), axis=0),
            ]
        )
        qkv_grad = jnp.einsum("nd,ne->de", normed, mixed_grad, preferred_element_type=jnp.float32)
        normed_grad = jnp.einsum(
            "ne,de->nd", mixed_grad, qkv_full, preferred_element_type=jnp.float32
        )
        _, norm_one_back = jax.vjp(layer_norm, hidden_in, gains[0], shifts[0])
        hidden_part, gain_one, shift_one = norm_one_back(normed_grad)
        grad = middle_grad + hidden_part
        gain_grad = jnp.stack([gain_one, gain_two])
        shift_grad = jnp.stack([shift_one, shift_two])
        bias_out_grad = jnp.stack([attn_out_bias_grad, mlp_bias_grad])
        shards = (
            lax.psum_scatter(
                qkv_grad.astype(jnp.bfloat16), "dp", scatter_dimension=0, tiled=True
            ).astype(jnp.float32),
            lax.psum_scatter(
                proj_grad.astype(jnp.bfloat16), "dp", scatter_dimension=0, tiled=True
            ).astype(jnp.float32),
            lax.psum_scatter(
                fc_grad.astype(jnp.bfloat16), "dp", scatter_dimension=0, tiled=True
            ).astype(jnp.float32),
            lax.psum_scatter(
                fc2_grad.astype(jnp.bfloat16), "dp", scatter_dimension=1, tiled=True
            ).astype(jnp.float32),
            lax.psum_scatter(
                fc_bias_grad.astype(jnp.bfloat16), "dp", scatter_dimension=0, tiled=True
            ).astype(jnp.float32),
            lax.psum_scatter(
                gain_grad.astype(jnp.bfloat16), "dp", scatter_dimension=1, tiled=True
            ).astype(jnp.float32),
            lax.psum_scatter(
                shift_grad.astype(jnp.bfloat16), "dp", scatter_dimension=1, tiled=True
            ).astype(jnp.float32),
            lax.psum_scatter(
                bias_in_grad.astype(jnp.bfloat16), "dp", scatter_dimension=1, tiled=True
            ).astype(jnp.float32),
            lax.psum_scatter(
                bias_out_grad.astype(jnp.bfloat16), "dp", scatter_dimension=1, tiled=True
            ).astype(jnp.float32),
        )
        projections = (
            lax.psum_scatter(
                shards[0].astype(jnp.bfloat16), "mp", scatter_dimension=1, tiled=True
            ).astype(jnp.float32),
            lax.psum_scatter(
                shards[1].astype(jnp.bfloat16), "mp", scatter_dimension=1, tiled=True
            ).astype(jnp.float32),
        )
        smaller = lax.psum((shards[5], shards[6], shards[7], shards[8]), "mp")
        factor = 1.0 / data_size
        collected.append(
            (
                projections[0] * factor,
                projections[1] * factor,
                shards[2] * factor,
                shards[3] * factor,
                shards[4] * factor,
                smaller[0] * factor,
                smaller[1] * factor,
                smaller[2] * factor,
                smaller[3] * factor,
            )
        )
    collected = collected[::-1]
    stacked = tuple((jnp.stack([entry[index] for entry in collected]) for index in range(9)))
    input_grad = grad.reshape(seqs, local, width)
    return (
        outputs,
        input_grad,
        stacked[0],
        stacked[1],
        stacked[2],
        stacked[3],
        stacked[4],
        stacked[5],
        stacked[6],
        stacked[7],
        stacked[8],
    )


def grid_index(mesh):
    shape = dict(mesh.shape)
    return shape["dp"] // 2, shape["mp"]


def spots(planes):
    return [(z, c, y, x) for z in range(planes) for c in range(2) for y in range(2) for x in range(2)]


def flat(z, c, y, x):
    return (z * 2 + c) * 4 + y * 2 + x


def pairs_of(planes, move):
    both = [(flat(*spot), flat(*move(*spot))) for spot in spots(planes)]
    return [pair for pair in both if pair[0] != pair[1]]


AXES = ("dp", "mp")
LANES = 128


def nt(a, b):
    return lax.dot_general(a, b, (((1,), (1,)), ((), ())), preferred_element_type=jnp.float32)


def tn(a, b):
    return lax.dot_general(a, b, (((0,), (0,)), ((), ())), preferred_element_type=jnp.float32)


def nn(a, b):
    return jnp.dot(a, b, preferred_element_type=jnp.float32)


def sort_keys(slot_ref, blocks, ok, own_ref, other_ref, cat, put):
    half = blocks * LANES // 2
    cat[:half] = jnp.where(ok, own_ref[...], 0)
    cat[half:] = jnp.where(ok, other_ref[...], 0)
    for j in range(blocks):
        start = pl.multiple_of(slot_ref[j] * LANES, LANES)
        put(j, cat[pl.ds(start, LANES), :])


def two_heads(rows, first):
    zero = jnp.zeros_like(rows)
    return jnp.concatenate([jnp.where(first, rows, zero), jnp.where(first, zero, rows)], axis=0)


def attend_kernel(width, blocks, qblocks, place_ref, slot_ref, q_ref, ko_ref, ks_ref, vo_ref, vs_ref,
                  o_ref, lse_ref, cat, ksort, vsort):
    lane = lax.broadcasted_iota(jnp.int32, (1, LANES), 1)
    ok = lane + pl.program_id(0) * LANES < width
    first = lane < HD

    def put_k(j, rows):
        ksort[j * LANES:(j + 1) * LANES, :] = rows

    def put_v(j, rows):
        vsort[j * LANES:(j + 1) * LANES, :] = rows

    sort_keys(slot_ref, blocks, ok, ko_ref, ks_ref, cat, put_k)
    sort_keys(slot_ref, blocks, ok, vo_ref, vs_ref, cat, put_v)

    def one(b, carry):
        place = place_ref[b]
        here = pl.ds(pl.multiple_of(b * LANES, LANES), LANES)
        rows = (jnp.where(ok, q_ref[here, :], 0) * (HD ** -0.5)).astype(jnp.bfloat16)
        q2 = two_heads(rows, first)
        for n in range(1, blocks // 2 + 1):
            @pl.when(place // 2 == n - 1)
            def _(n=n):
                keys = 2 * LANES * n
                s = nt(ksort[:keys, :], q2)
                row = lax.broadcasted_iota(jnp.int32, (2 * LANES, 2 * LANES), 0) + (keys - 2 * LANES)
                col = lax.broadcasted_iota(jnp.int32, (2 * LANES, 2 * LANES), 1) % LANES + place * LANES
                tail = jnp.where(row <= col, s[keys - 2 * LANES:], -1e30)
                s = tail if n == 1 else jnp.concatenate([s[:keys - 2 * LANES], tail], axis=0)
                top = jnp.max(s, axis=0, keepdims=True)
                e = jnp.exp(s - top)
                total = jnp.sum(e, axis=0, keepdims=True)
                turned = tn(vsort[:keys, :], e.astype(jnp.bfloat16)) / total
                joined = jnp.concatenate([turned[:HD, :LANES], turned[HD:, LANES:]], axis=0)
                o_ref[here, :] = joined.T.astype(jnp.bfloat16)
                lse = top + jnp.log(total)
                lse_ref[0, 0:1, here] = lse[:, :LANES]
                lse_ref[0, 1:2, here] = lse[:, LANES:]
        return carry

    lax.fori_loop(0, qblocks, one, 0)


def attend_back_kernel(width, blocks, qblocks, place_ref, slot_ref, q_ref, ko_ref, ks_ref, vo_ref, vs_ref,
                       do_ref, o_ref, lse_ref, dq_ref, dko_ref, dks_ref, dvo_ref, dvs_ref,
                       cat, ksort, kturn, vsort, dk, dv, loose):
    lane = lax.broadcasted_iota(jnp.int32, (1, LANES), 1)
    ok = lane + pl.program_id(0) * LANES < width
    first = lane < HD

    def put_k(j, rows):
        ksort[j * LANES:(j + 1) * LANES, :] = rows
        kturn[:, j * LANES:(j + 1) * LANES] = rows.astype(jnp.float32).T.astype(jnp.bfloat16)

    def put_v(j, rows):
        vsort[j * LANES:(j + 1) * LANES, :] = rows

    sort_keys(slot_ref, blocks, ok, ko_ref, ks_ref, cat, put_k)
    sort_keys(slot_ref, blocks, ok, vo_ref, vs_ref, cat, put_v)
    dk[...] = jnp.zeros_like(dk)
    dv[...] = jnp.zeros_like(dv)

    def one(b, carry):
        place = place_ref[b]
        here = pl.ds(pl.multiple_of(b * LANES, LANES), LANES)
        rows = (jnp.where(ok, q_ref[here, :], 0) * (HD ** -0.5)).astype(jnp.bfloat16)
        q2 = two_heads(rows, first)
        do = jnp.where(ok, do_ref[here, :], 0)
        do2 = two_heads(do, first)
        both = (do.astype(jnp.float32) * jnp.where(ok, o_ref[here, :], 0).astype(jnp.float32)).T
        delta = jnp.concatenate(
            [jnp.sum(both[:HD], axis=0, keepdims=True), jnp.sum(both[HD:], axis=0, keepdims=True)], axis=1
        )
        lse = jnp.concatenate([lse_ref[0, 0:1, here], lse_ref[0, 1:2, here]], axis=1)
        for n in range(1, blocks // 2 + 1):
            @pl.when(place // 2 == n - 1)
            def _(n=n):
                keys = 2 * LANES * n
                s = nt(ksort[:keys, :], q2)
                row = lax.broadcasted_iota(jnp.int32, (2 * LANES, 2 * LANES), 0) + (keys - 2 * LANES)
                col = lax.broadcasted_iota(jnp.int32, (2 * LANES, 2 * LANES), 1) % LANES + place * LANES
                tail = jnp.where(row <= col, s[keys - 2 * LANES:], -1e30)
                s = tail if n == 1 else jnp.concatenate([s[:keys - 2 * LANES], tail], axis=0)
                p = jnp.exp(s - lse)
                dp = nt(vsort[:keys, :], do2)
                ds = (p * (dp - delta)).astype(jnp.bfloat16)
                dv[:keys, :] += nn(p.astype(jnp.bfloat16), do2)
                dk[:keys, :] += nn(ds, q2)
                turned = nn(kturn[:, :keys], ds) * (HD ** -0.5)
                joined = jnp.concatenate([turned[:HD, :LANES], turned[HD:, LANES:]], axis=0)
                dq_ref[here, :] = joined.T.astype(jnp.bfloat16)
        return carry

    lax.fori_loop(0, qblocks, one, 0)
    half = blocks * LANES // 2
    for source, mine, theirs in ((dk, dko_ref, dks_ref), (dv, dvo_ref, dvs_ref)):
        for j in range(blocks):
            start = pl.multiple_of(slot_ref[j] * LANES, LANES)
            loose[pl.ds(start, LANES), :] = source[j * LANES:(j + 1) * LANES, :]
        mine[...] = loose[:half]
        theirs[...] = loose[half:].astype(jnp.bfloat16)


def attention_specs(rows):
    tall = pl.BlockSpec((rows, LANES), lambda i, *_: (0, i))
    stat = pl.BlockSpec((1, 2, rows), lambda i, *_: (i, 0, 0))
    return tall, stat


def attention(place, slot, q, ko, ks, vo, vs):
    rows, width = q.shape
    steps = -(-width // LANES)
    blocks, keys = slot.shape[0], slot.shape[0] * LANES
    tall, stat = attention_specs(rows)
    elems = rows * keys * steps * 2
    return pl.pallas_call(
        functools.partial(attend_kernel, width, blocks, place.shape[0]),
        grid_spec=pltpu.PrefetchScalarGridSpec(
            num_scalar_prefetch=2,
            grid=(steps,),
            in_specs=[tall] * 5,
            out_specs=[tall, stat],
            scratch_shapes=[
                pltpu.VMEM((keys, LANES), jnp.bfloat16),
                pltpu.VMEM((keys, LANES), jnp.bfloat16),
                pltpu.VMEM((keys, LANES), jnp.bfloat16),
            ],
        ),
        out_shape=[
            jax.ShapeDtypeStruct((rows, width), jnp.bfloat16),
            jax.ShapeDtypeStruct((steps, 2, rows), jnp.float32),
        ],
        cost_estimate=pl.CostEstimate(flops=elems * HD * 8, bytes_accessed=rows * width * 12, transcendentals=elems),
        compiler_params=pltpu.CompilerParams(vmem_limit_bytes=40 * 2 ** 20),
        name="attention",
    )(place, slot, q, ko, ks, vo, vs)


def attention_back(place, slot, q, ko, ks, vo, vs, do, o, lse):
    rows, width = q.shape
    steps = -(-width // LANES)
    blocks, keys = slot.shape[0], slot.shape[0] * LANES
    tall, stat = attention_specs(rows)
    elems = rows * keys * steps * 2
    wide = jax.ShapeDtypeStruct((rows, steps * LANES), jnp.float32)
    thin = jax.ShapeDtypeStruct((rows, steps * LANES), jnp.bfloat16)
    narrow = jax.ShapeDtypeStruct((rows, width), jnp.bfloat16)
    return pl.pallas_call(
        functools.partial(attend_back_kernel, width, blocks, place.shape[0]),
        grid_spec=pltpu.PrefetchScalarGridSpec(
            num_scalar_prefetch=2,
            grid=(steps,),
            in_specs=[tall] * 7 + [stat],
            out_specs=[tall] * 5,
            scratch_shapes=[
                pltpu.VMEM((keys, LANES), jnp.bfloat16),
                pltpu.VMEM((keys, LANES), jnp.bfloat16),
                pltpu.VMEM((LANES, keys), jnp.bfloat16),
                pltpu.VMEM((keys, LANES), jnp.bfloat16),
                pltpu.VMEM((keys, LANES), jnp.float32),
                pltpu.VMEM((keys, LANES), jnp.float32),
                pltpu.VMEM((keys, LANES), jnp.float32),
            ],
        ),
        out_shape=[narrow, wide, thin, wide, thin],
        cost_estimate=pl.CostEstimate(flops=elems * HD * 20, bytes_accessed=rows * width * 30, transcendentals=elems),
        compiler_params=pltpu.CompilerParams(vmem_limit_bytes=40 * 2 ** 20),
        name="attention_back",
    )(place, slot, q, ko, ks, vo, vs, do, o, lse)


def gather_kernel(planes, piece_ref, small_ref, token_ref, out_ref, small_out, token_out,
                  send_sem, recv_sem, small_send, small_recv, swap_send, swap_recv, own_sem):
    dp, mp = lax.axis_index("dp"), lax.axis_index("mp")
    z, c = dp // 2, dp % 2
    y, x = mp // 2, mp % 2
    side = mp + 1 - 2 * x
    across = mp + 2 - 4 * y
    corner = 3 - mp
    to_x, to_y, to_c = (dp, side), (dp, across), (dp + 1 - 2 * c, mp)
    to_z = [(lax.rem(z + k, planes) * 2 + c, mp) for k in range(1, planes)]
    same, turned = (z * 2 + y, c * 2 + x), (z * 2 + y, c * 2 + 1 - x)
    barrier = pltpu.get_barrier_semaphore()
    for peer in (to_x, to_y, to_c, *to_z, turned):
        pl.semaphore_signal(barrier, inc=1, device_id=peer, device_id_type=pl.DeviceIdType.MESH)

    @pl.when(y != c)
    def _():
        pl.semaphore_signal(barrier, inc=1, device_id=same, device_id_type=pl.DeviceIdType.MESH)

    pl.semaphore_wait(barrier, 4 + len(to_z) + (y - c) * (y - c))

    locals_ = [
        pltpu.make_async_copy(piece_ref, out_ref.at[mp, dp], own_sem.at[0]),
        pltpu.make_async_copy(small_ref, small_out.at[dp], own_sem.at[1]),
    ]
    for copy in locals_:
        copy.start()
    sent = []

    def remote(source, target, sems, peer):
        copy = pltpu.make_async_remote_copy(
            src_ref=source,
            dst_ref=target,
            send_sem=sems[0],
            recv_sem=sems[1],
            device_id=peer,
            device_id_type=pl.DeviceIdType.MESH,
        )
        copy.start()
        return copy

    def send(source, index, row, peer):
        sent.append(remote(source, out_ref.at[index, row], (send_sem.at[len(sent)], recv_sem.at[index, row]), peer))

    def arrived(index, row):
        pltpu.make_async_copy(out_ref.at[index, row], out_ref.at[index, row], recv_sem.at[index, row]).wait()
        return out_ref.at[index, row]

    def swap(source, target, which):
        moved = remote(source.at[1 - x], target.at[1], (swap_send.at[which, 1], swap_recv.at[which, 1]), turned)
        kept = pltpu.make_async_copy(source.at[x], target.at[0], own_sem.at[2 + which])
        pair = (source.at[x], target.at[0], (swap_send.at[which, 0], swap_recv.at[which, 0]), same)

        @pl.when(y == c)
        def _():
            kept.start()

        @pl.when(y != c)
        def _():
            remote(*pair)

        def finish():
            moved.wait()

            @pl.when(y == c)
            def _():
                kept.wait()

            @pl.when(y != c)
            def _():
                pltpu.make_async_remote_copy(
                    src_ref=pair[0],
                    dst_ref=pair[1],
                    send_sem=pair[2][0],
                    recv_sem=pair[2][1],
                    device_id=same,
                    device_id_type=pl.DeviceIdType.MESH,
                ).wait()

        return finish

    rows = [lax.rem(z - k + planes, planes) * 2 + c for k in range(planes)]
    little = []

    def send_small(source, row, peer):
        little.append(
            remote(source, small_out.at[row], (small_send.at[len(little)], small_recv.at[row]), peer)
        )

    def small_arrived(row):
        pltpu.make_async_copy(small_out.at[row], small_out.at[row], small_recv.at[row]).wait()
        return small_out.at[row]

    for peer in (*to_z, to_c):
        send_small(small_ref, dp, peer)
    for peer in to_z:
        send(piece_ref, mp, dp, peer)
    for peer in (to_x, to_y, to_c):
        send(piece_ref, mp, dp, peer)
    finishes = [swap(token_ref, token_out, 0)]
    for k in range(planes):
        if k > 0:
            send_small(small_arrived(rows[k]), rows[k], to_c)
            block = arrived(mp, rows[k])
            for peer in (to_x, to_y, to_c):
                send(block, mp, rows[k], peer)
            send(arrived(corner, rows[k - 1]), corner, rows[k - 1], to_c)
        block = arrived(side, rows[k])
        if k % 2 == 0:
            send(block, side, rows[k], to_y)
        send(block, side, rows[k], to_c)
        block = arrived(across, rows[k])
        if k % 2 == 1:
            send(block, across, rows[k], to_x)
        send(block, across, rows[k], to_c)
    send(arrived(corner, rows[-1]), corner, rows[-1], to_c)
    for k in range(planes):
        beside = rows[k] + 1 - 2 * c
        small_arrived(beside)
        for index in (mp, side, across, corner):
            arrived(index, beside)
    for copy in sent + little:
        copy.wait_send()
    for finish in finishes:
        finish()
    for copy in locals_:
        copy.wait()


def gather_four(planes, piece, small, tokens):
    count = (planes - 1) + 3 * planes + planes + 3 * planes
    anywhere = pl.BlockSpec(memory_space=pl.ANY)
    return pl.pallas_call(
        functools.partial(gather_kernel, planes),
        in_specs=[anywhere] * 3,
        out_specs=[anywhere] * 3,
        out_shape=[
            jax.ShapeDtypeStruct((4, 2 * planes) + piece.shape, piece.dtype),
            jax.ShapeDtypeStruct((2 * planes,) + small.shape, small.dtype),
            jax.ShapeDtypeStruct(tokens.shape, tokens.dtype),
        ],
        scratch_shapes=[
            pltpu.SemaphoreType.DMA((count,)),
            pltpu.SemaphoreType.DMA((4, 2 * planes)),
            pltpu.SemaphoreType.DMA((2 * planes,)),
            pltpu.SemaphoreType.DMA((2 * planes,)),
            pltpu.SemaphoreType.DMA((2, 2)),
            pltpu.SemaphoreType.DMA((2, 2)),
            pltpu.SemaphoreType.DMA((4,)),
        ],
        cost_estimate=pl.CostEstimate(flops=0, bytes_accessed=300 * 2 ** 20, transcendentals=0),
        compiler_params=pltpu.CompilerParams(collective_id=0, has_side_effects=True),
        name="gather_four",
    )(piece, small, tokens)


GROUPS, PARTS = 4, 2


def tiles(width, body):
    whole = width // 256

    def step(j, carry):
        body(pl.multiple_of(j * 256, 256), 256)
        return carry

    lax.fori_loop(0, whole, step, 0)
    if width % 256:
        body(whole * 256, width % 256)


def units_kernel(back, counts, *refs):
    x_ref, wa_own, wb_own, *refs = refs
    (*wa_moved,), refs = refs[:counts[0]], refs[counts[0]:]
    (*wb_moved,), refs = refs[:counts[1]], refs[counts[1]:]
    if back:
        (slope_ref, act_ref, out_ref, rows_ref, left_ref, sums_ref, grad_ref, act, grad, *scratch) = refs
    else:
        (bias_ref, out_ref, rows_ref, left_ref, slope_ref, *scratch) = refs
    (wa, wb, rows, own, far, beside, corner, got_c, got_f, give, got_y, left, slope,
     in_sem, send_sem, recv_sem, out_sem) = scratch
    width = wa.shape[1]
    part = rows.shape[2]
    dp, mp = lax.axis_index("dp"), lax.axis_index("mp")
    to_c = (dp + 1 - 2 * (dp % 2), mp)
    to_y = (dp, mp + 2 - 4 * (mp // 2))
    loads = [
        pltpu.make_async_copy(x_ref.at[pl.ds(h * part, part)], rows.at[0, h], in_sem.at[h]) for h in range(PARTS)
    ]
    moved = []
    for slot, (own_ref, moved_refs, target) in enumerate(((wa_own, wa_moved, wa), (wb_own, wb_moved, wb))):
        tall = wa.shape[0] // len(moved_refs)
        for side, part_ref in enumerate(moved_refs):
            span = pl.ds(side * tall, tall)
            sem = in_sem.at[6 + 2 * slot + side]
            loads.append(pltpu.make_async_copy(own_ref.at[span], target.at[span], sem))
            moved.append(pltpu.make_async_copy(part_ref, target.at[span], sem))
    for load in loads[:PARTS]:
        load.start()

    @pl.when(mp % 2 == dp % 2)
    def _():
        for load in loads[PARTS:]:
            load.start()

    @pl.when(mp % 2 != dp % 2)
    def _():
        for load in moved:
            load.start()

    barrier = pltpu.get_barrier_semaphore()
    for peer in (to_c, to_y):
        pl.semaphore_signal(barrier, inc=1, device_id=peer, device_id_type=pl.DeviceIdType.MESH)
    pl.semaphore_wait(barrier, 2)
    sent = []

    def send(source, target, slot, peer):
        copy = pltpu.make_async_remote_copy(
            src_ref=source,
            dst_ref=target,
            send_sem=send_sem.at[slot],
            recv_sem=recv_sem.at[slot],
            device_id=peer,
            device_id_type=pl.DeviceIdType.MESH,
        )
        copy.start()
        sent.append(copy)
        return copy

    kinds = {name: i for i, name in enumerate(("y", "c", "f", "beside", "corner", "give"))}

    def slot_of(kind, h):
        return kinds[kind] * PARTS + h

    arrivals = {}
    for h in range(PARTS):
        loads[h].wait()
        arrivals["y", h] = send(rows.at[0, h], rows.at[2, h], slot_of("y", h), to_y)
        arrivals["c", h] = send(rows.at[0, h], rows.at[1, h], slot_of("c", h), to_c)
    stores = []
    busy = [[], []]
    order = [(0, 0), (0, 1), (1, 0), (1, 1), (2, 0), (3, 0), (2, 1), (3, 1)]

    def place(index):
        group, h = order[index]
        return pl.ds((group * PARTS + h) * part, part)

    def fetch(index):
        copy = pltpu.make_async_copy(slope_ref.at[place(index)], slope.at[index % 2], in_sem.at[4 + index % 2])
        copy.start()
        return copy

    def store(source, target, index, kind):
        copy = pltpu.make_async_copy(source, target, out_sem.at[kind, index])
        copy.start()
        return copy

    fetched = {}
    if back:
        sums_ref[...] = jnp.zeros_like(sums_ref)
        fetched[0] = fetch(0)
        act_load = pltpu.make_async_copy(act_ref, act, in_sem.at[10])
        act_load.start()
    for load in loads[PARTS:]:
        load.wait()

    def work(index, target):
        group, h = order[index]
        side = index % 2
        for copy in busy[side]:
            copy.wait()
        busy[side] = []
        source = rows.at[group, h]
        if back:
            fetched[index].wait()
            if index + 1 < len(order):
                fetched[index + 1] = fetch(index + 1)

        def first(at, size):
            span = pl.ds(at, size)
            value = nn(source[...], wa[:, span])
            if back:
                value = bf(value * f32(slope[side, :, span]))
                left[side, :, span] = value
                sums_ref[:, span] += jnp.sum(f32(value), axis=0, keepdims=True)
            else:
                value = value + bias_ref[:, span]
                square = value * value
                bend = jnp.tanh(0.7978845608028654 * value * (1.0 + 0.044715 * square))
                half = 0.5 * (1.0 + bend)
                left[side, :, span] = bf(value * half)
                slope[side, :, span] = bf(
                    half + 0.5 * value * (1.0 - bend * bend) * 0.7978845608028654 * (1.0 + 0.134145 * square)
                )

        tiles(width, first)
        busy[side].append(store(left.at[side], left_ref.at[place(index)], index, 0))
        if not back:
            busy[side].append(store(slope.at[side], slope_ref.at[place(index)], index, 1))
        stores.append(store(source, rows_ref.at[place(index)], index, 2))

        def second(at, size):
            span = pl.ds(at, size)
            target[:, span] = nt(left[side], wb[span, :]).astype(target.dtype)

        tiles(width, second)

    def combine(h):
        arrivals["corner", h].wait_recv()
        give[h] = bf(far[h] + f32(got_f[h]))
        arrivals["give", h] = send(give.at[h], got_y.at[h], slot_of("give", h), to_y)

    work(0, own.at[0])
    work(1, own.at[1])
    for h in range(PARTS):
        arrivals["c", h].wait_recv()
        work(2 + h, beside.at[h])
        arrivals["beside", h] = send(beside.at[h], got_c.at[h], slot_of("beside", h), to_c)
    for h in range(PARTS):
        arrivals["y", h].wait_recv()
        arrivals["f", h] = send(rows.at[2, h], rows.at[3, h], slot_of("f", h), to_c)
        work(4 + 2 * h, far.at[h])
        arrivals["f", h].wait_recv()
        work(5 + 2 * h, corner.at[h])
        arrivals["corner", h] = send(corner.at[h], got_f.at[h], slot_of("corner", h), to_c)
        combine(h)
    if back:
        act_load.wait()
        leaving = {}
        for j in range(-(-width // 256)):
            at, size, side = j * 256, min(256, width - j * 256), j % 2
            if j >= 2:
                leaving[j - 2].wait()

            def column(first, length, at=at, size=size, side=side):
                span = pl.ds(first, length)
                value = None
                for group in range(GROUPS):
                    for h in range(PARTS):
                        here = pl.ds((group * PARTS + h) * part, part)
                        term = tn(rows[group, h, :, at:at + size], act[here, span])
                        value = term if value is None else value + term
                grad[side, :size, span] = bf(value)

            tiles(width, column)
            leaving[j] = pltpu.make_async_copy(
                grad.at[side, pl.ds(0, size)], grad_ref.at[pl.ds(at, size)], in_sem.at[11 + side]
            )
            leaving[j].start()
        for j in list(leaving)[-2:]:
            leaving[j].wait()
    for h in range(PARTS):
        arrivals["beside", h].wait_recv()
        arrivals["give", h].wait_recv()
        out_ref[pl.ds(h * part, part), :] = own[h] + f32(got_c[h]) + f32(got_y[h])
    for copy in sent:
        copy.wait_send()
    for copy in stores + busy[0] + busy[1]:
        copy.wait()


def units(back, x, wa, wb, *extra):
    rows, width = x.shape
    part = rows // PARTS
    half = jax.ShapeDtypeStruct((GROUPS * rows, width), jnp.bfloat16)
    anywhere = pl.BlockSpec(memory_space=pl.ANY)
    inside = pl.BlockSpec(memory_space=pltpu.VMEM)
    thin, wide = pltpu.VMEM((PARTS, part, width), jnp.bfloat16), pltpu.VMEM((PARTS, part, width), jnp.float32)
    count = 6 * PARTS
    moved = (*wa[1:], *wb[1:])
    square = wa[0].shape
    work = []
    if back:
        work = [pltpu.VMEM((GROUPS * rows, width), jnp.bfloat16), pltpu.VMEM((2, 256, width), jnp.bfloat16)]
    return pl.pallas_call(
        functools.partial(units_kernel, back, (len(wa) - 1, len(wb) - 1)),
        in_specs=[anywhere] * (3 + len(moved)) + ([anywhere] * 2 if back else [inside]),
        out_specs=[inside, anywhere, anywhere] + ([inside, anywhere] if back else [anywhere]),
        out_shape=[jax.ShapeDtypeStruct((rows, width), jnp.float32), half, half]
        + ([jax.ShapeDtypeStruct((1, width), jnp.float32), jax.ShapeDtypeStruct(square, jnp.bfloat16)] if back else [half]),
        scratch_shapes=[
            *work,
            pltpu.VMEM(square, jnp.bfloat16),
            pltpu.VMEM(square, jnp.bfloat16),
            pltpu.VMEM((GROUPS, PARTS, part, width), jnp.bfloat16),
            wide, wide, thin, thin, thin, thin, thin, thin, thin, thin,
            pltpu.SemaphoreType.DMA((13,)),
            pltpu.SemaphoreType.DMA((count,)),
            pltpu.SemaphoreType.DMA((count,)),
            pltpu.SemaphoreType.DMA((3, GROUPS * PARTS)),
        ],
        cost_estimate=pl.CostEstimate(
            flops=60 * 10 ** 9, bytes_accessed=60 * 2 ** 20, transcendentals=0
        ),
        compiler_params=pltpu.CompilerParams(
            collective_id=2 if back else 1, has_side_effects=True, vmem_limit_bytes=58 * 2 ** 20
        ),
        name="units_back" if back else "units",
    )(x, wa[0], wb[0], *moved, *extra)


def settle_kernel(planes, keep_ref, send_ref, piece_ref, sum_ref, out_ref, sum_out, pieces, outgo, income, total, from_y, from_x, to_give,
                  final, from_z, sum_at, sum_from, load_sem, c_send, c_recv, xy_send, xy_recv, z_send, z_recv,
                  sum_send, sum_recv):
    dp, mp = lax.axis_index("dp"), lax.axis_index("mp")
    z, c = dp // 2, dp % 2
    y, x = mp // 2, mp % 2
    to_x, to_y = (dp, mp + 1 - 2 * x), (dp, mp + 2 - 4 * y)
    to_c = (dp + 1 - 2 * c, mp)
    others = [lax.rem(z + k, planes) for k in range(1, planes)]
    barrier = pltpu.get_barrier_semaphore()
    for peer in (to_x, to_y, to_c, *[(other * 2 + c, mp) for other in others]):
        pl.semaphore_signal(barrier, inc=1, device_id=peer, device_id_type=pl.DeviceIdType.MESH)
    loads = []
    for k, (far_y, far_x) in enumerate(((1, 1), (1, 0), (0, 1), (0, 0))):
        index = 2 * (1 - y if far_y else y) + (1 - x if far_x else x)
        loads.append(pltpu.make_async_copy(piece_ref.at[index], pieces.at[k], load_sem.at[k]))
        loads[-1].start()
    pl.semaphore_wait(barrier, 3 + len(others))
    width = pieces.shape[2]
    tall = keep_ref.shape[0] // planes
    half = planes // 2

    def remote(source, target, sems, slot, peer):
        copy = pltpu.make_async_remote_copy(
            src_ref=source,
            dst_ref=target,
            send_sem=sems[0].at[slot],
            recv_sem=sems[1].at[slot],
            device_id=peer,
            device_id_type=pl.DeviceIdType.MESH,
        )
        copy.start()
        return copy

    def product(left_ref, k, write):
        def body(at, size):
            span = pl.ds(at, size)
            value = nn(left_ref[...], pieces[k, :, span])
            for block in range(planes):
                write(block, span, value[block * tall:(block + 1) * tall])

        tiles(width, body)

    adding = [remote(sum_ref, sum_from.at[0], (sum_send, sum_recv), 0, to_c)]

    def sum_step(k, source, peer):
        adding[k].wait_recv()
        sum_at[k] = source[...] + sum_from[k]
        if peer is not None:
            adding.append(remote(sum_at.at[k], sum_from.at[k + 1], (sum_send, sum_recv), k + 1, peer))

    crossing = []
    for k in range(4):
        loads[k].wait()

        def put(block, span, value, k=k):
            outgo[k, block, :, span] = bf(value)

        product(send_ref, k, put)
        crossing.append(remote(outgo.at[k], income.at[k], (c_send, c_recv), k, to_c))
    first, second = pl.ds(0, half), pl.ds(half, half)
    sent = []

    def chip(k):
        crossing[k].wait_recv()

        def put(block, span, value, k=k):
            total[k, block, :, span] = bf(value + f32(income[k, block, :, span]))

        product(keep_ref, k, put)

    def add(target, base, extras):
        for block in range(half):
            value = f32(base[block])
            for extra in extras:
                value = value + f32(extra[block])
            target[block] = value.astype(target.dtype)

    sems = (xy_send, xy_recv)
    sum_step(0, sum_ref, to_x)
    chip(0)
    y0 = remote(total.at[0, first], from_y.at[0], sems, 0, to_y)
    x0 = remote(total.at[0, second], from_x.at[0], sems, 1, to_x)
    chip(1)
    y1 = remote(total.at[1, first], from_y.at[1], sems, 2, to_y)
    sum_step(1, sum_at.at[0], to_y)
    chip(2)
    x1 = remote(total.at[2, second], from_x.at[1], sems, 3, to_x)
    chip(3)
    sum_step(2, sum_at.at[1], None)
    for k, other in enumerate(others):
        adding.append(remote(sum_at.at[2], sum_from.at[3 + k], (sum_send, sum_recv), 3 + k, (other * 2 + c, mp)))
    y0.wait_recv()
    add(to_give.at[0], total.at[2, first], [from_y.at[0]])
    x2 = remote(to_give.at[0], from_x.at[2], sems, 4, to_x)
    x0.wait_recv()
    add(to_give.at[1], total.at[1, second], [from_x.at[0]])
    y2 = remote(to_give.at[1], from_y.at[2], sems, 5, to_y)
    y1.wait_recv()
    x2.wait_recv()
    add(final.at[first], total.at[3, first], [from_y.at[1], from_x.at[2]])
    x1.wait_recv()
    y2.wait_recv()
    add(final.at[second], total.at[3, second], [from_x.at[1], from_y.at[2]])
    leaving = []
    for k, other in enumerate(others):
        leaving.append(remote(final.at[other], from_z.at[k], (z_send, z_recv), k, (other * 2 + c, mp)))
    value = f32(final[z])
    for k in range(len(others)):
        leaving[k].wait_recv()
        value = value + f32(from_z[k])
    out_ref[...] = value * (1.0 / (2 * planes))
    value = sum_at[2]
    for k in range(len(others)):
        adding[3 + k].wait_recv()
        value = value + sum_from[3 + k]
    sum_out[...] = value
    for copy in (*crossing, y0, x0, y1, x1, x2, y2, *leaving, *adding):
        copy.wait_send()


def settle_columns(planes, keep, send, pieces, sums):
    rows, width = keep.shape[0], pieces.shape[2]
    tall = rows // planes
    half = planes // 2
    low = lambda *shape: pltpu.VMEM((*shape, tall, width), jnp.bfloat16)
    inside = pl.BlockSpec(memory_space=pltpu.VMEM)
    return pl.pallas_call(
        functools.partial(settle_kernel, planes),
        in_specs=[inside, inside, pl.BlockSpec(memory_space=pl.ANY), inside],
        out_specs=[inside, inside],
        out_shape=[
            jax.ShapeDtypeStruct((tall, width), jnp.float32),
            jax.ShapeDtypeStruct(sums.shape, jnp.float32),
        ],
        scratch_shapes=[
            pltpu.VMEM(pieces.shape, jnp.bfloat16),
            low(4, planes), low(4, planes), low(4, planes),
            low(3, half), low(3, half), low(2, half), low(planes), low(planes - 1),
            pltpu.VMEM((3, *sums.shape), jnp.float32),
            pltpu.VMEM((2 + planes, *sums.shape), jnp.float32),
            pltpu.SemaphoreType.DMA((4,)),
            pltpu.SemaphoreType.DMA((4,)), pltpu.SemaphoreType.DMA((4,)),
            pltpu.SemaphoreType.DMA((6,)), pltpu.SemaphoreType.DMA((6,)),
            pltpu.SemaphoreType.DMA((planes - 1,)), pltpu.SemaphoreType.DMA((planes - 1,)),
            pltpu.SemaphoreType.DMA((2 + planes,)), pltpu.SemaphoreType.DMA((2 + planes,)),
        ],
        cost_estimate=pl.CostEstimate(flops=16 * 10 ** 9, bytes_accessed=60 * 2 ** 20, transcendentals=0),
        compiler_params=pltpu.CompilerParams(
            collective_id=3, has_side_effects=True, vmem_limit_bytes=58 * 2 ** 20
        ),
        name="settle_columns",
    )(keep, send, pieces, sums)


def bf(value):
    return value.astype(jnp.bfloat16)


def f32(value):
    return value.astype(jnp.float32)


def norm_parts(value):
    mean = jnp.mean(value, axis=-1, keepdims=True)
    centred = value - mean
    spread = jnp.mean(centred * centred, axis=-1, keepdims=True)
    return centred, lax.rsqrt(spread + eps)


def norm_back(grad, value, gain):
    centred, rate = norm_parts(value)
    hat = centred * rate
    scaled = grad * gain
    inner = scaled - jnp.mean(scaled, axis=-1, keepdims=True) - hat * jnp.mean(scaled * hat, axis=-1, keepdims=True)
    return inner * rate, jnp.sum(grad * hat, axis=0), jnp.sum(grad, axis=0)


def quick_body(
    planes,
    tokens,
    cotangent,
    block_order,
    qkv_weight,
    proj_weight,
    fc_weight,
    fc2_weight,
    fc_bias,
    norm_gain,
    norm_shift,
    attn_bias,
    out_bias,
):
    seqs, local, width = tokens.shape
    slots = local // LANES
    dp_rank = lax.axis_index("dp")
    mp_rank = lax.axis_index("mp")
    core, row, col = dp_rank % 2, mp_rank // 2, mp_rank % 2
    over_x = pairs_of(planes, lambda z, c, y, x: (z, c, y, 1 - x))
    over_y = pairs_of(planes, lambda z, c, y, x: (z, c, 1 - y, x))
    over_xy = pairs_of(planes, lambda z, c, y, x: (z, c, 1 - y, 1 - x))
    over_c = pairs_of(planes, lambda z, c, y, x: (z, 1 - c, y, x))
    swap_yc = pairs_of(planes, lambda z, c, y, x: (z, y, c, x))
    swap_xc = pairs_of(planes, lambda z, c, y, x: (z, x, y, c))

    along_z = [
        [flat(z, c, y, x) for z in range(planes)] for c in range(2) for y in range(2) for x in range(2)
    ]

    along_dp = [[flat(z, c, y, x) for z in range(planes) for c in range(2)] for y in range(2) for x in range(2)]

    def go(value, pairs):
        return lax.ppermute(value, AXES, pairs)

    def turn_yc(value):
        return jnp.where(row == core, value, go(value, swap_yc))

    def turn_xc(value):
        return jnp.where(col == core, value, go(value, swap_xc))

    def sum_z(value):
        return lax.psum_scatter(value, AXES, axis_index_groups=along_z, scatter_dimension=0, tiled=True)

    ranks = jnp.stack([2 * core + col, 2 * core + 1 - col])
    others = jnp.stack([2 * (1 - core) + col, 2 * (1 - core) + 1 - col])

    def places(which):
        return block_order.reshape(-1, slots)[which].reshape(-1)

    place = places(ranks)
    keyed = jnp.concatenate([place, places(others)])
    blocks = keyed.shape[0]
    order = jnp.arange(blocks, dtype=jnp.int32)
    slot = jnp.sum(jnp.where(keyed[None, :] == order[:, None], order[None, :], 0), axis=1).astype(jnp.int32)

    def add_pair(a, b):
        return bf(f32(a) + f32(b))

    def core_columns(value, which):
        parts = value.reshape(value.shape[0], planes, 2, -1)
        return lax.dynamic_index_in_dim(parts, which, 2, keepdims=False).reshape(value.shape[0], -1)

    def chip_sums(left, right):
        keep, send = core_columns(left, core), core_columns(left, 1 - core)
        size = right.shape[1] // 4

        def one(near_y, near_x):
            index = 2 * (row if near_y else 1 - row) + (col if near_x else 1 - col)
            piece = lax.dynamic_slice_in_dim(right, index * size, size, axis=1)
            return add_pair(tn(keep, piece), go(bf(tn(send, piece)), over_c))

        return one(False, False), one(False, True), one(True, False), one(True, True)

    def gather_dp(piece):
        return lax.all_gather(piece, "dp", axis=0, tiled=True)

    def after(values, *done):
        return lax.optimization_barrier((values, done))[0]

    def fence(*values):
        return lax.optimization_barrier(values)

    def stacked(layer):
        qkv = qkv_weight[layer]
        return jnp.stack([qkv[:, :width], qkv[:, width:2 * width], qkv[:, 2 * width:], proj_weight[layer]])

    small = f32(jnp.concatenate([norm_gain, norm_shift, attn_bias, out_bias, fc_bias[:, None, :]], axis=1))
    count = small.shape[0] * small.shape[1]
    small = jnp.pad(small.reshape(count, -1), ((0, -count % 8), (0, 0)))
    piece = lax.dynamic_index_in_dim(stacked(0), mp_rank, 0, keepdims=False)
    full, small, token_rows = gather_four(planes, piece, small, tokens)
    first_four = full.reshape(4, width, width)
    small = jnp.transpose(small[:, :count].reshape(-1, LAYERS, 9, width // (2 * planes)), (1, 2, 0, 3))
    small = small.reshape(LAYERS, 9, width)
    units_bias = turn_xc(small[:, 8])

    fc_slice = [None] * LAYERS
    fc2_slice = [None] * LAYERS
    fc_slice[0] = gather_dp(fc_weight[0])
    fc2_slice[0] = gather_dp(fc2_weight[0].T)
    qkv1 = qkv_weight[1]
    pair = gather_dp(jnp.where(row == 0, qkv1[:, :width], qkv1[:, width:2 * width]))
    tall = width // 2

    def pair_join(whole, got, bit):
        got = jnp.concatenate(got, axis=0)
        beside = go(got, over_c)
        other = jnp.concatenate([jnp.where(core == 0, got, beside), jnp.where(core == 0, beside, got)], axis=0)
        return jnp.where(bit == 0, whole, other), jnp.where(bit == 0, other, whole)

    def halves(value):
        middle = value.shape[0] // 2
        return value[:middle], value[middle:]

    def padded(value):
        return jnp.pad(value, ((0, 0), (0, -width % LANES)))

    def normal(value, layer, which):
        centred, rate = norm_parts(value)
        return bf(centred * rate * small[layer, which] + small[layer, 2 + which])

    def attend(layer, hidden, w):
        normed = normal(hidden, layer, 0)
        key = padded(bf(nn(normed, w["k"])))
        key_other = go(key, over_c)
        value = padded(bf(nn(normed, w["v"]) + small[layer, 5]))
        value_other = go(value, over_c)
        query = bf(nn(normed, w["q"]) + small[layer, 4])
        return normed, query, key, key_other, value, value_other

    def project(layer, hidden, attended, w):
        middle = hidden + nn(attended, w["proj"]) + small[layer, 6]
        return middle, normal(middle, layer, 1)

    turn_far = pairs_of(planes, lambda z, c, y, x: (z, y, c, 1 - x))

    def cot_regroup():
        mine = lax.dynamic_index_in_dim(cotangent, col, 0, keepdims=False)
        theirs = lax.dynamic_index_in_dim(cotangent, 1 - col, 0, keepdims=False)
        return mine, go(mine, swap_yc), go(theirs, turn_far)

    saved = []
    hidden = f32(token_rows.reshape(-1, width))
    w = dict(q=first_four[0], k=first_four[1], v=first_four[2], proj=first_four[3])
    first_fc = after(fc_slice[0], units_bias)
    fc_moved = go(first_fc, swap_xc)
    fc_slice[1] = gather_dp(after(fc_weight[1], small))
    parts = attend(0, hidden, w)
    *parts, fc_moved, fc2_now, pair = fence(*parts, fc_moved, fc2_slice[0], pair)
    normed, query, key, key_other, value, value_other = parts
    v1 = gather_dp(after(qkv1[:, 2 * width:], normed))
    fc2_parts = halves(fc2_now)
    pair_parts = halves(lax.dynamic_slice_in_dim(pair, core * tall, tall, axis=0))
    fc2_top = go(fc2_parts[0], swap_xc)
    got = [go(pair_parts[0], over_y)]
    attended, lse = attention(place, slot, query, key, key_other, value, value_other)
    attended, lse, fc2_top, got[0] = fence(attended, lse, fc2_top, got[0])
    proj1 = gather_dp(after(proj_weight[1], attended))
    fc2_end = go(fc2_parts[1], swap_xc)
    got.append(go(pair_parts[1], over_y))
    middle, normed_two = project(0, hidden, attended, w)
    middle, normed_two, fc2_end, got[1], fc_now = fence(middle, normed_two, fc2_end, got[1], fc_slice[1])
    w["fc"] = (first_fc, fc_moved)
    w["fc2"] = (fc2_now, fc2_top, fc2_end)
    fc2_slice[1] = gather_dp(after(fc2_weight[1].T, middle))
    fc_moved = go(fc_now, swap_xc)
    ff_out, rows_in, active, slope = units(False, normed_two, w["fc"], w["fc2"], units_bias[0:1])
    ff_out, rows_in, active, slope, fc_moved, v1 = fence(ff_out, rows_in, active, slope, fc_moved, v1)
    saved.append((hidden, *parts, attended, lse, middle, rows_in, active, slope, w))
    w = dict(v=v1, proj=proj1, fc=(fc_now, fc_moved))
    w["q"], w["k"] = pair_join(pair, got, row)
    hidden = middle + ff_out + small[0, 7]
    cot_moved = cot_regroup()
    *parts, cot_moved, fc2_now = fence(*attend(1, hidden, w), cot_moved, fc2_slice[1])
    normed, query, key, key_other, value, value_other = parts
    fc2_parts = halves(fc2_now)
    fc2_top = go(fc2_parts[0], swap_xc)
    attended, lse = attention(place, slot, query, key, key_other, value, value_other)
    attended, lse, fc2_top = fence(attended, lse, fc2_top)
    fc2_end = go(fc2_parts[1], swap_xc)
    middle, normed_two = project(1, hidden, attended, w)
    w["fc2"] = (fc2_now, fc2_top, fc2_end)
    middle, normed_two, fc2_end = fence(middle, normed_two, fc2_end)
    w["fc2"] = (fc2_now, fc2_top, fc2_end)
    ff_out, rows_in, active, slope = units(False, normed_two, w["fc"], w["fc2"], units_bias[1:2])
    saved.append((hidden, *parts, attended, lse, middle, rows_in, active, slope, w))
    final = bf(middle + ff_out + small[1, 7])

    factor = 1.0 / lax.axis_size("dp")
    results = [None] * LAYERS

    def units_split(value):
        quarters = value.reshape(planes, 2, -1, width)
        kept = lax.dynamic_index_in_dim(quarters, col, 1, keepdims=False)
        return kept, lax.dynamic_index_in_dim(quarters, 1 - col, 1, keepdims=False)

    def halves_of(value):
        halves = value.reshape(2, -1, width)
        kept = lax.dynamic_index_in_dim(halves, col, 0, keepdims=False)
        return kept, lax.dynamic_index_in_dim(halves, 1 - col, 0, keepdims=False)

    def sum_dp(value):
        return lax.psum_scatter(value, AXES, axis_index_groups=along_dp, scatter_dimension=0, tiled=True)

    def mp_pieces(*values):
        def piece(y, x):
            parts = []
            for value in values:
                size = value.shape[1] // 4
                parts.append(lax.dynamic_slice_in_dim(value, (2 * y + x) * size, size, axis=1))
            return jnp.concatenate(parts, axis=1)

        return [
            piece(row, col),
            go(piece(row, 1 - col), over_x),
            go(piece(1 - row, col), over_y),
            go(piece(1 - row, 1 - col), over_xy),
        ]

    def columns_of(values, parts, index):
        cut = []
        for value in values:
            size = value.shape[1] // parts
            cut.append(lax.dynamic_slice_in_dim(value, index * size, size, axis=1))
        return jnp.concatenate(cut, axis=1)

    def total_of(pieces):
        return sum(f32(piece) for piece in pieces[1:]) + f32(pieces[0])

    def mlp_back(layer, out_grad, *held):
        (*_, active, slope, w) = saved[layer]
        return units(True, out_grad, w["fc2"], w["fc"], slope, active)

    def middle_back(layer, grad, da2):
        middle, w = saved[layer][9], saved[layer][-1]
        part, gain, shift = norm_back(da2, middle, small[layer, 1])
        middle_grad = grad + part
        branch = bf(middle_grad)
        return middle_grad, branch, bf(nt(branch, w["proj"])), gain, shift, jnp.sum(f32(branch), axis=0)

    def heads_back(layer, attended_grad):
        hidden, normed, query, key, key_other, value, value_other, attended, lse = saved[layer][:9]
        return attention_back(place, slot, query, key, key_other, value, value_other, attended_grad, attended, lse)

    def input_back(layer, middle_grad, dq, dk, dv):
        hidden, w = saved[layer][0], saved[layer][-1]
        normed_grad = nt(dq, w["q"]) + nt(dk, w["k"]) + nt(dv, w["v"])
        part, gain, shift = norm_back(normed_grad, hidden, small[layer, 0])
        return middle_grad + part, gain, shift

    def mixed_of(dq, dkm, dkt, dvm, dvt):
        dk = bf(dkm + f32(go(dkt, over_c)))[:, :width]
        dv = bf(dvm + f32(go(dvt, over_c)))[:, :width]
        return dq, dk, dv

    def last_sum(parts, away, side):
        return bf(f32(parts[3]) + f32(away) + f32(side))

    def regroup(value):
        value = padded(value)
        return go(value[:local], swap_yc), go(value[local:], turn_far)

    def settle(value, mine, theirs):
        mine, theirs = mine[:, :width], theirs[:, :width]
        mine = jnp.where(row == core, value[:local], mine)
        return f32(jnp.stack([jnp.where(col == 0, mine, theirs), jnp.where(col == 0, theirs, mine)]))

    def bias_sums(gains, shifts, dq, dv, branch_sum, out_grad):
        return jnp.stack(
            [*gains, *shifts, jnp.sum(f32(dq), axis=0), jnp.sum(f32(dv), axis=0), branch_sum, jnp.sum(f32(out_grad), axis=0)]
        )

    def row_parts(left):
        columns = jnp.transpose(left).reshape(planes, 2, -1, left.shape[0])
        keep = lax.dynamic_index_in_dim(columns, core, 1, keepdims=False)
        send = lax.dynamic_index_in_dim(columns, 1 - core, 1, keepdims=False)
        return keep.reshape(-1, left.shape[0]), send.reshape(-1, left.shape[0])

    out_grad = jnp.concatenate([jnp.where(row == core, cot_moved[0], cot_moved[1]), cot_moved[2]], axis=0)
    grad = f32(out_grad)
    final, out_grad = fence(final, out_grad)
    da2, rows_grad, inner_grad, units_sum, fc2_grad = mlp_back(1, out_grad)
    final, da2, inner_grad, units_sum, fc2_grad = fence(final, da2, inner_grad, units_sum, fc2_grad)
    fc2_sum = sum_z(fc2_grad)
    fc_kept, fc_sent = units_split(bf(tn(saved[1][10], inner_grad)))
    fc_kept, fc_top, fc_end, da2 = fence(fc_kept, fc_sent[:planes // 2], fc_sent[planes // 2:], da2)
    fc_away = [go(fc_top, over_x)]
    middle_grad, branch, attended_grad, gain_two, shift_two, attn_out_grad = middle_back(1, grad, da2)
    proj_grad = bf(tn(saved[1][7], branch))
    fc_away[0], fc_end, middle_grad, branch, attended_grad, proj_grad = fence(
        fc_away[0], fc_end, middle_grad, branch, attended_grad, proj_grad
    )
    proj_sum = sum_dp(proj_grad)
    fc_away.append(go(fc_end, over_x))
    final_moved = regroup(final)
    back = fence(*heads_back(1, attended_grad), fc2_sum, fc_away[1], *final_moved)
    fc2_sum, fc_away[1], *final_moved = back[5:]
    dq, dk, dv = mixed_of(*back[:5])
    dq_grad = bf(tn(saved[1][1], back[0]))
    dq, dk, dv, dq_grad = fence(dq, dk, dv, dq_grad)
    dq_sum = sum_dp(dq_grad)
    below, gain_one, shift_one = input_back(1, middle_grad, dq, dk, dv)
    out_grad_low = bf(below)
    sums_one = bias_sums((gain_one, gain_two), (shift_one, shift_two), dq, dv, attn_out_grad, out_grad)
    out_grad_low, below, dq, dk, dv, sums_one = fence(out_grad_low, below, dq, dk, dv, sums_one)
    dkv_grad = bf(tn(saved[1][1], jnp.concatenate([dk, dv], axis=1)))
    fc_joined = add_pair(fc_kept, jnp.concatenate(fc_away, axis=0))
    fc2_kept, fc2_sent = halves_of(fc2_sum)
    out_grad_low, dkv_grad, fc_joined, fc2_sent = fence(out_grad_low, dkv_grad, fc_joined, fc2_sent)
    dkv_sum = sum_dp(dkv_grad)
    fc_sum = sum_z(fc_joined.reshape(-1, width))
    fc2_away = go(fc2_sent, over_x)
    da2, rows_grad, inner_grad, units_low, fc2_grad = mlp_back(0, out_grad_low)
    da2, inner_grad, units_low, fc2_grad, fc2_away, proj_sum, dq_sum = fence(
        da2, inner_grad, units_low, fc2_grad, fc2_away, proj_sum, dq_sum
    )
    fc2_high = add_pair(fc2_kept, fc2_away)
    fc2_kept, fc2_sent = units_split(fc2_grad)
    top = planes // 2
    fc2_kept, fc2_top, fc2_end, da2, fc2_high = fence(fc2_kept, fc2_sent[:top], fc2_sent[top:], da2, fc2_high)
    fc2_away = [go(fc2_top, over_x)]
    fc_kept, fc_sent = units_split(bf(tn(saved[0][10], inner_grad)))
    fc2_away[0], fc2_end, fc_kept, fc_sent, da2 = fence(fc2_away[0], fc2_end, fc_kept, fc_sent, da2)
    fc2_away.append(go(fc2_end, over_x))
    middle_grad, branch, attended_grad, gain_two, shift_two, attn_out_grad = middle_back(0, below, da2)
    proj_grad = bf(tn(saved[0][7], branch))
    fc2_away[1], fc_sent, middle_grad, branch, attended_grad, proj_grad = fence(
        fc2_away[1], fc_sent, middle_grad, branch, attended_grad, proj_grad
    )
    fc_away = go(fc_sent, over_x)
    fc2_low = sum_z(add_pair(fc2_kept, jnp.concatenate(fc2_away, axis=0)).reshape(-1, width))
    back = fence(*heads_back(0, attended_grad), fc_away, dkv_sum, fc_sum, fc2_high, dq_sum, proj_sum)
    fc_away, dkv_sum, fc_sum, fc2_high, dq_sum, proj_sum = back[5:]
    turned = turn_xc(jnp.concatenate([fc_sum, fc2_high], axis=0))
    qkv_sum = jnp.concatenate([dq_sum, dkv_sum], axis=1)
    near_columns, far_columns = [columns_of((qkv_sum, proj_sum), 2, side) for side in (row, 1 - row)]
    far_top, far_end = halves(far_columns)
    far_top = go(far_top, over_y)
    dq, dk, dv = mixed_of(*back[:5])
    dq, dk, dv, proj_grad, turned, near_columns, far_top, far_end = fence(
        dq, dk, dv, proj_grad, turned, near_columns, far_top, far_end
    )
    far_end = go(far_end, over_y)
    proj_low = sum_dp(proj_grad)
    fc_low = sum_z(add_pair(fc_kept, fc_away).reshape(-1, width))
    lowest, gain_one, shift_one = input_back(0, middle_grad, dq, dk, dv)
    lowest, far_end = fence(lowest, far_end)
    far_columns = jnp.concatenate([far_top, far_end], axis=0)
    sums_zero = bias_sums((gain_one, gain_two), (shift_one, shift_two), dq, dv, attn_out_grad, out_grad_low)
    low = bf(lowest)
    third = 3 * width // 4
    mixed = jnp.concatenate([dq, dk, dv], axis=1)
    pieces = jnp.stack([mixed[:, i * third:(i + 1) * third] for i in range(4)])
    keep, send = row_parts(saved[0][1])
    spread = (jnp.arange(4) == 2 * row + core).astype(jnp.float32)
    sums = jnp.concatenate(
        [
            sums_zero,
            sums_one,
            (spread[None, :, None] * jnp.concatenate([units_low, units_sum], axis=0)[:, None, :]).reshape(2 * 4, width),
        ]
    )
    held_rows = proj_sum.shape[0]
    split = 3 * width // 2
    columns = add_pair(near_columns, far_columns)
    halves_x = columns[:, :split], columns[:, split:]
    near_columns, far_columns = [columns_of(halves_x, 2, side) for side in (col, 1 - col)]
    low, sums, pieces, keep, send, fc2_low, near_columns, far_columns = fence(
        low, sums, pieces, keep, send, fc2_low, near_columns, far_columns
    )
    fc2_low = turn_xc(fc2_low)
    low_moved = regroup(low)
    far_columns = go(far_columns, over_x)
    qkv_low, sums = settle_columns(planes, keep, send, pieces, sums)
    qkv_low, sums, fc_low, proj_low, fc2_low, far_columns, low_moved = fence(
        qkv_low, sums, fc_low, proj_low, fc2_low, far_columns, low_moved
    )
    columns = f32(near_columns) + f32(far_columns)
    qkv_high = columns[:, :third]
    results_zero = [turn_xc(fc_low), fc2_low, total_of(mp_pieces(proj_low))]
    results_one = [turned[:held_rows], turned[held_rows:], columns[:, third:]]
    outputs = settle(final, *final_moved)
    input_grad = settle(low, *low_moved)
    held = width // (2 * planes)
    sums = lax.dynamic_slice_in_dim(sums, dp_rank * held, held, axis=1) * factor
    unit_rows = lax.dynamic_index_in_dim(sums[16:].reshape(2, 4, held), mp_rank, 1, keepdims=False)
    sums = sums[:16].reshape(2, 8, held)
    qkv_high = qkv_high * factor
    results = [results_zero, results_one]
    return (
        outputs,
        input_grad,
        jnp.stack([qkv_low, qkv_high]),
        jnp.stack([f32(entry[2]) for entry in results]) * factor,
        jnp.stack([f32(entry[0]) for entry in results]) * factor,
        jnp.stack([f32(entry[1]).T for entry in results]) * factor,
        unit_rows,
        sums[:, 0:2],
        sums[:, 2:4],
        sums[:, 4:6],
        sums[:, 6:8],
    )


def solution(mesh):
    planes = mesh.shape["dp"] // 2
    if mesh.shape["mp"] == 4:
        body = functools.partial(quick_body, planes)
    else:
        body = general_body
    return jax.shard_map(
        body,
        mesh=mesh,
        in_specs=(
            P("dp", "mp", None),
            P("dp", "mp", None),
            P(),
            P(None, "dp", None),
            P(None, "dp", None),
            P(None, "dp", "mp"),
            P(None, "mp", "dp"),
            P(None, ("mp", "dp")),
            P(None, None, "dp"),
            P(None, None, "dp"),
            P(None, None, "dp"),
            P(None, None, "dp"),
        ),
        out_specs=(
            P("dp", "mp", None),
            P("dp", "mp", None),
            P(None, "dp", "mp"),
            P(None, "dp", "mp"),
            P(None, "dp", "mp"),
            P(None, "mp", "dp"),
            P(None, ("mp", "dp")),
            P(None, None, "dp"),
            P(None, None, "dp"),
            P(None, None, "dp"),
            P(None, None, "dp"),
        ),
        check_vma=False,
    )
```

```python
import functools

import jax
import jax.numpy as jnp
from jax import lax
from jax.experimental import pallas as pl
from jax.experimental.pallas import tpu as pltpu
from jax.sharding import PartitionSpec as P

HD = 64
LAYERS = 2


eps = 1e-05


def layer_norm(value, gain, shift):
    mean = jnp.mean(value, axis=-1, keepdims=True)
    centred = value - mean
    spread = jnp.mean(centred * centred, axis=-1, keepdims=True)
    return centred * lax.rsqrt(spread + eps) * gain + shift


def fetch_params(weights, layer):
    pieces = tuple((w[layer] for w in weights))
    return (
        lax.all_gather(pieces[0], "dp", axis=0, tiled=True),
        lax.all_gather(pieces[1], "dp", axis=0, tiled=True),
        lax.all_gather(pieces[2], "dp", axis=0, tiled=True),
        lax.all_gather(pieces[3], "dp", axis=1, tiled=True),
        lax.all_gather(pieces[4], "dp", axis=0, tiled=True),
        lax.all_gather(pieces[5], "dp", axis=1, tiled=True),
        lax.all_gather(pieces[6], "dp", axis=1, tiled=True),
        lax.all_gather(pieces[7], "dp", axis=1, tiled=True),
        lax.all_gather(pieces[8], "dp", axis=1, tiled=True),
    )


def fetch_again(weights, layer):
    pieces = tuple((w[layer] for w in weights))
    return (
        lax.all_gather(pieces[0], "dp", axis=0, tiled=True),
        lax.all_gather(pieces[1], "dp", axis=0, tiled=True),
        lax.all_gather(pieces[2], "dp", axis=0, tiled=True),
        lax.all_gather(pieces[3], "dp", axis=1, tiled=True),
        lax.all_gather(pieces[4], "dp", axis=0, tiled=True),
        lax.all_gather(pieces[5], "dp", axis=1, tiled=True),
        lax.all_gather(pieces[6], "dp", axis=1, tiled=True),
        lax.all_gather(pieces[7], "dp", axis=1, tiled=True),
        lax.all_gather(pieces[8], "dp", axis=1, tiled=True),
    )


def scores_of(query_heads, key_heads, visible, scale):
    scores = (
        jnp.einsum("qhd,khd->hqk", query_heads, key_heads, preferred_element_type=jnp.float32)
        * scale
    )
    return jnp.where(visible, scores, -1e30)


def general_body(
    tokens,
    cotangent,
    block_order,
    qkv_weight,
    proj_weight,
    fc_weight,
    fc2_weight,
    fc_bias,
    norm_gain,
    norm_shift,
    attn_bias,
    out_bias,
):
    weights = (
        qkv_weight,
        proj_weight,
        fc_weight,
        fc2_weight,
        fc_bias,
        norm_gain,
        norm_shift,
        attn_bias,
        out_bias,
    )
    seqs, local, width = tokens.shape
    heads = width // HD
    scale = HD ** (-0.5)
    model_size = lax.axis_size("mp")
    data_size = lax.axis_size("dp")
    length = local * model_size
    half = local // 2
    rank = lax.axis_index("mp")
    owned = lax.dynamic_slice_in_dim(block_order, 2 * rank, 2)
    offsets = jnp.arange(local, dtype=jnp.int32)
    query_place = jnp.where(offsets < half, owned[0], owned[1]) * half + offsets % half
    every = jnp.arange(length, dtype=jnp.int32)
    key_place = jnp.repeat(block_order, half) * half + every % half
    visible = key_place[None, :] <= query_place[:, None]
    count = seqs * local

    def attend_one(pack):
        query_heads, key_heads, value_heads = pack
        scores = scores_of(query_heads, key_heads, visible, scale)
        top = jnp.max(scores, axis=-1, keepdims=True)
        expo = jnp.exp(scores - top)
        total = jnp.sum(expo, axis=-1, keepdims=True)
        probs = (expo / total).astype(jnp.bfloat16)
        logsum = top + jnp.log(total)
        attended = jnp.einsum(
            "hqk,khd->qhd", probs, value_heads, preferred_element_type=jnp.float32
        )
        return (attended.reshape(local, width).astype(jnp.bfloat16), logsum)

    def attend_back(pack):
        query_heads, key_heads, value_heads, grad_heads, logsum = pack
        scores = scores_of(query_heads, key_heads, visible, scale)
        probs = jnp.exp(scores - logsum)
        prob_grad = jnp.einsum(
            "qhd,khd->hqk", grad_heads, value_heads, preferred_element_type=jnp.float32
        )
        value_grad = jnp.einsum(
            "hqk,qhd->khd",
            probs.astype(jnp.bfloat16),
            grad_heads,
            preferred_element_type=jnp.float32,
        )
        score_grad = (
            probs * (prob_grad - jnp.sum(probs * prob_grad, axis=-1, keepdims=True))
        ).astype(jnp.bfloat16)
        query_grad = (
            jnp.einsum("hqk,khd->qhd", score_grad, key_heads, preferred_element_type=jnp.float32)
            * scale
        )
        key_grad = (
            jnp.einsum("hqk,qhd->khd", score_grad, query_heads, preferred_element_type=jnp.float32)
            * scale
        )
        return (
            query_grad.reshape(local, width),
            key_grad.reshape(length, width),
            value_grad.reshape(length, width),
        )

    hidden = tokens.reshape(count, width).astype(jnp.float32)
    saved = []
    for layer in range(LAYERS):
        params = fetch_params(weights, layer)
        qkv_full, proj_full, fc_full, fc2_full, fc_b = (
            params[0],
            params[1],
            params[2],
            params[3],
            params[4],
        )
        gains = params[5].astype(jnp.float32)
        shifts = params[6].astype(jnp.float32)
        bias_in = params[7].astype(jnp.float32)
        bias_out = params[8].astype(jnp.float32)
        normed = layer_norm(hidden, gains[0], shifts[0]).astype(jnp.bfloat16)
        mixed = jnp.dot(normed, qkv_full, preferred_element_type=jnp.float32)
        query = (mixed[:, :width] + bias_in[0]).astype(jnp.bfloat16)
        key = mixed[:, width : 2 * width].astype(jnp.bfloat16)
        value = (mixed[:, 2 * width :] + bias_in[1]).astype(jnp.bfloat16)
        keys, values = (
            lax.all_gather(key.reshape(seqs, local, width), "mp", axis=1, tiled=True),
            lax.all_gather(value.reshape(seqs, local, width), "mp", axis=1, tiled=True),
        )
        query_heads = query.reshape(seqs, local, heads, HD)
        key_heads = keys.reshape(seqs, length, heads, HD)
        value_heads = values.reshape(seqs, length, heads, HD)
        attended, logsum = lax.map(attend_one, (query_heads, key_heads, value_heads))
        attended = attended.reshape(count, width)
        middle = (
            hidden + jnp.dot(attended, proj_full, preferred_element_type=jnp.float32) + bias_out[0]
        )
        normed_two = layer_norm(middle, gains[1], shifts[1]).astype(jnp.bfloat16)
        group_rows = lax.all_gather(normed_two, "mp", axis=0, tiled=True)
        inner = jnp.dot(group_rows, fc_full, preferred_element_type=jnp.float32) + fc_b.astype(
            jnp.float32
        )
        active = jax.nn.gelu(inner, approximate=True).astype(jnp.bfloat16)

        def down_rows(start, rows, active=active, fc2_full=fc2_full):
            return jnp.dot(active, fc2_full, preferred_element_type=jnp.float32)

        reduced = lax.psum_scatter(
            down_rows(jnp.int32(0), lax.axis_size("mp") * count).astype(jnp.bfloat16),
            "mp",
            scatter_dimension=0,
            tiled=True,
        ).astype(jnp.float32)
        output = middle + reduced + bias_out[1]
        kept_params = None
        kept_pairs = None
        saved.append(
            (
                hidden,
                normed,
                query,
                key,
                value,
                logsum,
                attended,
                middle,
                group_rows,
                inner,
                kept_params,
                kept_pairs,
            )
        )
        hidden = output
    outputs = hidden.reshape(seqs, local, width)
    grad = cotangent.reshape(count, width).astype(jnp.float32)
    collected = []
    for layer in reversed(range(LAYERS)):
        (
            hidden_in,
            normed,
            query,
            key,
            value,
            logsum,
            attended,
            middle,
            group_rows,
            inner,
            kept_params,
            kept_pairs,
        ) = saved[layer]
        params = fetch_again(weights, layer)
        keys, values = (
            lax.all_gather(key.reshape(seqs, local, width), "mp", axis=1, tiled=True),
            lax.all_gather(value.reshape(seqs, local, width), "mp", axis=1, tiled=True),
        )
        qkv_full, proj_full, fc_full, fc2_full = (params[0], params[1], params[2], params[3])
        gains = params[5].astype(jnp.float32)
        shifts = params[6].astype(jnp.float32)
        out_grad = grad.astype(jnp.bfloat16)
        mlp_bias_grad = jnp.sum(out_grad.astype(jnp.float32), axis=0)
        group_grad = lax.all_gather(out_grad, "mp", axis=0, tiled=True)
        active = jax.nn.gelu(inner, approximate=True).astype(jnp.bfloat16)
        fc2_grad = jnp.einsum("nf,nd->fd", active, group_grad, preferred_element_type=jnp.float32)
        active_grad = jnp.einsum(
            "nd,fd->nf", group_grad, fc2_full, preferred_element_type=jnp.float32
        )
        _, gelu_back = jax.vjp(lambda v: jax.nn.gelu(v, approximate=True), inner)
        inner_grad = gelu_back(active_grad)[0].astype(jnp.bfloat16)
        fc_bias_grad = jnp.sum(inner_grad.astype(jnp.float32), axis=0)
        fc_grad = jnp.einsum(
            "nd,nf->df", group_rows, inner_grad, preferred_element_type=jnp.float32
        )

        def back_rows(start, rows, inner_grad=inner_grad, fc_full=fc_full):
            return jnp.einsum("nf,df->nd", inner_grad, fc_full, preferred_element_type=jnp.float32)

        normed_two_grad = lax.psum_scatter(
            back_rows(jnp.int32(0), lax.axis_size("mp") * count).astype(jnp.bfloat16),
            "mp",
            scatter_dimension=0,
            tiled=True,
        ).astype(jnp.float32)
        _, norm_two_back = jax.vjp(layer_norm, middle, gains[1], shifts[1])
        middle_part, gain_two, shift_two = norm_two_back(normed_two_grad)
        middle_grad = grad + middle_part
        branch_grad = middle_grad.astype(jnp.bfloat16)
        attn_out_bias_grad = jnp.sum(branch_grad.astype(jnp.float32), axis=0)
        proj_grad = jnp.einsum(
            "nd,ne->de", attended, branch_grad, preferred_element_type=jnp.float32
        )
        attended_grad = jnp.einsum(
            "ne,de->nd", branch_grad, proj_full, preferred_element_type=jnp.float32
        ).astype(jnp.bfloat16)
        grad_heads = attended_grad.reshape(seqs, local, heads, HD)
        query_heads = query.reshape(seqs, local, heads, HD)
        key_heads = keys.reshape(seqs, length, heads, HD)
        value_heads = values.reshape(seqs, length, heads, HD)
        query_grad, key_grad, value_grad = lax.map(
            attend_back, (query_heads, key_heads, value_heads, grad_heads, logsum)
        )
        key_part, value_part = (
            lax.psum_scatter(
                key_grad.astype(jnp.bfloat16), "mp", scatter_dimension=1, tiled=True
            ).astype(jnp.float32),
            lax.psum_scatter(
                value_grad.astype(jnp.bfloat16), "mp", scatter_dimension=1, tiled=True
            ).astype(jnp.float32),
        )
        query_round = query_grad.reshape(count, width).astype(jnp.bfloat16)
        key_round = key_part.reshape(count, width).astype(jnp.bfloat16)
        value_round = value_part.reshape(count, width).astype(jnp.bfloat16)
        mixed_grad = jnp.concatenate([query_round, key_round, value_round], axis=1)
        bias_in_grad = jnp.stack(
            [
                jnp.sum(query_round.astype(jnp.float32), axis=0),
                jnp.sum(value_round.astype(jnp.float32), axis=0),
            ]
        )
        qkv_grad = jnp.einsum("nd,ne->de", normed, mixed_grad, preferred_element_type=jnp.float32)
        normed_grad = jnp.einsum(
            "ne,de->nd", mixed_grad, qkv_full, preferred_element_type=jnp.float32
        )
        _, norm_one_back = jax.vjp(layer_norm, hidden_in, gains[0], shifts[0])
        hidden_part, gain_one, shift_one = norm_one_back(normed_grad)
        grad = middle_grad + hidden_part
        gain_grad = jnp.stack([gain_one, gain_two])
        shift_grad = jnp.stack([shift_one, shift_two])
        bias_out_grad = jnp.stack([attn_out_bias_grad, mlp_bias_grad])
        shards = (
            lax.psum_scatter(
                qkv_grad.astype(jnp.bfloat16), "dp", scatter_dimension=0, tiled=True
            ).astype(jnp.float32),
            lax.psum_scatter(
                proj_grad.astype(jnp.bfloat16), "dp", scatter_dimension=0, tiled=True
            ).astype(jnp.float32),
            lax.psum_scatter(
                fc_grad.astype(jnp.bfloat16), "dp", scatter_dimension=0, tiled=True
            ).astype(jnp.float32),
            lax.psum_scatter(
                fc2_grad.astype(jnp.bfloat16), "dp", scatter_dimension=1, tiled=True
            ).astype(jnp.float32),
            lax.psum_scatter(
                fc_bias_grad.astype(jnp.bfloat16), "dp", scatter_dimension=0, tiled=True
            ).astype(jnp.float32),
            lax.psum_scatter(
                gain_grad.astype(jnp.bfloat16), "dp", scatter_dimension=1, tiled=True
            ).astype(jnp.float32),
            lax.psum_scatter(
                shift_grad.astype(jnp.bfloat16), "dp", scatter_dimension=1, tiled=True
            ).astype(jnp.float32),
            lax.psum_scatter(
                bias_in_grad.astype(jnp.bfloat16), "dp", scatter_dimension=1, tiled=True
            ).astype(jnp.float32),
            lax.psum_scatter(
                bias_out_grad.astype(jnp.bfloat16), "dp", scatter_dimension=1, tiled=True
            ).astype(jnp.float32),
        )
        projections = (
            lax.psum_scatter(
                shards[0].astype(jnp.bfloat16), "mp", scatter_dimension=1, tiled=True
            ).astype(jnp.float32),
            lax.psum_scatter(
                shards[1].astype(jnp.bfloat16), "mp", scatter_dimension=1, tiled=True
            ).astype(jnp.float32),
        )
        smaller = lax.psum((shards[5], shards[6], shards[7], shards[8]), "mp")
        factor = 1.0 / data_size
        collected.append(
            (
                projections[0] * factor,
                projections[1] * factor,
                shards[2] * factor,
                shards[3] * factor,
                shards[4] * factor,
                smaller[0] * factor,
                smaller[1] * factor,
                smaller[2] * factor,
                smaller[3] * factor,
            )
        )
    collected = collected[::-1]
    stacked = tuple((jnp.stack([entry[index] for entry in collected]) for index in range(9)))
    input_grad = grad.reshape(seqs, local, width)
    return (
        outputs,
        input_grad,
        stacked[0],
        stacked[1],
        stacked[2],
        stacked[3],
        stacked[4],
        stacked[5],
        stacked[6],
        stacked[7],
        stacked[8],
    )


def grid_index(mesh):
    shape = dict(mesh.shape)
    return shape["dp"] // 2, shape["mp"]


def spots(planes):
    return [(z, c, y, x) for z in range(planes) for c in range(2) for y in range(2) for x in range(2)]


def flat(z, c, y, x):
    return (z * 2 + c) * 4 + y * 2 + x


def pairs_of(planes, move):
    both = [(flat(*spot), flat(*move(*spot))) for spot in spots(planes)]
    return [pair for pair in both if pair[0] != pair[1]]


AXES = ("dp", "mp")
LANES = 128


def nt(a, b):
    return lax.dot_general(a, b, (((1,), (1,)), ((), ())), preferred_element_type=jnp.float32)


def tn(a, b):
    return lax.dot_general(a, b, (((0,), (0,)), ((), ())), preferred_element_type=jnp.float32)


def nn(a, b):
    return jnp.dot(a, b, preferred_element_type=jnp.float32)


def sort_keys(slot_ref, blocks, ok, own_ref, other_ref, cat, put):
    half = blocks * LANES // 2
    cat[:half] = jnp.where(ok, own_ref[...], 0)
    cat[half:] = jnp.where(ok, other_ref[...], 0)
    for j in range(blocks):
        start = pl.multiple_of(slot_ref[j] * LANES, LANES)
        put(j, cat[pl.ds(start, LANES), :])


def two_heads(rows, first):
    zero = jnp.zeros_like(rows)
    return jnp.concatenate([jnp.where(first, rows, zero), jnp.where(first, zero, rows)], axis=0)


def attend_kernel(width, blocks, qblocks, place_ref, slot_ref, q_ref, ko_ref, ks_ref, vo_ref, vs_ref,
                  o_ref, lse_ref, cat, ksort, vsort):
    lane = lax.broadcasted_iota(jnp.int32, (1, LANES), 1)
    ok = lane + pl.program_id(0) * LANES < width
    first = lane < HD

    def put_k(j, rows):
        ksort[j * LANES:(j + 1) * LANES, :] = rows

    def put_v(j, rows):
        vsort[j * LANES:(j + 1) * LANES, :] = rows

    sort_keys(slot_ref, blocks, ok, ko_ref, ks_ref, cat, put_k)
    sort_keys(slot_ref, blocks, ok, vo_ref, vs_ref, cat, put_v)

    def one(b, carry):
        place = place_ref[b]
        here = pl.ds(pl.multiple_of(b * LANES, LANES), LANES)
        rows = (jnp.where(ok, q_ref[here, :], 0) * (HD ** -0.5)).astype(jnp.bfloat16)
        q2 = two_heads(rows, first)
        for n in range(1, blocks // 2 + 1):
            @pl.when(place // 2 == n - 1)
            def _(n=n):
                keys = 2 * LANES * n
                s = nt(ksort[:keys, :], q2)
                row = lax.broadcasted_iota(jnp.int32, (2 * LANES, 2 * LANES), 0) + (keys - 2 * LANES)
                col = lax.broadcasted_iota(jnp.int32, (2 * LANES, 2 * LANES), 1) % LANES + place * LANES
                tail = jnp.where(row <= col, s[keys - 2 * LANES:], -1e30)
                s = tail if n == 1 else jnp.concatenate([s[:keys - 2 * LANES], tail], axis=0)
                top = jnp.max(s, axis=0, keepdims=True)
                e = jnp.exp(s - top)
                total = jnp.sum(e, axis=0, keepdims=True)
                turned = tn(vsort[:keys, :], e.astype(jnp.bfloat16)) / total
                joined = jnp.concatenate([turned[:HD, :LANES], turned[HD:, LANES:]], axis=0)
                o_ref[here, :] = joined.T.astype(jnp.bfloat16)
                lse = top + jnp.log(total)
                lse_ref[0, 0:1, here] = lse[:, :LANES]
                lse_ref[0, 1:2, here] = lse[:, LANES:]
        return carry

    lax.fori_loop(0, qblocks, one, 0)


def attend_back_kernel(width, blocks, qblocks, place_ref, slot_ref, q_ref, ko_ref, ks_ref, vo_ref, vs_ref,
                       do_ref, o_ref, lse_ref, dq_ref, dko_ref, dks_ref, dvo_ref, dvs_ref,
                       cat, ksort, kturn, vsort, dk, dv, loose):
    lane = lax.broadcasted_iota(jnp.int32, (1, LANES), 1)
    ok = lane + pl.program_id(0) * LANES < width
    first = lane < HD

    def put_k(j, rows):
        ksort[j * LANES:(j + 1) * LANES, :] = rows
        kturn[:, j * LANES:(j + 1) * LANES] = rows.astype(jnp.float32).T.astype(jnp.bfloat16)

    def put_v(j, rows):
        vsort[j * LANES:(j + 1) * LANES, :] = rows

    sort_keys(slot_ref, blocks, ok, ko_ref, ks_ref, cat, put_k)
    sort_keys(slot_ref, blocks, ok, vo_ref, vs_ref, cat, put_v)
    dk[...] = jnp.zeros_like(dk)
    dv[...] = jnp.zeros_like(dv)

    def one(b, carry):
        place = place_ref[b]
        here = pl.ds(pl.multiple_of(b * LANES, LANES), LANES)
        rows = (jnp.where(ok, q_ref[here, :], 0) * (HD ** -0.5)).astype(jnp.bfloat16)
        q2 = two_heads(rows, first)
        do = jnp.where(ok, do_ref[here, :], 0)
        do2 = two_heads(do, first)
        both = (do.astype(jnp.float32) * jnp.where(ok, o_ref[here, :], 0).astype(jnp.float32)).T
        delta = jnp.concatenate(
            [jnp.sum(both[:HD], axis=0, keepdims=True), jnp.sum(both[HD:], axis=0, keepdims=True)], axis=1
        )
        lse = jnp.concatenate([lse_ref[0, 0:1, here], lse_ref[0, 1:2, here]], axis=1)
        for n in range(1, blocks // 2 + 1):
            @pl.when(place // 2 == n - 1)
            def _(n=n):
                keys = 2 * LANES * n
                s = nt(ksort[:keys, :], q2)
                row = lax.broadcasted_iota(jnp.int32, (2 * LANES, 2 * LANES), 0) + (keys - 2 * LANES)
                col = lax.broadcasted_iota(jnp.int32, (2 * LANES, 2 * LANES), 1) % LANES + place * LANES
                tail = jnp.where(row <= col, s[keys - 2 * LANES:], -1e30)
                s = tail if n == 1 else jnp.concatenate([s[:keys - 2 * LANES], tail], axis=0)
                p = jnp.exp(s - lse)
                dp = nt(vsort[:keys, :], do2)
                ds = (p * (dp - delta)).astype(jnp.bfloat16)
                dv[:keys, :] += nn(p.astype(jnp.bfloat16), do2)
                dk[:keys, :] += nn(ds, q2)
                turned = nn(kturn[:, :keys], ds) * (HD ** -0.5)
                joined = jnp.concatenate([turned[:HD, :LANES], turned[HD:, LANES:]], axis=0)
                dq_ref[here, :] = joined.T.astype(jnp.bfloat16)
        return carry

    lax.fori_loop(0, qblocks, one, 0)
    half = blocks * LANES // 2
    for source, mine, theirs in ((dk, dko_ref, dks_ref), (dv, dvo_ref, dvs_ref)):
        for j in range(blocks):
            start = pl.multiple_of(slot_ref[j] * LANES, LANES)
            loose[pl.ds(start, LANES), :] = source[j * LANES:(j + 1) * LANES, :]
        mine[...] = loose[:half]
        theirs[...] = loose[half:].astype(jnp.bfloat16)


def attention_specs(rows):
    tall = pl.BlockSpec((rows, LANES), lambda i, *_: (0, i))
    stat = pl.BlockSpec((1, 2, rows), lambda i, *_: (i, 0, 0))
    return tall, stat


def attention(place, slot, q, ko, ks, vo, vs):
    rows, width = q.shape
    steps = -(-width // LANES)
    blocks, keys = slot.shape[0], slot.shape[0] * LANES
    tall, stat = attention_specs(rows)
    elems = rows * keys * steps * 2
    return pl.pallas_call(
        functools.partial(attend_kernel, width, blocks, place.shape[0]),
        grid_spec=pltpu.PrefetchScalarGridSpec(
            num_scalar_prefetch=2,
            grid=(steps,),
            in_specs=[tall] * 5,
            out_specs=[tall, stat],
            scratch_shapes=[
                pltpu.VMEM((keys, LANES), jnp.bfloat16),
                pltpu.VMEM((keys, LANES), jnp.bfloat16),
                pltpu.VMEM((keys, LANES), jnp.bfloat16),
            ],
        ),
        out_shape=[
            jax.ShapeDtypeStruct((rows, width), jnp.bfloat16),
            jax.ShapeDtypeStruct((steps, 2, rows), jnp.float32),
        ],
        cost_estimate=pl.CostEstimate(flops=elems * HD * 8, bytes_accessed=rows * width * 12, transcendentals=elems),
        compiler_params=pltpu.CompilerParams(vmem_limit_bytes=40 * 2 ** 20),
        name="attention",
    )(place, slot, q, ko, ks, vo, vs)


def attention_back(place, slot, q, ko, ks, vo, vs, do, o, lse):
    rows, width = q.shape
    steps = -(-width // LANES)
    blocks, keys = slot.shape[0], slot.shape[0] * LANES
    tall, stat = attention_specs(rows)
    elems = rows * keys * steps * 2
    wide = jax.ShapeDtypeStruct((rows, steps * LANES), jnp.float32)
    thin = jax.ShapeDtypeStruct((rows, steps * LANES), jnp.bfloat16)
    narrow = jax.ShapeDtypeStruct((rows, width), jnp.bfloat16)
    return pl.pallas_call(
        functools.partial(attend_back_kernel, width, blocks, place.shape[0]),
        grid_spec=pltpu.PrefetchScalarGridSpec(
            num_scalar_prefetch=2,
            grid=(steps,),
            in_specs=[tall] * 7 + [stat],
            out_specs=[tall] * 5,
            scratch_shapes=[
                pltpu.VMEM((keys, LANES), jnp.bfloat16),
                pltpu.VMEM((keys, LANES), jnp.bfloat16),
                pltpu.VMEM((LANES, keys), jnp.bfloat16),
                pltpu.VMEM((keys, LANES), jnp.bfloat16),
                pltpu.VMEM((keys, LANES), jnp.float32),
                pltpu.VMEM((keys, LANES), jnp.float32),
                pltpu.VMEM((keys, LANES), jnp.float32),
            ],
        ),
        out_shape=[narrow, wide, thin, wide, thin],
        cost_estimate=pl.CostEstimate(flops=elems * HD * 20, bytes_accessed=rows * width * 30, transcendentals=elems),
        compiler_params=pltpu.CompilerParams(vmem_limit_bytes=40 * 2 ** 20),
        name="attention_back",
    )(place, slot, q, ko, ks, vo, vs, do, o, lse)


def gather_kernel(planes, piece_ref, small_ref, token_ref, out_ref, small_out, token_out,
                  send_sem, recv_sem, small_send, small_recv, swap_send, swap_recv, own_sem):
    dp, mp = lax.axis_index("dp"), lax.axis_index("mp")
    z, c = dp // 2, dp % 2
    y, x = mp // 2, mp % 2
    side = mp + 1 - 2 * x
    across = mp + 2 - 4 * y
    corner = 3 - mp
    to_x, to_y, to_c = (dp, side), (dp, across), (dp + 1 - 2 * c, mp)
    to_z = [(lax.rem(z + k, planes) * 2 + c, mp) for k in range(1, planes)]
    same, turned = (z * 2 + y, c * 2 + x), (z * 2 + y, c * 2 + 1 - x)
    barrier = pltpu.get_barrier_semaphore()
    for peer in (to_x, to_y, to_c, *to_z, turned):
        pl.semaphore_signal(barrier, inc=1, device_id=peer, device_id_type=pl.DeviceIdType.MESH)

    @pl.when(y != c)
    def _():
        pl.semaphore_signal(barrier, inc=1, device_id=same, device_id_type=pl.DeviceIdType.MESH)

    pl.semaphore_wait(barrier, 4 + len(to_z) + (y - c) * (y - c))

    locals_ = [
        pltpu.make_async_copy(piece_ref, out_ref.at[mp, dp], own_sem.at[0]),
        pltpu.make_async_copy(small_ref, small_out.at[dp], own_sem.at[1]),
    ]
    for copy in locals_:
        copy.start()
    sent = []

    def remote(source, target, sems, peer):
        copy = pltpu.make_async_remote_copy(
            src_ref=source,
            dst_ref=target,
            send_sem=sems[0],
            recv_sem=sems[1],
            device_id=peer,
            device_id_type=pl.DeviceIdType.MESH,
        )
        copy.start()
        return copy

    def send(source, index, row, peer):
        sent.append(remote(source, out_ref.at[index, row], (send_sem.at[len(sent)], recv_sem.at[index, row]), peer))

    def arrived(index, row):
        pltpu.make_async_copy(out_ref.at[index, row], out_ref.at[index, row], recv_sem.at[index, row]).wait()
        return out_ref.at[index, row]

    def swap(source, target, which):
        moved = remote(source.at[1 - x], target.at[1], (swap_send.at[which, 1], swap_recv.at[which, 1]), turned)
        kept = pltpu.make_async_copy(source.at[x], target.at[0], own_sem.at[2 + which])
        pair = (source.at[x], target.at[0], (swap_send.at[which, 0], swap_recv.at[which, 0]), same)

        @pl.when(y == c)
        def _():
            kept.start()

        @pl.when(y != c)
        def _():
            remote(*pair)

        def finish():
            moved.wait()

            @pl.when(y == c)
            def _():
                kept.wait()

            @pl.when(y != c)
            def _():
                pltpu.make_async_remote_copy(
                    src_ref=pair[0],
                    dst_ref=pair[1],
                    send_sem=pair[2][0],
                    recv_sem=pair[2][1],
                    device_id=same,
                    device_id_type=pl.DeviceIdType.MESH,
                ).wait()

        return finish

    rows = [lax.rem(z - k + planes, planes) * 2 + c for k in range(planes)]
    little = []

    def send_small(source, row, peer):
        little.append(
            remote(source, small_out.at[row], (small_send.at[len(little)], small_recv.at[row]), peer)
        )

    def small_arrived(row):
        pltpu.make_async_copy(small_out.at[row], small_out.at[row], small_recv.at[row]).wait()
        return small_out.at[row]

    for peer in (*to_z, to_c):
        send_small(small_ref, dp, peer)
    for peer in to_z:
        send(piece_ref, mp, dp, peer)
    for peer in (to_x, to_y, to_c):
        send(piece_ref, mp, dp, peer)
    finishes = [swap(token_ref, token_out, 0)]
    for k in range(planes):
        if k > 0:
            send_small(small_arrived(rows[k]), rows[k], to_c)
            block = arrived(mp, rows[k])
            for peer in (to_x, to_y, to_c):
                send(block, mp, rows[k], peer)
            send(arrived(corner, rows[k - 1]), corner, rows[k - 1], to_c)
        block = arrived(side, rows[k])
        if k % 2 == 0:
            send(block, side, rows[k], to_y)
        send(block, side, rows[k], to_c)
        block = arrived(across, rows[k])
        if k % 2 == 1:
            send(block, across, rows[k], to_x)
        send(block, across, rows[k], to_c)
    send(arrived(corner, rows[-1]), corner, rows[-1], to_c)
    for k in range(planes):
        beside = rows[k] + 1 - 2 * c
        small_arrived(beside)
        for index in (mp, side, across, corner):
            arrived(index, beside)
    for copy in sent + little:
        copy.wait_send()
    for finish in finishes:
        finish()
    for copy in locals_:
        copy.wait()


def gather_four(planes, piece, small, tokens):
    count = (planes - 1) + 3 * planes + planes + 3 * planes
    anywhere = pl.BlockSpec(memory_space=pl.ANY)
    return pl.pallas_call(
        functools.partial(gather_kernel, planes),
        in_specs=[anywhere] * 3,
        out_specs=[anywhere] * 3,
        out_shape=[
            jax.ShapeDtypeStruct((4, 2 * planes) + piece.shape, piece.dtype),
            jax.ShapeDtypeStruct((2 * planes,) + small.shape, small.dtype),
            jax.ShapeDtypeStruct(tokens.shape, tokens.dtype),
        ],
        scratch_shapes=[
            pltpu.SemaphoreType.DMA((count,)),
            pltpu.SemaphoreType.DMA((4, 2 * planes)),
            pltpu.SemaphoreType.DMA((2 * planes,)),
            pltpu.SemaphoreType.DMA((2 * planes,)),
            pltpu.SemaphoreType.DMA((2, 2)),
            pltpu.SemaphoreType.DMA((2, 2)),
            pltpu.SemaphoreType.DMA((4,)),
        ],
        cost_estimate=pl.CostEstimate(flops=0, bytes_accessed=300 * 2 ** 20, transcendentals=0),
        compiler_params=pltpu.CompilerParams(collective_id=0, has_side_effects=True),
        name="gather_four",
    )(piece, small, tokens)


GROUPS, PARTS = 4, 2


def tiles(width, body):
    whole = width // 256

    def step(j, carry):
        body(pl.multiple_of(j * 256, 256), 256)
        return carry

    lax.fori_loop(0, whole, step, 0)
    if width % 256:
        body(whole * 256, width % 256)


def units_kernel(back, counts, *refs):
    x_ref, wa_own, wb_own, *refs = refs
    (*wa_moved,), refs = refs[:counts[0]], refs[counts[0]:]
    (*wb_moved,), refs = refs[:counts[1]], refs[counts[1]:]
    if back:
        (slope_ref, act_ref, out_ref, rows_ref, left_ref, sums_ref, grad_ref, act, grad, *scratch) = refs
    else:
        (bias_ref, out_ref, rows_ref, left_ref, slope_ref, *scratch) = refs
    (wa, wb, rows, own, far, beside, corner, got_c, got_f, give, got_y, left, slope,
     in_sem, send_sem, recv_sem, out_sem) = scratch
    width = wa.shape[1]
    part = rows.shape[2]
    dp, mp = lax.axis_index("dp"), lax.axis_index("mp")
    to_c = (dp + 1 - 2 * (dp % 2), mp)
    to_y = (dp, mp + 2 - 4 * (mp // 2))
    loads = [
        pltpu.make_async_copy(x_ref.at[pl.ds(h * part, part)], rows.at[0, h], in_sem.at[h]) for h in range(PARTS)
    ]
    moved = []
    for slot, (own_ref, moved_refs, target) in enumerate(((wa_own, wa_moved, wa), (wb_own, wb_moved, wb))):
        tall = wa.shape[0] // len(moved_refs)
        for side, part_ref in enumerate(moved_refs):
            span = pl.ds(side * tall, tall)
            sem = in_sem.at[6 + 2 * slot + side]
            loads.append(pltpu.make_async_copy(own_ref.at[span], target.at[span], sem))
            moved.append(pltpu.make_async_copy(part_ref, target.at[span], sem))
    for load in loads[:PARTS]:
        load.start()

    @pl.when(mp % 2 == dp % 2)
    def _():
        for load in loads[PARTS:]:
            load.start()

    @pl.when(mp % 2 != dp % 2)
    def _():
        for load in moved:
            load.start()

    barrier = pltpu.get_barrier_semaphore()
    for peer in (to_c, to_y):
        pl.semaphore_signal(barrier, inc=1, device_id=peer, device_id_type=pl.DeviceIdType.MESH)
    pl.semaphore_wait(barrier, 2)
    sent = []

    def send(source, target, slot, peer):
        copy = pltpu.make_async_remote_copy(
            src_ref=source,
            dst_ref=target,
            send_sem=send_sem.at[slot],
            recv_sem=recv_sem.at[slot],
            device_id=peer,
            device_id_type=pl.DeviceIdType.MESH,
        )
        copy.start()
        sent.append(copy)
        return copy

    kinds = {name: i for i, name in enumerate(("y", "c", "f", "beside", "corner", "give"))}

    def slot_of(kind, h):
        return kinds[kind] * PARTS + h

    arrivals = {}
    for h in range(PARTS):
        loads[h].wait()
        arrivals["y", h] = send(rows.at[0, h], rows.at[2, h], slot_of("y", h), to_y)
        arrivals["c", h] = send(rows.at[0, h], rows.at[1, h], slot_of("c", h), to_c)
    stores = []
    busy = [[], []]
    order = [(0, 0), (0, 1), (1, 0), (1, 1), (2, 0), (3, 0), (2, 1), (3, 1)]

    def place(index):
        group, h = order[index]
        return pl.ds((group * PARTS + h) * part, part)

    def fetch(index):
        copy = pltpu.make_async_copy(slope_ref.at[place(index)], slope.at[index % 2], in_sem.at[4 + index % 2])
        copy.start()
        return copy

    def store(source, target, index, kind):
        copy = pltpu.make_async_copy(source, target, out_sem.at[kind, index])
        copy.start()
        return copy

    fetched = {}
    if back:
        sums_ref[...] = jnp.zeros_like(sums_ref)
        fetched[0] = fetch(0)
        act_load = pltpu.make_async_copy(act_ref, act, in_sem.at[10])
        act_load.start()
    for load in loads[PARTS:]:
        load.wait()

    def work(index, target):
        group, h = order[index]
        side = index % 2
        for copy in busy[side]:
            copy.wait()
        busy[side] = []
        source = rows.at[group, h]
        if back:
            fetched[index].wait()
            if index + 1 < len(order):
                fetched[index + 1] = fetch(index + 1)

        def first(at, size):
            span = pl.ds(at, size)
            value = nn(source[...], wa[:, span])
            if back:
                value = bf(value * f32(slope[side, :, span]))
                left[side, :, span] = value
                sums_ref[:, span] += jnp.sum(f32(value), axis=0, keepdims=True)
            else:
                value = value + bias_ref[:, span]
                square = value * value
                bend = jnp.tanh(0.7978845608028654 * value * (1.0 + 0.044715 * square))
                half = 0.5 * (1.0 + bend)
                left[side, :, span] = bf(value * half)
                slope[side, :, span] = bf(
                    half + 0.5 * value * (1.0 - bend * bend) * 0.7978845608028654 * (1.0 + 0.134145 * square)
                )

        tiles(width, first)
        busy[side].append(store(left.at[side], left_ref.at[place(index)], index, 0))
        if not back:
            busy[side].append(store(slope.at[side], slope_ref.at[place(index)], index, 1))
        stores.append(store(source, rows_ref.at[place(index)], index, 2))

        def second(at, size):
            span = pl.ds(at, size)
            target[:, span] = nt(left[side], wb[span, :]).astype(target.dtype)

        tiles(width, second)

    def combine(h):
        arrivals["corner", h].wait_recv()
        give[h] = bf(far[h] + f32(got_f[h]))
        arrivals["give", h] = send(give.at[h], got_y.at[h], slot_of("give", h), to_y)

    work(0, own.at[0])
    work(1, own.at[1])
    for h in range(PARTS):
        arrivals["c", h].wait_recv()
        work(2 + h, beside.at[h])
        arrivals["beside", h] = send(beside.at[h], got_c.at[h], slot_of("beside", h), to_c)
    for h in range(PARTS):
        arrivals["y", h].wait_recv()
        arrivals["f", h] = send(rows.at[2, h], rows.at[3, h], slot_of("f", h), to_c)
        work(4 + 2 * h, far.at[h])
        arrivals["f", h].wait_recv()
        work(5 + 2 * h, corner.at[h])
        arrivals["corner", h] = send(corner.at[h], got_f.at[h], slot_of("corner", h), to_c)
        combine(h)
    if back:
        act_load.wait()
        leaving = {}
        for j in range(-(-width // 256)):
            at, size, side = j * 256, min(256, width - j * 256), j % 2
            if j >= 2:
                leaving[j - 2].wait()

            def column(first, length, at=at, size=size, side=side):
                span = pl.ds(first, length)
                value = None
                for group in range(GROUPS):
                    for h in range(PARTS):
                        here = pl.ds((group * PARTS + h) * part, part)
                        term = tn(rows[group, h, :, at:at + size], act[here, span])
                        value = term if value is None else value + term
                grad[side, :size, span] = bf(value)

            tiles(width, column)
            leaving[j] = pltpu.make_async_copy(
                grad.at[side, pl.ds(0, size)], grad_ref.at[pl.ds(at, size)], in_sem.at[11 + side]
            )
            leaving[j].start()
        for j in list(leaving)[-2:]:
            leaving[j].wait()
    for h in range(PARTS):
        arrivals["beside", h].wait_recv()
        arrivals["give", h].wait_recv()
        out_ref[pl.ds(h * part, part), :] = own[h] + f32(got_c[h]) + f32(got_y[h])
    for copy in sent:
        copy.wait_send()
    for copy in stores + busy[0] + busy[1]:
        copy.wait()


def units(back, x, wa, wb, *extra):
    rows, width = x.shape
    part = rows // PARTS
    half = jax.ShapeDtypeStruct((GROUPS * rows, width), jnp.bfloat16)
    anywhere = pl.BlockSpec(memory_space=pl.ANY)
    inside = pl.BlockSpec(memory_space=pltpu.VMEM)
    thin, wide = pltpu.VMEM((PARTS, part, width), jnp.bfloat16), pltpu.VMEM((PARTS, part, width), jnp.float32)
    count = 6 * PARTS
    moved = (*wa[1:], *wb[1:])
    square = wa[0].shape
    work = []
    if back:
        work = [pltpu.VMEM((GROUPS * rows, width), jnp.bfloat16), pltpu.VMEM((2, 256, width), jnp.bfloat16)]
    return pl.pallas_call(
        functools.partial(units_kernel, back, (len(wa) - 1, len(wb) - 1)),
        in_specs=[anywhere] * (3 + len(moved)) + ([anywhere] * 2 if back else [inside]),
        out_specs=[inside, anywhere, anywhere] + ([inside, anywhere] if back else [anywhere]),
        out_shape=[jax.ShapeDtypeStruct((rows, width), jnp.float32), half, half]
        + ([jax.ShapeDtypeStruct((1, width), jnp.float32), jax.ShapeDtypeStruct(square, jnp.bfloat16)] if back else [half]),
        scratch_shapes=[
            *work,
            pltpu.VMEM(square, jnp.bfloat16),
            pltpu.VMEM(square, jnp.bfloat16),
            pltpu.VMEM((GROUPS, PARTS, part, width), jnp.bfloat16),
            wide, wide, thin, thin, thin, thin, thin, thin, thin, thin,
            pltpu.SemaphoreType.DMA((13,)),
            pltpu.SemaphoreType.DMA((count,)),
            pltpu.SemaphoreType.DMA((count,)),
            pltpu.SemaphoreType.DMA((3, GROUPS * PARTS)),
        ],
        cost_estimate=pl.CostEstimate(
            flops=60 * 10 ** 9, bytes_accessed=60 * 2 ** 20, transcendentals=0
        ),
        compiler_params=pltpu.CompilerParams(
            collective_id=2 if back else 1, has_side_effects=True, vmem_limit_bytes=58 * 2 ** 20
        ),
        name="units_back" if back else "units",
    )(x, wa[0], wb[0], *moved, *extra)


def settle_kernel(planes, keep_ref, send_ref, piece_ref, sum_ref, out_ref, sum_out, pieces, outgo, income, total, from_y, from_x, to_give,
                  final, from_z, sum_at, sum_from, load_sem, c_send, c_recv, xy_send, xy_recv, z_send, z_recv,
                  sum_send, sum_recv):
    dp, mp = lax.axis_index("dp"), lax.axis_index("mp")
    z, c = dp // 2, dp % 2
    y, x = mp // 2, mp % 2
    to_x, to_y = (dp, mp + 1 - 2 * x), (dp, mp + 2 - 4 * y)
    to_c = (dp + 1 - 2 * c, mp)
    others = [lax.rem(z + k, planes) for k in range(1, planes)]
    barrier = pltpu.get_barrier_semaphore()
    for peer in (to_x, to_y, to_c, *[(other * 2 + c, mp) for other in others]):
        pl.semaphore_signal(barrier, inc=1, device_id=peer, device_id_type=pl.DeviceIdType.MESH)
    loads = []
    for k, (far_y, far_x) in enumerate(((1, 1), (1, 0), (0, 1), (0, 0))):
        index = 2 * (1 - y if far_y else y) + (1 - x if far_x else x)
        loads.append(pltpu.make_async_copy(piece_ref.at[index], pieces.at[k], load_sem.at[k]))
        loads[-1].start()
    pl.semaphore_wait(barrier, 3 + len(others))
    width = pieces.shape[2]
    tall = keep_ref.shape[0] // planes
    half = planes // 2

    def remote(source, target, sems, slot, peer):
        copy = pltpu.make_async_remote_copy(
            src_ref=source,
            dst_ref=target,
            send_sem=sems[0].at[slot],
            recv_sem=sems[1].at[slot],
            device_id=peer,
            device_id_type=pl.DeviceIdType.MESH,
        )
        copy.start()
        return copy

    def product(left_ref, k, write):
        def body(at, size):
            span = pl.ds(at, size)
            value = nn(left_ref[...], pieces[k, :, span])
            for block in range(planes):
                write(block, span, value[block * tall:(block + 1) * tall])

        tiles(width, body)

    adding = [remote(sum_ref, sum_from.at[0], (sum_send, sum_recv), 0, to_c)]

    def sum_step(k, source, peer):
        adding[k].wait_recv()
        sum_at[k] = source[...] + sum_from[k]
        if peer is not None:
            adding.append(remote(sum_at.at[k], sum_from.at[k + 1], (sum_send, sum_recv), k + 1, peer))

    crossing = []
    for k in range(4):
        loads[k].wait()

        def put(block, span, value, k=k):
            outgo[k, block, :, span] = bf(value)

        product(send_ref, k, put)
        crossing.append(remote(outgo.at[k], income.at[k], (c_send, c_recv), k, to_c))
    first, second = pl.ds(0, half), pl.ds(half, half)
    sent = []

    def chip(k):
        crossing[k].wait_recv()

        def put(block, span, value, k=k):
            total[k, block, :, span] = bf(value + f32(income[k, block, :, span]))

        product(keep_ref, k, put)

    def add(target, base, extras):
        for block in range(half):
            value = f32(base[block])
            for extra in extras:
                value = value + f32(extra[block])
            target[block] = value.astype(target.dtype)

    sems = (xy_send, xy_recv)
    sum_step(0, sum_ref, to_x)
    chip(0)
    y0 = remote(total.at[0, first], from_y.at[0], sems, 0, to_y)
    x0 = remote(total.at[0, second], from_x.at[0], sems, 1, to_x)
    chip(1)
    y1 = remote(total.at[1, first], from_y.at[1], sems, 2, to_y)
    sum_step(1, sum_at.at[0], to_y)
    chip(2)
    x1 = remote(total.at[2, second], from_x.at[1], sems, 3, to_x)
    chip(3)
    sum_step(2, sum_at.at[1], None)
    for k, other in enumerate(others):
        adding.append(remote(sum_at.at[2], sum_from.at[3 + k], (sum_send, sum_recv), 3 + k, (other * 2 + c, mp)))
    y0.wait_recv()
    add(to_give.at[0], total.at[2, first], [from_y.at[0]])
    x2 = remote(to_give.at[0], from_x.at[2], sems, 4, to_x)
    x0.wait_recv()
    add(to_give.at[1], total.at[1, second], [from_x.at[0]])
    y2 = remote(to_give.at[1], from_y.at[2], sems, 5, to_y)
    y1.wait_recv()
    x2.wait_recv()
    add(final.at[first], total.at[3, first], [from_y.at[1], from_x.at[2]])
    x1.wait_recv()
    y2.wait_recv()
    add(final.at[second], total.at[3, second], [from_x.at[1], from_y.at[2]])
    leaving = []
    for k, other in enumerate(others):
        leaving.append(remote(final.at[other], from_z.at[k], (z_send, z_recv), k, (other * 2 + c, mp)))
    value = f32(final[z])
    for k in range(len(others)):
        leaving[k].wait_recv()
        value = value + f32(from_z[k])
    out_ref[...] = value * (1.0 / (2 * planes))
    value = sum_at[2]
    for k in range(len(others)):
        adding[3 + k].wait_recv()
        value = value + sum_from[3 + k]
    sum_out[...] = value
    for copy in (*crossing, y0, x0, y1, x1, x2, y2, *leaving, *adding):
        copy.wait_send()


def settle_columns(planes, keep, send, pieces, sums):
    rows, width = keep.shape[0], pieces.shape[2]
    tall = rows // planes
    half = planes // 2
    low = lambda *shape: pltpu.VMEM((*shape, tall, width), jnp.bfloat16)
    inside = pl.BlockSpec(memory_space=pltpu.VMEM)
    return pl.pallas_call(
        functools.partial(settle_kernel, planes),
        in_specs=[inside, inside, pl.BlockSpec(memory_space=pl.ANY), inside],
        out_specs=[inside, inside],
        out_shape=[
            jax.ShapeDtypeStruct((tall, width), jnp.float32),
            jax.ShapeDtypeStruct(sums.shape, jnp.float32),
        ],
        scratch_shapes=[
            pltpu.VMEM(pieces.shape, jnp.bfloat16),
            low(4, planes), low(4, planes), low(4, planes),
            low(3, half), low(3, half), low(2, half), low(planes), low(planes - 1),
            pltpu.VMEM((3, *sums.shape), jnp.float32),
            pltpu.VMEM((2 + planes, *sums.shape), jnp.float32),
            pltpu.SemaphoreType.DMA((4,)),
            pltpu.SemaphoreType.DMA((4,)), pltpu.SemaphoreType.DMA((4,)),
            pltpu.SemaphoreType.DMA((6,)), pltpu.SemaphoreType.DMA((6,)),
            pltpu.SemaphoreType.DMA((planes - 1,)), pltpu.SemaphoreType.DMA((planes - 1,)),
            pltpu.SemaphoreType.DMA((2 + planes,)), pltpu.SemaphoreType.DMA((2 + planes,)),
        ],
        cost_estimate=pl.CostEstimate(flops=16 * 10 ** 9, bytes_accessed=60 * 2 ** 20, transcendentals=0),
        compiler_params=pltpu.CompilerParams(
            collective_id=3, has_side_effects=True, vmem_limit_bytes=58 * 2 ** 20
        ),
        name="settle_columns",
    )(keep, send, pieces, sums)


def bf(value):
    return value.astype(jnp.bfloat16)


def f32(value):
    return value.astype(jnp.float32)


def norm_parts(value):
    mean = jnp.mean(value, axis=-1, keepdims=True)
    centred = value - mean
    spread = jnp.mean(centred * centred, axis=-1, keepdims=True)
    return centred, lax.rsqrt(spread + eps)


def norm_back(grad, value, gain):
    centred, rate = norm_parts(value)
    hat = centred * rate
    scaled = grad * gain
    inner = scaled - jnp.mean(scaled, axis=-1, keepdims=True) - hat * jnp.mean(scaled * hat, axis=-1, keepdims=True)
    return inner * rate, jnp.sum(grad * hat, axis=0), jnp.sum(grad, axis=0)


def quick_body(
    planes,
    tokens,
    cotangent,
    block_order,
    qkv_weight,
    proj_weight,
    fc_weight,
    fc2_weight,
    fc_bias,
    norm_gain,
    norm_shift,
    attn_bias,
    out_bias,
):
    seqs, local, width = tokens.shape
    slots = local // LANES
    dp_rank = lax.axis_index("dp")
    mp_rank = lax.axis_index("mp")
    core, row, col = dp_rank % 2, mp_rank // 2, mp_rank % 2
    over_x = pairs_of(planes, lambda z, c, y, x: (z, c, y, 1 - x))
    over_y = pairs_of(planes, lambda z, c, y, x: (z, c, 1 - y, x))
    over_xy = pairs_of(planes, lambda z, c, y, x: (z, c, 1 - y, 1 - x))
    over_c = pairs_of(planes, lambda z, c, y, x: (z, 1 - c, y, x))
    swap_yc = pairs_of(planes, lambda z, c, y, x: (z, y, c, x))
    swap_xc = pairs_of(planes, lambda z, c, y, x: (z, x, y, c))

    along_z = [
        [flat(z, c, y, x) for z in range(planes)] for c in range(2) for y in range(2) for x in range(2)
    ]

    along_dp = [[flat(z, c, y, x) for z in range(planes) for c in range(2)] for y in range(2) for x in range(2)]

    def go(value, pairs):
        return lax.ppermute(value, AXES, pairs)

    def turn_yc(value):
        return jnp.where(row == core, value, go(value, swap_yc))

    def turn_xc(value):
        return jnp.where(col == core, value, go(value, swap_xc))

    def sum_z(value):
        return lax.psum_scatter(value, AXES, axis_index_groups=along_z, scatter_dimension=0, tiled=True)

    ranks = jnp.stack([2 * core + col, 2 * core + 1 - col])
    others = jnp.stack([2 * (1 - core) + col, 2 * (1 - core) + 1 - col])

    def places(which):
        return block_order.reshape(-1, slots)[which].reshape(-1)

    place = places(ranks)
    keyed = jnp.concatenate([place, places(others)])
    blocks = keyed.shape[0]
    order = jnp.arange(blocks, dtype=jnp.int32)
    slot = jnp.sum(jnp.where(keyed[None, :] == order[:, None], order[None, :], 0), axis=1).astype(jnp.int32)

    def add_pair(a, b):
        return bf(f32(a) + f32(b))

    def core_columns(value, which):
        parts = value.reshape(value.shape[0], planes, 2, -1)
        return lax.dynamic_index_in_dim(parts, which, 2, keepdims=False).reshape(value.shape[0], -1)

    def chip_sums(left, right):
        keep, send = core_columns(left, core), core_columns(left, 1 - core)
        size = right.shape[1] // 4

        def one(near_y, near_x):
            index = 2 * (row if near_y else 1 - row) + (col if near_x else 1 - col)
            piece = lax.dynamic_slice_in_dim(right, index * size, size, axis=1)
            return add_pair(tn(keep, piece), go(bf(tn(send, piece)), over_c))

        return one(False, False), one(False, True), one(True, False), one(True, True)

    def gather_dp(piece):
        return lax.all_gather(piece, "dp", axis=0, tiled=True)

    def after(values, *done):
        return lax.optimization_barrier((values, done))[0]

    def fence(*values):
        return lax.optimization_barrier(values)

    def stacked(layer):
        qkv = qkv_weight[layer]
        return jnp.stack([qkv[:, :width], qkv[:, width:2 * width], qkv[:, 2 * width:], proj_weight[layer]])

    small = f32(jnp.concatenate([norm_gain, norm_shift, attn_bias, out_bias, fc_bias[:, None, :]], axis=1))
    count = small.shape[0] * small.shape[1]
    small = jnp.pad(small.reshape(count, -1), ((0, -count % 8), (0, 0)))
    piece = lax.dynamic_index_in_dim(stacked(0), mp_rank, 0, keepdims=False)
    full, small, token_rows = gather_four(planes, piece, small, tokens)
    first_four = full.reshape(4, width, width)
    small = jnp.transpose(small[:, :count].reshape(-1, LAYERS, 9, width // (2 * planes)), (1, 2, 0, 3))
    small = small.reshape(LAYERS, 9, width)
    units_bias = turn_xc(small[:, 8])

    fc_slice = [None] * LAYERS
    fc2_slice = [None] * LAYERS
    fc_slice[0] = gather_dp(fc_weight[0])
    fc2_slice[0] = gather_dp(fc2_weight[0].T)
    qkv1 = qkv_weight[1]
    pair = gather_dp(jnp.where(row == 0, qkv1[:, :width], qkv1[:, width:2 * width]))
    tall = width // 2

    def pair_join(whole, got, bit):
        got = jnp.concatenate(got, axis=0)
        beside = go(got, over_c)
        other = jnp.concatenate([jnp.where(core == 0, got, beside), jnp.where(core == 0, beside, got)], axis=0)
        return jnp.where(bit == 0, whole, other), jnp.where(bit == 0, other, whole)

    def halves(value):
        middle = value.shape[0] // 2
        return value[:middle], value[middle:]

    def padded(value):
        return jnp.pad(value, ((0, 0), (0, -width % LANES)))

    def normal(value, layer, which):
        centred, rate = norm_parts(value)
        return bf(centred * rate * small[layer, which] + small[layer, 2 + which])

    def attend(layer, hidden, w):
        normed = normal(hidden, layer, 0)
        key = padded(bf(nn(normed, w["k"])))
        key_other = go(key, over_c)
        value = padded(bf(nn(normed, w["v"]) + small[layer, 5]))
        value_other = go(value, over_c)
        query = bf(nn(normed, w["q"]) + small[layer, 4])
        return normed, query, key, key_other, value, value_other

    def project(layer, hidden, attended, w):
        middle = hidden + nn(attended, w["proj"]) + small[layer, 6]
        return middle, normal(middle, layer, 1)

    turn_far = pairs_of(planes, lambda z, c, y, x: (z, y, c, 1 - x))

    def cot_regroup():
        mine = lax.dynamic_index_in_dim(cotangent, col, 0, keepdims=False)
        theirs = lax.dynamic_index_in_dim(cotangent, 1 - col, 0, keepdims=False)
        return mine, go(mine, swap_yc), go(theirs, turn_far)

    saved = []
    hidden = f32(token_rows.reshape(-1, width))
    w = dict(q=first_four[0], k=first_four[1], v=first_four[2], proj=first_four[3])
    first_fc = after(fc_slice[0], units_bias)
    fc_moved = go(first_fc, swap_xc)
    fc_slice[1] = gather_dp(after(fc_weight[1], small))
    parts = attend(0, hidden, w)
    fc2_now = fc2_slice[0]
    *parts, fc_moved, fc2_top, fc2_end, pair = fence(*parts, fc_moved, *halves(fc2_now), pair)
    normed, query, key, key_other, value, value_other = parts
    v1 = gather_dp(after(qkv1[:, 2 * width:], normed))
    fc2_parts = fc2_top, fc2_end
    pair_parts = halves(lax.dynamic_slice_in_dim(pair, core * tall, tall, axis=0))
    fc2_top = go(fc2_parts[0], swap_xc)
    got = [go(pair_parts[0], over_y)]
    attended, lse = attention(place, slot, query, key, key_other, value, value_other)
    attended, lse, fc2_top, got[0] = fence(attended, lse, fc2_top, got[0])
    proj1 = gather_dp(after(proj_weight[1], attended))
    fc2_end = go(fc2_parts[1], swap_xc)
    got.append(go(pair_parts[1], over_y))
    middle, normed_two = project(0, hidden, attended, w)
    middle, normed_two, fc2_end, got[1], fc_now = fence(middle, normed_two, fc2_end, got[1], fc_slice[1])
    w["fc"] = (first_fc, fc_moved)
    w["fc2"] = (fc2_now, fc2_top, fc2_end)
    fc2_slice[1] = gather_dp(after(fc2_weight[1].T, middle))
    fc_moved = go(fc_now, swap_xc)
    ff_out, rows_in, active, slope = units(False, normed_two, w["fc"], w["fc2"], units_bias[0:1])
    ff_out, rows_in, active, slope, fc_moved, v1 = fence(ff_out, rows_in, active, slope, fc_moved, v1)
    saved.append((hidden, *parts, attended, lse, middle, rows_in, active, slope, w))
    w = dict(v=v1, proj=proj1, fc=(fc_now, fc_moved))
    w["q"], w["k"] = pair_join(pair, got, row)
    hidden = middle + ff_out + small[0, 7]
    cot_moved = cot_regroup()
    *parts, cot_moved, fc2_now = fence(*attend(1, hidden, w), cot_moved, fc2_slice[1])
    normed, query, key, key_other, value, value_other = parts
    fc2_parts = halves(fc2_now)
    fc2_top = go(fc2_parts[0], swap_xc)
    attended, lse = attention(place, slot, query, key, key_other, value, value_other)
    attended, lse, fc2_top = fence(attended, lse, fc2_top)
    fc2_end = go(fc2_parts[1], swap_xc)
    middle, normed_two = project(1, hidden, attended, w)
    w["fc2"] = (fc2_now, fc2_top, fc2_end)
    middle, normed_two, fc2_end = fence(middle, normed_two, fc2_end)
    w["fc2"] = (fc2_now, fc2_top, fc2_end)
    ff_out, rows_in, active, slope = units(False, normed_two, w["fc"], w["fc2"], units_bias[1:2])
    saved.append((hidden, *parts, attended, lse, middle, rows_in, active, slope, w))
    final = bf(middle + ff_out + small[1, 7])

    factor = 1.0 / lax.axis_size("dp")
    results = [None] * LAYERS

    def units_split(value):
        quarters = value.reshape(planes, 2, -1, width)
        kept = lax.dynamic_index_in_dim(quarters, col, 1, keepdims=False)
        return kept, lax.dynamic_index_in_dim(quarters, 1 - col, 1, keepdims=False)

    def halves_of(value):
        halves = value.reshape(2, -1, width)
        kept = lax.dynamic_index_in_dim(halves, col, 0, keepdims=False)
        return kept, lax.dynamic_index_in_dim(halves, 1 - col, 0, keepdims=False)

    def sum_dp(value):
        return lax.psum_scatter(value, AXES, axis_index_groups=along_dp, scatter_dimension=0, tiled=True)

    def mp_pieces(*values):
        def piece(y, x):
            parts = []
            for value in values:
                size = value.shape[1] // 4
                parts.append(lax.dynamic_slice_in_dim(value, (2 * y + x) * size, size, axis=1))
            return jnp.concatenate(parts, axis=1)

        return [
            piece(row, col),
            go(piece(row, 1 - col), over_x),
            go(piece(1 - row, col), over_y),
            go(piece(1 - row, 1 - col), over_xy),
        ]

    def columns_of(values, parts, index):
        cut = []
        for value in values:
            size = value.shape[1] // parts
            cut.append(lax.dynamic_slice_in_dim(value, index * size, size, axis=1))
        return jnp.concatenate(cut, axis=1)

    def total_of(pieces):
        return sum(f32(piece) for piece in pieces[1:]) + f32(pieces[0])

    def mlp_back(layer, out_grad, *held):
        (*_, active, slope, w) = saved[layer]
        return units(True, out_grad, w["fc2"], w["fc"], slope, active)

    def middle_back(layer, grad, da2):
        middle, w = saved[layer][9], saved[layer][-1]
        part, gain, shift = norm_back(da2, middle, small[layer, 1])
        middle_grad = grad + part
        branch = bf(middle_grad)
        return middle_grad, branch, bf(nt(branch, w["proj"])), gain, shift, jnp.sum(f32(branch), axis=0)

    def heads_back(layer, attended_grad):
        hidden, normed, query, key, key_other, value, value_other, attended, lse = saved[layer][:9]
        return attention_back(place, slot, query, key, key_other, value, value_other, attended_grad, attended, lse)

    def input_back(layer, middle_grad, dq, dk, dv):
        hidden, w = saved[layer][0], saved[layer][-1]
        normed_grad = nt(dq, w["q"]) + nt(dk, w["k"]) + nt(dv, w["v"])
        part, gain, shift = norm_back(normed_grad, hidden, small[layer, 0])
        return middle_grad + part, gain, shift

    def mixed_of(dq, dkm, dkt, dvm, dvt):
        dk = bf(dkm + f32(go(dkt, over_c)))[:, :width]
        dv = bf(dvm + f32(go(dvt, over_c)))[:, :width]
        return dq, dk, dv

    def last_sum(parts, away, side):
        return bf(f32(parts[3]) + f32(away) + f32(side))

    def regroup(value):
        value = padded(value)
        return go(value[:local], swap_yc), go(value[local:], turn_far)

    def settle(value, mine, theirs):
        mine, theirs = mine[:, :width], theirs[:, :width]
        mine = jnp.where(row == core, value[:local], mine)
        return f32(jnp.stack([jnp.where(col == 0, mine, theirs), jnp.where(col == 0, theirs, mine)]))

    def bias_sums(gains, shifts, dq, dv, branch_sum, out_grad):
        return jnp.stack(
            [*gains, *shifts, jnp.sum(f32(dq), axis=0), jnp.sum(f32(dv), axis=0), branch_sum, jnp.sum(f32(out_grad), axis=0)]
        )

    def row_parts(left):
        columns = jnp.transpose(left).reshape(planes, 2, -1, left.shape[0])
        keep = lax.dynamic_index_in_dim(columns, core, 1, keepdims=False)
        send = lax.dynamic_index_in_dim(columns, 1 - core, 1, keepdims=False)
        return keep.reshape(-1, left.shape[0]), send.reshape(-1, left.shape[0])

    out_grad = jnp.concatenate([jnp.where(row == core, cot_moved[0], cot_moved[1]), cot_moved[2]], axis=0)
    grad = f32(out_grad)
    final, out_grad = fence(final, out_grad)
    da2, rows_grad, inner_grad, units_sum, fc2_grad = mlp_back(1, out_grad)
    final, da2, inner_grad, units_sum, fc2_grad = fence(final, da2, inner_grad, units_sum, fc2_grad)
    fc2_sum = sum_z(fc2_grad)
    fc_kept, fc_sent = units_split(bf(tn(saved[1][10], inner_grad)))
    fc_kept, fc_one, fc_two, fc_three, da2 = fence(fc_kept, fc_sent[:1], fc_sent[1:3], fc_sent[3:], da2)
    fc_away = [go(fc_one, over_x)]
    middle_grad, branch, attended_grad, gain_two, shift_two, attn_out_grad = middle_back(1, grad, da2)
    proj_grad = bf(tn(saved[1][7], branch))
    fc_away[0], fc_two, fc_three, middle_grad, branch, attended_grad, proj_grad = fence(
        fc_away[0], fc_two, fc_three, middle_grad, branch, attended_grad, proj_grad
    )
    proj_sum = sum_dp(proj_grad)
    fc_away.append(go(fc_two, over_x))
    final_moved = regroup(final)
    back = fence(*heads_back(1, attended_grad), fc2_sum, fc_away[1], fc_three, *final_moved)
    fc2_sum, fc_away[1], fc_three, *final_moved = back[5:]
    fc_away.append(go(fc_three, over_x))
    dq, dk, dv = mixed_of(*back[:5])
    dq_grad = bf(tn(saved[1][1], back[0]))
    dq, dk, dv, dq_grad, fc_away[2] = fence(dq, dk, dv, dq_grad, fc_away[2])
    dq_sum = sum_dp(dq_grad)
    below, gain_one, shift_one = input_back(1, middle_grad, dq, dk, dv)
    out_grad_low = bf(below)
    sums_one = bias_sums((gain_one, gain_two), (shift_one, shift_two), dq, dv, attn_out_grad, out_grad)
    out_grad_low, below, dq, dk, dv, sums_one = fence(out_grad_low, below, dq, dk, dv, sums_one)
    dkv_grad = bf(tn(saved[1][1], jnp.concatenate([dk, dv], axis=1)))
    fc_joined = add_pair(fc_kept, jnp.concatenate(fc_away, axis=0))
    fc2_kept, fc2_sent = halves_of(fc2_sum)
    out_grad_low, dkv_grad, fc_joined, fc2_sent = fence(out_grad_low, dkv_grad, fc_joined, fc2_sent)
    dkv_sum = sum_dp(dkv_grad)
    fc_sum = sum_z(fc_joined.reshape(-1, width))
    fc2_away = go(fc2_sent, over_x)
    da2, rows_grad, inner_grad, units_low, fc2_grad = mlp_back(0, out_grad_low)
    da2, inner_grad, units_low, fc2_grad, fc2_away, proj_sum, dq_sum = fence(
        da2, inner_grad, units_low, fc2_grad, fc2_away, proj_sum, dq_sum
    )
    fc2_high = add_pair(fc2_kept, fc2_away)
    fc2_kept, fc2_sent = units_split(fc2_grad)
    fc2_kept, fc2_one, fc2_two, fc2_three, da2, fc2_high = fence(
        fc2_kept, fc2_sent[:1], fc2_sent[1:2], fc2_sent[2:], da2, fc2_high
    )
    fc2_away = [go(fc2_one, over_x)]
    fc_kept, fc_sent = units_split(bf(tn(saved[0][10], inner_grad)))
    fc2_away[0], fc2_two, fc2_three, fc_kept, fc_sent, da2 = fence(
        fc2_away[0], fc2_two, fc2_three, fc_kept, fc_sent, da2
    )
    fc2_away.append(go(fc2_two, over_x))
    middle_grad, branch, attended_grad, gain_two, shift_two, attn_out_grad = middle_back(0, below, da2)
    proj_grad = bf(tn(saved[0][7], branch))
    fc2_away[1], fc2_three, fc_sent, middle_grad, branch, attended_grad, proj_grad = fence(
        fc2_away[1], fc2_three, fc_sent, middle_grad, branch, attended_grad, proj_grad
    )
    fc2_away.append(go(fc2_three, over_x))
    fc_away = [go(fc_sent[:1], over_x)]
    fc_one, fc_two, fc_three = fc_sent[1:2], fc_sent[2:3], fc_sent[3:]
    back = fence(
        *heads_back(0, attended_grad), fc2_away[2], fc_away[0], fc_one, fc_two, fc_three,
        dkv_sum, fc_sum, fc2_high, dq_sum, proj_sum
    )
    fc2_away[2], fc_away[0], fc_one, fc_two, fc_three, dkv_sum, fc_sum, fc2_high, dq_sum, proj_sum = back[5:]
    fc2_low = sum_z(add_pair(fc2_kept, jnp.concatenate(fc2_away, axis=0)).reshape(-1, width))
    fc_away.append(go(fc_one, over_x))
    turned = turn_xc(jnp.concatenate([fc_sum, fc2_high], axis=0))
    qkv_sum = jnp.concatenate([dq_sum, dkv_sum], axis=1)
    near_columns, far_columns = [columns_of((qkv_sum, proj_sum), 2, side) for side in (row, 1 - row)]
    far_top, far_end = halves(far_columns)
    far_top = go(far_top, over_y)
    dq, dk, dv = mixed_of(*back[:5])
    dq, dk, dv, proj_grad, turned, near_columns, far_top, far_end, fc_away[1], fc_two, fc_three = fence(
        dq, dk, dv, proj_grad, turned, near_columns, far_top, far_end, fc_away[1], fc_two, fc_three
    )
    far_end = go(far_end, over_y)
    fc_away.append(go(fc_two, over_x))
    proj_low = sum_dp(proj_grad)
    lowest, gain_one, shift_one = input_back(0, middle_grad, dq, dk, dv)
    lowest, far_end, fc_away[2], fc_three = fence(lowest, far_end, fc_away[2], fc_three)
    fc_away.append(go(fc_three, over_x))
    far_columns = jnp.concatenate([far_top, far_end], axis=0)
    sums_zero = bias_sums((gain_one, gain_two), (shift_one, shift_two), dq, dv, attn_out_grad, out_grad_low)
    low = bf(lowest)
    third = 3 * width // 4
    mixed = jnp.concatenate([dq, dk, dv], axis=1)
    pieces = jnp.stack([mixed[:, i * third:(i + 1) * third] for i in range(4)])
    keep, send = row_parts(saved[0][1])
    spread = (jnp.arange(4) == 2 * row + core).astype(jnp.float32)
    sums = jnp.concatenate(
        [
            sums_zero,
            sums_one,
            (spread[None, :, None] * jnp.concatenate([units_low, units_sum], axis=0)[:, None, :]).reshape(2 * 4, width),
        ]
    )
    held_rows = proj_sum.shape[0]
    split = 3 * width // 2
    columns = add_pair(near_columns, far_columns)
    halves_x = columns[:, :split], columns[:, split:]
    near_columns, far_columns = [columns_of(halves_x, 2, side) for side in (col, 1 - col)]
    low, sums, pieces, keep, send, fc2_low, near_columns, far_columns, fc_away[3] = fence(
        low, sums, pieces, keep, send, fc2_low, near_columns, far_columns, fc_away[3]
    )
    fc_low = sum_z(add_pair(fc_kept, jnp.concatenate(fc_away, axis=0)).reshape(-1, width))
    fc2_low = turn_xc(fc2_low)
    low_moved = regroup(low)
    far_columns = go(far_columns, over_x)
    qkv_low, sums = settle_columns(planes, keep, send, pieces, sums)
    qkv_low, sums, fc_low, proj_low, fc2_low, far_columns, low_moved = fence(
        qkv_low, sums, fc_low, proj_low, fc2_low, far_columns, low_moved
    )
    columns = f32(near_columns) + f32(far_columns)
    qkv_high = columns[:, :third]
    results_zero = [turn_xc(fc_low), fc2_low, total_of(mp_pieces(proj_low))]
    results_one = [turned[:held_rows], turned[held_rows:], columns[:, third:]]
    outputs = settle(final, *final_moved)
    input_grad = settle(low, *low_moved)
    held = width // (2 * planes)
    sums = lax.dynamic_slice_in_dim(sums, dp_rank * held, held, axis=1) * factor
    unit_rows = lax.dynamic_index_in_dim(sums[16:].reshape(2, 4, held), mp_rank, 1, keepdims=False)
    sums = sums[:16].reshape(2, 8, held)
    qkv_high = qkv_high * factor
    results = [results_zero, results_one]
    return (
        outputs,
        input_grad,
        jnp.stack([qkv_low, qkv_high]),
        jnp.stack([f32(entry[2]) for entry in results]) * factor,
        jnp.stack([f32(entry[0]) for entry in results]) * factor,
        jnp.stack([f32(entry[1]).T for entry in results]) * factor,
        unit_rows,
        sums[:, 0:2],
        sums[:, 2:4],
        sums[:, 4:6],
        sums[:, 6:8],
    )


def solution(mesh):
    planes = mesh.shape["dp"] // 2
    if mesh.shape["mp"] == 4 and planes == 4:
        body = functools.partial(quick_body, planes)
    else:
        body = general_body
    return jax.shard_map(
        body,
        mesh=mesh,
        in_specs=(
            P("dp", "mp", None),
            P("dp", "mp", None),
            P(),
            P(None, "dp", None),
            P(None, "dp", None),
            P(None, "dp", "mp"),
            P(None, "mp", "dp"),
            P(None, ("mp", "dp")),
            P(None, None, "dp"),
            P(None, None, "dp"),
            P(None, None, "dp"),
            P(None, None, "dp"),
        ),
        out_specs=(
            P("dp", "mp", None),
            P("dp", "mp", None),
            P(None, "dp", "mp"),
            P(None, "dp", "mp"),
            P(None, "dp", "mp"),
            P(None, "mp", "dp"),
            P(None, ("mp", "dp")),
            P(None, None, "dp"),
            P(None, None, "dp"),
            P(None, None, "dp"),
            P(None, None, "dp"),
        ),
        check_vma=False,
    )
```
